32 devices in a mesh: seq: 16 (over z, y, core), fsdp: 2 (over x).
Axes of the slice: x: 2, y: 2, z: 4, core: 2. Of those that a mesh axis runs over, the one named last changes fastest.
Arguments:
- target: bfloat16 [2, 2, 8192, 768], P(None, 'fsdp', 'seq'), may hold values from -6 to 6
- memory: bfloat16 [2, 2, 8192, 768], P(None, 'fsdp', 'seq'), may hold values from -6 to 6
- cotangent: bfloat16 [2, 2, 8192, 768], P(None, 'fsdp', 'seq'), may hold values from -6 to 6
- seg_target: int32 [2, 2, 8192], P(None, 'fsdp', 'seq'), may hold values from 0 to 4, as said below
- seg_memory: int32 [2, 2, 8192], P(None, 'fsdp', 'seq'), may hold values from 0 to 4, as said below
- attn_master: float32 [8, 768, 768], P(None, ('seq', 'fsdp'))
- attn_first: float32 [8, 768, 768], P(None, ('seq', 'fsdp')), may hold values from -512 to 512
- attn_second: float32 [8, 768, 768], P(None, ('seq', 'fsdp')), may hold values from 8192 to 32768
- in_master: float32 [768, 3072], P(('seq', 'fsdp')), may hold values from -0.21875 to 0.21875
- in_first: float32 [768, 3072], P(('seq', 'fsdp')), may hold values from -256 to 256
- in_second: float32 [768, 3072], P(('seq', 'fsdp')), may hold values from 2048 to 8192
- out_master: float32 [3072, 768], P(('seq', 'fsdp')), may hold values from -0.109375 to 0.109375
- out_first: float32 [3072, 768], P(('seq', 'fsdp')), may hold values from -640 to 640
- out_second: float32 [3072, 768], P(('seq', 'fsdp')), may hold values from 11796.48 to 47185.92
- vec_master: float32 [17, 768], P(None, ('seq', 'fsdp'))
- vec_first: float32 [17, 768], P(None, ('seq', 'fsdp')), may hold values from -1024 to 1024
- vec_second: float32 [17, 768], P(None, ('seq', 'fsdp')), may hold values from 32768 to 131072
Outputs:
- block_out: float32 [2, 2, 8192, 768], P(None, 'fsdp', 'seq')
- grad_target: float32 [2, 2, 8192, 768], P(None, 'fsdp', 'seq')
- grad_memory: float32 [2, 2, 8192, 768], P(None, 'fsdp', 'seq')
- attn_master_new: float32 [8, 768, 768], P(None, ('seq', 'fsdp'))
- attn_first_new: float32 [8, 768, 768], P(None, ('seq', 'fsdp'))
- attn_second_new: float32 [8, 768, 768], P(None, ('seq', 'fsdp'))
- attn_weight: bfloat16 [8, 768, 768], P(None, ('seq', 'fsdp'))
- in_master_new: float32 [768, 3072], P(('seq', 'fsdp'))
- in_first_new: float32 [768, 3072], P(('seq', 'fsdp'))
- in_second_new: float32 [768, 3072], P(('seq', 'fsdp'))
- in_weight: bfloat16 [768, 3072], P(('seq', 'fsdp'))
- out_master_new: float32 [3072, 768], P(('seq', 'fsdp'))
- out_first_new: float32 [3072, 768], P(('seq', 'fsdp'))
- out_second_new: float32 [3072, 768], P(('seq', 'fsdp'))
- out_weight: bfloat16 [3072, 768], P(('seq', 'fsdp'))
- vec_master_new: float32 [17, 768], P(None, ('seq', 'fsdp'))
- vec_first_new: float32 [17, 768], P(None, ('seq', 'fsdp'))
- vec_second_new: float32 [17, 768], P(None, ('seq', 'fsdp'))
- vec_weight: bfloat16 [17, 768], P(None, ('seq', 'fsdp'))
The draws below stay inside these ranges and needn't reach their ends.
Inputs may be any that keep to these rules, and one draw needn't show every extreme that they name: `seg_target`: within each sequence of 1024 positions the ids never fall and each of 0 to 4 appears; document 2 starts in the first 512 positions and ends in the last 512. `seg_memory`: within each sequence of 1024 positions the ids never fall and each of 0 to 4 appears; document 2 starts in the first 512 positions and ends in the last 512.
All inputs are finite; a program needn't handle non-finite values.
Results may differ from the reference program's by a relative error of at most 0.02.
The reference program's roundings to bfloat16 on the way count: a program that leaves them out, or rounds other values in their place, can miss the bound.
Values may be sent and summed in bfloat16 or wider, within the bound.
No kernel may reach another device: no remote copies, remote signals or barrier semaphores. Data moves between devices by JAX's collectives and lax.ppermute only.
A program may use at most 256 MiB of HBM per device.

```python
import math
import jax
import jax.numpy as jnp
from jax import lax

D = 768
HEADS = 12
FF = 3072
HDIM = 64
TOK_DEV = 512
MICRO = 2
STEP = 10
LEN = 1024
SIDE = 2
TOKS = 8192
ALLTOK = 32768


def sequence_cuts(key, half):
    sub_keys = jax.random.split(key, 4)
    front_cut = jax.random.randint(sub_keys[0], (), 2, half)
    inner_front = jax.random.randint(sub_keys[1], (), 1, front_cut)
    back_cut = jax.random.randint(sub_keys[2], (), 2, half)
    inner_back = jax.random.randint(sub_keys[3], (), 1, back_cut)
    length = 2 * half
    places = jnp.arange(length, dtype=jnp.int32)
    marks = jnp.stack([inner_front, front_cut, length - back_cut, length - back_cut + inner_back]).astype(jnp.int32)
    return jnp.sum((places[:, None] >= marks[None, :]).astype(jnp.int32), axis=1)


def segment_table(key, salt_value):
    seq_count = MICRO * SIDE * TOKS // LEN
    keys_all = jax.random.split(jax.random.fold_in(key, salt_value), seq_count)
    seg_table = jax.vmap(lambda one_key: sequence_cuts(one_key, TOK_DEV))(keys_all)
    return seg_table.reshape(MICRO, SIDE, TOKS)


def draw_seg_target(key, part):
    return segment_table(key, 11)


def draw_seg_memory(key, part):
    return segment_table(key, 23)


def draw_attn_master(key, part):
    base_draw = jax.random.normal(key, (8, D, D), jnp.float32)
    row_index = jnp.arange(8)
    row_scale = jnp.where(row_index % 4 == 3, LEN ** 0.5 / 4.0, 1.0) * D ** (-0.5)
    return base_draw * row_scale[:, None, None]


def draw_vec_master(key, part):
    noise_draw = jax.random.normal(key, (17, D), jnp.float32)
    row_index = jnp.arange(17)
    is_gain = (row_index == 7) | (row_index == 9) | (row_index == 11)
    return jnp.where(is_gain[:, None], 1.0 + 0.15 * noise_draw, 0.3 * noise_draw)


def with_spikes(array, key, source, target, shards_of, factor):
    owner, partner = [(jnp.arange(array.shape[axis_at]) // (array.shape[axis_at] // shards_of)).reshape([-1 if axis == axis_at else 1 for axis in range(array.ndim)]) for axis_at in (source, target)]
    chosen = jax.random.permutation(key, shards_of)[partner]
    strong = (owner == chosen) | (owner == (partner + shards_of // 2) % shards_of)
    return jnp.where(strong, factor * array, array)


def steps_of(own_key, shape, cuts, low, high):
    loudness = 1.0
    for position, shards_of in cuts:
        steps = jax.random.uniform(jax.random.fold_in(jax.random.fold_in(own_key, 6), position), (shards_of,), jnp.float32, low / len(cuts), high / len(cuts))
        loudness = loudness * jnp.repeat(jnp.exp(steps), shape[position] // shards_of).reshape((-1,) + (1,) * (len(shape) - 1 - position))
    return loudness


def normal_values(stream_key, dims, scale, bound, cuts=(), kind=jnp.bfloat16):
    factor_of = steps_of(stream_key, dims, cuts, -0.22, 0.18) if cuts else 1.0
    values = jax.random.normal(stream_key, dims, jnp.float32) * scale * factor_of
    return jnp.minimum(jnp.maximum(values, -bound), bound).astype(kind)


def heavy_noise(stream_key, dims, scale, most, cuts, heavy, kind=jnp.bfloat16):
    values = scale * jax.random.normal(stream_key, dims, jnp.float32)
    if cuts:
        values = values * steps_of(stream_key, dims, cuts, -0.22, 0.18)
    return jnp.clip(with_spikes(values, jax.random.fold_in(stream_key, 3), *heavy), -most, most).astype(kind)


def setup_inputs(seed: int = 0) -> dict:
    key_of = jax.random.split(jax.random.key(seed), 18)
    return {
        "target": normal_values(key_of[0], (MICRO, SIDE, TOKS, D), 1.0, 6.0, ((1, 2), (2, 16))),
        "memory": normal_values(key_of[1], (MICRO, SIDE, TOKS, D), 1.0, 6.0, ((1, 2), (2, 16))),
        "cotangent": heavy_noise(key_of[2], (MICRO, SIDE, TOKS, D), 1.0, 6.0, ((1, 2), (2, 16)), (2, 3, 16, 2.0)),
        "seg_target": draw_seg_target(jax.random.fold_in(key_of[17], 71), 0),
        "seg_memory": draw_seg_memory(jax.random.fold_in(key_of[17], 71), 0),
        "attn_master": draw_attn_master(jax.random.fold_in(key_of[17], 71), 0),
        "attn_first": normal_values(key_of[6], (8, D, D), (0.5 * ALLTOK ** 0.5), 512.0, ((1, 32),), jnp.float32),
        "attn_second": jnp.clip(jnp.exp(math.log(32768.0) - 1.3862944 * jax.random.uniform(key_of[7], (8, D, D), jnp.float32) ** steps_of(key_of[7], (8, D, D), ((1, 32),), -0.2, 0.2)), 8192.0, 32768.0),
        "in_master": normal_values(key_of[8], (D, FF), D ** -0.5, 0.21875, ((0, 32),), jnp.float32),
        "in_first": normal_values(key_of[9], (D, FF), (0.25 * ALLTOK ** 0.5), 256.0, ((0, 32),), jnp.float32),
        "in_second": jnp.clip(jnp.exp(math.log(8192.0) - 1.3862944 * jax.random.uniform(key_of[10], (D, FF), jnp.float32) ** steps_of(key_of[10], (D, FF), ((0, 32),), -0.2, 0.2)), 2048.0, 8192.0),
        "out_master": normal_values(key_of[11], (FF, D), FF ** -0.5, 0.109375, ((0, 32),), jnp.float32),
        "out_first": normal_values(key_of[12], (FF, D), (0.6 * ALLTOK ** 0.5), 640.0, ((0, 32),), jnp.float32),
        "out_second": jnp.clip(jnp.exp(math.log(47185.92) - 1.3862944 * jax.random.uniform(key_of[13], (FF, D), jnp.float32) ** steps_of(key_of[13], (FF, D), ((0, 32),), -0.2, 0.2)), 11796.48, 47185.92),
        "vec_master": draw_vec_master(jax.random.fold_in(key_of[17], 71), 0),
        "vec_first": normal_values(key_of[15], (17, D), (ALLTOK ** 0.5), 1024.0, ((1, 32),), jnp.float32),
        "vec_second": jnp.clip(jnp.exp(math.log(131072.0) - 1.3862944 * jax.random.uniform(key_of[16], (17, D), jnp.float32) ** steps_of(key_of[16], (17, D), ((1, 32),), -0.2, 0.2)), 32768.0, 131072.0),
    }


@jax.custom_vjp
def low(v):
    return lax.optimization_barrier(v.astype(jnp.bfloat16)).astype(jnp.float32)

@jax.custom_vjp
def low_back(v):
    return v

def low_keep(v):
    return (low(v), None)

def low_pass(kept, grad):
    return (grad,)

def back_keep(v):
    return (v, None)

def back_low(kept, grad):
    return (low(grad),)
low.defvjp(low_keep, low_pass)
low_back.defvjp(back_keep, back_low)
precise = lax.Precision.HIGHEST
norm_eps = 1e-05
adam_eps = 1e-08

def product(left_side, right_side):
    return jnp.dot(left_side, right_side, precision=precise, preferred_element_type=jnp.float32)

def rounded_both(value_in):
    return low_back(low(value_in))

def layer_norm(residual, gain_row, shift_row):
    row_mean = lax.optimization_barrier(jnp.mean(residual, axis=-1, keepdims=True))
    centred = residual - row_mean
    row_var = lax.optimization_barrier(jnp.mean(centred * centred, axis=-1, keepdims=True))
    return centred * lax.rsqrt(row_var + norm_eps) * gain_row + shift_row

def attend(queries, key_rows, value_rows, allowed):
    length_q = queries.shape[0]
    length_k = key_rows.shape[0]
    heads_q = queries.reshape(length_q, HEADS, HDIM)
    heads_k = key_rows.reshape(length_k, HEADS, HDIM)
    heads_v = value_rows.reshape(length_k, HEADS, HDIM)
    scores = low_back(jnp.einsum('qhd,khd->hqk', heads_q, heads_k, precision=precise))
    scores = jnp.where(allowed[None], scores, -1e+30)
    row_top = lax.optimization_barrier(jnp.max(scores, axis=-1, keepdims=True))
    weights_exp = jnp.exp(scores - row_top)
    probs = weights_exp / lax.optimization_barrier(jnp.sum(weights_exp, axis=-1, keepdims=True))
    mixed_heads = jnp.einsum('hqk,khd->qhd', low(probs), heads_v, precision=precise)
    return rounded_both(mixed_heads.reshape(length_q, HEADS * HDIM))

def decoder_layer(weights, inputs, segments):
    attn_mats, w_in, w_out, vec_rows = weights
    target_rows, memory_rows = inputs
    seg_t, seg_m = segments
    ff_bias = vec_rows[13:17].reshape(FF)
    places = jnp.arange(LEN)
    self_ok = (places[:, None] >= places[None, :]) & (seg_t[:, None] == seg_t[None, :])
    cross_ok = seg_t[:, None] == seg_m[None, :]
    queries = rounded_both((product(target_rows, attn_mats[0]) + vec_rows[0]) * 0.125)
    key_rows = rounded_both(product(target_rows, attn_mats[1]))
    value_rows = rounded_both(product(target_rows, attn_mats[2]) + vec_rows[1])
    self_out = attend(queries, key_rows, value_rows, self_ok)
    branch_one = low_back(product(self_out, attn_mats[3]) + vec_rows[2])
    first_norm = layer_norm(target_rows + branch_one, vec_rows[7], vec_rows[8])
    first_low = low(first_norm)
    cross_q = rounded_both((product(first_low, attn_mats[4]) + vec_rows[3]) * 0.125)
    mem_keys = rounded_both(product(memory_rows, attn_mats[5]))
    mem_values = rounded_both(product(memory_rows, attn_mats[6]) + vec_rows[4])
    cross_out = attend(cross_q, mem_keys, mem_values, cross_ok)
    branch_two = low_back(product(cross_out, attn_mats[7]) + vec_rows[5])
    second_norm = layer_norm(first_norm + branch_two, vec_rows[9], vec_rows[10])
    second_low = low(second_norm)
    pre_act = low_back(product(second_low, w_in) + ff_bias)
    activated = low(jax.nn.gelu(pre_act, approximate=False))
    branch_three = low_back(product(activated, w_out) + vec_rows[6])
    return layer_norm(second_norm + branch_three, vec_rows[11], vec_rows[12])

def adam_step(master, first_m, second_m, grad_sum, rate, decay):
    first_new = 0.5 * first_m + 0.5 * grad_sum
    second_new = 0.5 * second_m + 0.5 * grad_sum * grad_sum
    fix_term = 1.0 - 0.5 ** STEP
    update = first_new / fix_term / (jnp.sqrt(second_new / fix_term) + adam_eps)
    master_new = master - rate * (update + decay * master)
    return (master_new, first_new, second_new, master_new.astype(jnp.bfloat16))

def reference(target, memory, cotangent, seg_target, seg_memory, attn_master, attn_first, attn_second, in_master, in_first, in_second, out_master, out_first, out_second, vec_master, vec_first, vec_second):
    masters = (attn_master, in_master, out_master, vec_master)
    weights = tuple((master_now.astype(jnp.bfloat16).astype(jnp.float32) for master_now in masters))
    seq_count = MICRO * SIDE * TOKS // LEN

    def regroup(array_in):
        return array_in.reshape((seq_count, LEN) + array_in.shape[3:])
    sequences = (regroup(target).astype(jnp.float32), regroup(memory).astype(jnp.float32), regroup(cotangent).astype(jnp.float32), regroup(seg_target), regroup(seg_memory))

    def per_sequence(totals, pieces):
        target_rows, memory_rows, cot_rows, seg_t, seg_m = pieces
        output_rows, layer_pull = jax.vjp(lambda weights_now, inputs_now: decoder_layer(weights_now, inputs_now, (seg_t, seg_m)), weights, (target_rows, memory_rows))
        grad_weights, grad_inputs = layer_pull(cot_rows)
        totals = jax.tree.map(jnp.add, totals, grad_weights)
        return (totals, (output_rows, grad_inputs[0], grad_inputs[1]))
    zeros_start = jax.tree.map(jnp.zeros_like, weights)
    grads, (outputs_all, grad_x_all, grad_e_all) = lax.scan(per_sequence, zeros_start, sequences)
    shape_out = (MICRO, SIDE, TOKS, D)
    block_out = outputs_all.reshape(shape_out)
    grad_target = grad_x_all.reshape(shape_out)
    grad_memory = grad_e_all.reshape(shape_out)
    attn_new, attn_m, attn_s, attn_w = adam_step(attn_master, attn_first, attn_second, grads[0], 0.1, 0.01)
    in_new, in_m, in_s, in_w = adam_step(in_master, in_first, in_second, grads[1], 0.05, 0.01)
    out_new, out_m, out_s, out_w = adam_step(out_master, out_first, out_second, grads[2], 0.03, 0.01)
    vec_new, vec_m, vec_s, vec_w = adam_step(vec_master, vec_first, vec_second, grads[3], 0.3, 0.0)
    return (block_out, grad_target, grad_memory, attn_new, attn_m, attn_s, attn_w, in_new, in_m, in_s, in_w, out_new, out_m, out_s, out_w, vec_new, vec_m, vec_s, vec_w)
```

```python
import functools

import jax
import jax.numpy as jnp
from jax import lax
from jax.experimental import pallas as pl
from jax.experimental.pallas import tpu as pltpu
from jax.sharding import PartitionSpec as P

HDIM = 64
STEP = 10
PAIR = 2 * HDIM
CHUNK = 256
DOCS = 5
MASKED = -1e30

BF = jnp.bfloat16
F32 = jnp.float32

norm_eps = 1e-05
adam_eps = 1e-08
VMEM_LIMIT = 58 * 2**20
COST = 0.1


def nn(a, b):
    return lax.dot_general(a, b, (((1,), (0,)), ((), ())), preferred_element_type=F32)


def nt(a, b):
    return lax.dot_general(a, b, (((1,), (1,)), ((), ())), preferred_element_type=F32)


def tn(a, b):
    return lax.dot_general(a, b, (((0,), (0,)), ((), ())), preferred_element_type=F32)


def call(name, kernel, grid, in_specs, out_specs, out_shape, operands, scratch=(), flops=0, prefetch=0):
    size = COST * sum(leaf.size * leaf.dtype.itemsize for leaf in list(operands) + list(out_shape))
    return pl.pallas_call(
        kernel,
        name=name,
        grid_spec=pltpu.PrefetchScalarGridSpec(
            num_scalar_prefetch=prefetch,
            grid=grid,
            in_specs=in_specs,
            out_specs=out_specs,
            scratch_shapes=scratch,
        ),
        out_shape=out_shape,
        compiler_params=pltpu.CompilerParams(vmem_limit_bytes=VMEM_LIMIT),
        cost_estimate=pl.CostEstimate(flops=int(COST * flops), bytes_accessed=int(size), transcendentals=0),
    )(*operands)


def shape(dims, dtype):
    return jax.ShapeDtypeStruct(tuple(dims), dtype)


def whole(array):
    zeros = (0,) * array.ndim
    return pl.BlockSpec(array.shape, lambda *_: zeros)


CORE = 2


def moved(array, flip):
    count = lax.axis_size("seq") * lax.axis_size("fsdp")
    return lax.ppermute(array, ("seq", "fsdp"), [(i, i ^ flip) for i in range(count)])


def own_bit(bit):
    if bit == 0:
        return lax.axis_index("fsdp")
    return (lax.axis_index("seq") >> (bit - 1)) & 1


def bit_sets(count):
    bits = [0] + list(range(2, count.bit_length() - 1))
    return [bits[i : i + 2] for i in range(0, len(bits), 2)]


def flips(bits):
    out = [0]
    for bit in bits:
        out = out + [f | 1 << bit for f in out]
    return out


def gather_bits(array, order, present=()):
    present = sorted(present, reverse=True)
    for bit in order:
        other = moved(array, 1 << bit)
        place = 1 + sum(b > bit for b in present)
        low = own_bit(bit) == 0
        array = jnp.stack([jnp.where(low, array, other), jnp.where(low, other, array)], axis=place)
        present = sorted(present + [bit], reverse=True)
    return array


def scatter_bits(array, order, present):
    present = sorted(present, reverse=True)
    for bit in order:
        place = 1 + present.index(bit)
        mine = own_bit(bit)
        send = lax.dynamic_index_in_dim(array, 1 - mine, place, keepdims=False)
        keep = lax.dynamic_index_in_dim(array, mine, place, keepdims=False)
        array = (keep.astype(F32) + moved(send, 1 << bit).astype(F32)).astype(BF)
        present.remove(bit)
    return array


def as_tile(rows, width):
    third = width // 3
    full = jnp.pad(rows, ((0, 24 - rows.shape[0]), (0, third - rows.shape[1])))
    return jnp.concatenate([full[0:8], full[8:16], full[16:24]], axis=1)


def from_tile(tile, count, columns):
    third = tile.shape[-1] // 3
    groups = [tile[..., n * third : n * third + columns] for n in range(3)]
    return jnp.concatenate(groups, axis=-2)[..., :count, :]


def far_parts(stacked, sets):
    rels, array = [0], stacked[None]
    for bits in sets[:0:-1]:
        got = [array] + [moved(array, f) for f in flips(bits)[1:]]
        rels = [f ^ r for f in flips(bits) for r in rels]
        array = jnp.concatenate(got, axis=0)
    return array, rels


def near_parts(array, sets):
    return [array] + [moved(array, f) for f in flips(sets[0])[1:]]


def assemble_kernel(near, rels, me_ref, *refs):
    parts, out = refs[: len(near)], refs[-1]
    for part, f in zip(parts, near):
        for i, r in enumerate(rels):
            for c in range(2):
                out[0, ((me_ref[0] & ~CORE) ^ (f ^ r)) + CORE * c] = part[i, c]


def part_specs(parts, rows):
    return [pl.BlockSpec((p.shape[0], 2, rows, p.shape[3]), lambda i, *_: (0, 0, i, 0)) for p in parts]


def assemble(me, parts, near, rels, rows):
    _, _, total, cols = parts[0].shape
    count = total // rows
    lots = 2 * len(near) * len(rels)
    out = call(
        "assemble",
        functools.partial(assemble_kernel, near, rels),
        (count,),
        part_specs(parts, rows),
        [pl.BlockSpec((1, lots, rows, cols), lambda i, *_: (i, 0, 0, 0))],
        [shape((count, lots, rows, cols), BF)],
        [me] + parts,
        prefetch=1,
    )[0]
    return out.reshape(count, lots * rows, cols)


def compact(number, removed):
    out, place = 0, 0
    for bit in range(number.bit_length()):
        if bit not in removed:
            out |= (number >> bit & 1) << place
            place += 1
    return out


def send_blocks(bits, gone, count, me, load, outs):
    kept = [b for b in range(count.bit_length() - 1) if b not in gone]
    mask = sum(1 << kept.index(b) for b in bits)
    here = 0
    for b in bits:
        here = here + (((me >> b) & 1) << kept.index(b))
    total = 1 << len(kept)
    for f, out in zip(flips(bits), outs):
        small = sum(((f >> b) & 1) << kept.index(b) for b in bits)
        j = 0
        for k in range(total):
            if k & mask == 0:
                out(j, load((here ^ small) + k))
                j += 1


def combine_kernel(bits, gone, count, me_ref, *refs):
    outs = refs[-(1 << len(bits)) :]
    ins = refs[: len(refs) - len(outs)]

    def load(k):
        total = ins[0][k].astype(F32)
        for ref in ins[1:]:
            total = total + ref[k].astype(F32)
        return total.astype(BF)

    def store(out):
        def put(j, value):
            out[j] = value

        return put

    send_blocks(bits, gone, count, me_ref[0], load, [store(out) for out in outs])


def combine(me, arrays, bits, gone, count):
    blocks = arrays[0].shape[0] >> len(bits)
    out = shape((blocks,) + arrays[0].shape[1:], BF)
    return call(
        "combine",
        functools.partial(combine_kernel, bits, gone, count),
        (1,),
        [whole(a) for a in arrays],
        [whole(out)] * (1 << len(bits)),
        [out] * (1 << len(bits)),
        [me] + arrays,
        prefetch=1,
    )


def reduce_near(me, outs, sets, count, beside=None):
    got = [outs[0]] + [moved(out, f) for out, f in zip(outs[1:], flips(sets[0])[1:])]
    if beside is not None:
        got[0], beside = lax.optimization_barrier((got[0], beside))
    return combine(me, got, (sets[1:] + [[1]])[0], sets[0], count), beside


def reduce_far(me, outs, sets, count, beside=()):
    gone, beside = sets[0], list(beside)
    for n, (here, after) in enumerate(zip(sets[1:], sets[2:] + [[1]])):
        gone = gone + here
        got = [outs[0]] + [moved(out, f) for out, f in zip(outs[1:], flips(here)[1:])]
        if n < len(beside):
            got[0], beside[n] = lax.optimization_barrier((got[0], beside[n]))
        outs = combine(me, got, after, gone, count)
    return outs[0][0], moved(outs[1], CORE)[0], beside


def both_halves(is_low, mine, other):
    return jnp.concatenate([jnp.where(is_low, mine, other), jnp.where(is_low, other, mine)], axis=-1)


def with_marks(pair, seg, half, lanes, is_key):
    mark = lanes - (HDIM if half == 0 else 0)
    mine = (lanes < HDIM) if half == 0 else (lanes >= HDIM)
    hit = seg == mark
    if is_key:
        extra = jnp.where(hit, 1.0, 0.0)
    else:
        extra = jnp.where(hit | (mark < 0) | (mark >= DOCS), 0.0, MASKED)
    return jnp.where(mine, pair.astype(F32), extra).astype(BF)


def down(row):
    return jnp.broadcast_to(row, (PAIR, row.shape[1])).T


def causal_tile():
    keys = lax.broadcasted_iota(jnp.int32, (CHUNK, CHUNK), 0)
    places = lax.broadcasted_iota(jnp.int32, (CHUNK, CHUNK), 1)
    return jnp.where(places >= keys, 0.0, MASKED)


def masked_scores(keys, queries, c, causal, tile):
    length = keys.shape[0]
    end = (c + 1) * CHUNK if causal else length
    s = nt(keys[:end], queries[c * CHUNK : (c + 1) * CHUNK])
    if causal:
        last = s[c * CHUNK :] + tile
        s = jnp.concatenate([s[: c * CHUNK], last], axis=0) if c else last
    return s


def halves_in(ref_a, ref_b, core, scratch):
    rows = ref_a.shape[-2]
    if core is None:
        scratch[0:rows, :] = ref_a[...].reshape(rows, PAIR)
        scratch[rows:, :] = ref_b[...].reshape(rows, PAIR)
    else:
        scratch[pl.ds(pl.multiple_of(core * rows, rows), rows), :] = ref_a[...].reshape(rows, PAIR)
        scratch[pl.ds(pl.multiple_of((1 - core) * rows, rows), rows), :] = ref_b[...].reshape(rows, PAIR)


def halves_out(scratch, core, ref_a, ref_b):
    rows = scratch.shape[0] // 2
    if core is None:
        a, b = scratch[0:rows, :], scratch[rows:, :]
    else:
        a = scratch[pl.ds(pl.multiple_of(core * rows, rows), rows), :]
        b = scratch[pl.ds(pl.multiple_of((1 - core) * rows, rows), rows), :]
    ref_a[...] = a.reshape(ref_a.shape)
    ref_b[...] = b.reshape(ref_b.shape)


def forward_kernel(causal, core_ref, *refs):
    if causal:
        q_ref, k_ref, v_ref, sq_ref, sk_ref, own_ref, send_ref, exact_ref, log_ref, out_s = refs
        core = core_ref[0]
        q = q_ref[0, 0]
    else:
        qa_ref, qb_ref, k_ref, v_ref, sq_ref, sk_ref, own_ref, send_ref, exact_ref, log_ref, out_s = refs
        core = None
        q = jnp.concatenate([qa_ref[0], qb_ref[0]], axis=0)
    k, v = k_ref[0, 0], v_ref[0, 0]
    sq, sk = down(sq_ref[0]), down(sk_ref[0])
    length = k.shape[0]
    lanes = lax.broadcasted_iota(jnp.int32, (length, PAIR), 1)
    rows = lax.broadcasted_iota(jnp.int32, (PAIR, CHUNK), 0)
    tile = causal_tile() if causal else None
    heads = []
    for half in range(2):
        mine = (lanes < HDIM) if half == 0 else (lanes >= HDIM)
        heads.append(
            (
                with_marks(q, sq, half, lanes, False),
                with_marks(k, sk, half, lanes, True),
                jnp.where(mine, v.astype(F32), 1.0).T.astype(BF),
            )
        )
    done = {}

    def scores(c, half):
        return masked_scores(heads[half][1], heads[half][0], c, causal, tile)

    def finish(c, half, s):
        top = jnp.max(s, axis=0, keepdims=True)
        p = jnp.exp(s - top).astype(BF)
        mixed = nn(heads[half][2][:, : s.shape[0]], p)
        total = mixed[HDIM : HDIM + 1] if half == 0 else mixed[0:1]
        done[half] = (mixed * (1.0 / total), top + jnp.log(total))
        if half == 1:
            cs = slice(c * CHUNK, (c + 1) * CHUNK)
            both = jnp.where(rows < HDIM, done[0][0], done[1][0]).T
            exact_ref[0, cs, :] = both
            out_s[cs, :] = both.astype(BF)
            log_ref[0, 0, 0:1, cs] = done[0][1]
            log_ref[0, 0, 1:2, cs] = done[1][1]

    jobs = [(c, half) for c in reversed(range(length // CHUNK)) for half in range(2)]
    waiting = None
    for job in jobs:
        s = scores(*job)
        if waiting is not None:
            finish(*waiting)
        waiting = (*job, s)
    finish(*waiting)
    halves_out(out_s, core, own_ref, send_ref)


def backward_kernel(causal, core_ref, *refs):
    if causal:
        q_ref, k_ref, v_ref, sq_ref, sk_ref, ga_ref, gb_ref, exact_ref, log_ref = refs[:9]
        own_ref, send_ref, sum_ref, p_s, ds_s, g_s, out_s = refs[9:]
        core = core_ref[0]
        q = q_ref[0, 0]
    else:
        qa_ref, qb_ref, k_ref, v_ref, sq_ref, sk_ref, ga_ref, gb_ref, exact_ref, log_ref = refs[:10]
        own_ref, send_ref, kv_own_ref, kv_oth_ref, sum_ref, p_s, ds_s, g_s, out_s = refs[10:]
        core = None
        q = jnp.concatenate([qa_ref[0], qb_ref[0]], axis=0)
    k, v = k_ref[0, 0], v_ref[0, 0]
    sq, sk = down(sq_ref[0]), down(sk_ref[0])
    length = k.shape[0]
    chunks = length // CHUNK
    halves_in(ga_ref, gb_ref, core, g_s)
    grad = g_s[...]
    lanes = lax.broadcasted_iota(jnp.int32, (length, PAIR), 1)
    tile = causal_tile() if causal else None
    pick = lax.broadcasted_iota(jnp.int32, (8, PAIR), 1) // HDIM == lax.broadcasted_iota(jnp.int32, (8, PAIR), 0)
    delta = lax.dot_general(
        jnp.where(pick, 1.0, 0.0),
        grad.astype(F32) * exact_ref[0],
        (((1,), (1,)), ((), ())),
        precision=lax.Precision.HIGHEST,
        preferred_element_type=F32,
    )
    heads = []
    for half in range(2):
        mine = (lanes < HDIM) if half == 0 else (lanes >= HDIM)
        only = lambda a: jnp.where(mine, a.astype(F32), 0.0)
        heads.append(
            dict(
                q=with_marks(q, sq, half, lanes, False),
                k=with_marks(k, sk, half, lanes, True),
                qm=only(q).astype(BF),
                kt=only(k).T.astype(BF),
                gm=only(grad).astype(BF),
                log=log_ref[0, 0, half : half + 1, :],
                delta=delta[half : half + 1, :],
            )
        )
    dq, dk, dv = {}, {}, {}

    def products(c, half):
        h = heads[half]
        cs = slice(c * CHUNK, (c + 1) * CHUNK)
        s = masked_scores(h["k"], h["q"], c, causal, tile)
        return s, nt(v[: s.shape[0]], h["gm"][cs])

    def finish(c, half, s, dp):
        h = heads[half]
        cs = slice(c * CHUNK, (c + 1) * CHUNK)
        end = s.shape[0]
        p = jnp.exp(s - h["log"][:, cs])
        ds = (p * (dp - h["delta"][:, cs])).astype(BF)
        p_s[half, :end, cs] = p.astype(BF)
        ds_s[half, :end, cs] = ds
        t = nn(h["kt"][:, :end], ds)
        dq[c] = t if half == 0 else dq[c] + t

    def keys_side(kb, half):
        h = heads[half]
        q0 = kb * CHUNK if causal else 0
        ks = slice(kb * CHUNK, (kb + 1) * CHUNK)
        a = nn(p_s[half, ks, q0:], h["gm"][q0:])
        b = nn(ds_s[half, ks, q0:], h["qm"][q0:])
        dv[kb] = a if half == 0 else dv[kb] + a
        dk[kb] = b if half == 0 else dk[kb] + b

    waiting = None
    for half in range(2):
        for c in range(chunks):
            pair = products(c, half)
            if waiting is not None:
                finish(*waiting)
            waiting = (c, half, *pair)
            if half == 1 and c > 0:
                keys_side(c - 1, 0)
    finish(*waiting)
    keys_side(chunks - 1, 0)
    for kb in range(chunks):
        keys_side(kb, 1)

    def put(n, parts):
        low = [part.astype(BF) for part in parts]
        for c in range(chunks):
            out_s[n, c * CHUNK : (c + 1) * CHUNK, :] = low[c]
        return sum(jnp.sum(one.astype(F32), axis=0, keepdims=True) for one in low)

    sum_q = put(0, [dq[c].T.astype(BF).astype(F32) * 0.125 for c in range(chunks)])
    sum_k = put(1, [dk[c] for c in range(chunks)])
    sum_v = put(2, [dv[c] for c in range(chunks)])
    pad = jnp.zeros((5, PAIR), F32)
    sum_ref[0] = jnp.concatenate([sum_q, sum_k, sum_v, pad], axis=0)
    if causal:
        for n in range(3):
            halves_out(out_s.at[n], core, own_ref.at[n], send_ref.at[n])
    else:
        halves_out(out_s.at[0], core, own_ref, send_ref)
        for n in range(2):
            halves_out(out_s.at[1 + n], None, kv_own_ref.at[n], kv_oth_ref.at[n])


def attention(causal, core, queries, keys, seg_q, seg_k, backward=None):
    source, k_at = keys
    _, micro, length, width = source.shape
    pairs = width // PAIR
    part = pl.BlockSpec((1, length // 2, PAIR), lambda i, j, s: (i, 0, j))
    full = pl.BlockSpec((1, length, PAIR), lambda i, j, s: (i, 0, j))
    at = lambda n: pl.BlockSpec((1, 1, length, PAIR), lambda i, j, s: (n, i, 0, j))
    seg = pl.BlockSpec((1, 1, length), lambda i, j, s: (i, 0, 0))
    stat = pl.BlockSpec((1, 1, 8, length), lambda i, j, s: (i, j, 0, 0))
    if causal:
        operands, specs = [source], [at(0)]
    else:
        operands, specs = list(queries), [part, part]
    operands += [source, source, seg_q, seg_k]
    specs += [at(k_at), at(k_at + 1), seg, seg]
    share = 0.625 if causal else 1.0
    unit = 2 * micro * pairs * 2 * length * length * PAIR * share
    half_out = shape((micro, length // 2, width), BF)
    if backward is None:
        return call(
            "attend",
            functools.partial(forward_kernel, causal),
            (micro, pairs),
            specs,
            [part, part, full, stat],
            [half_out, half_out, shape((micro, length, width), F32), shape((micro, pairs, 8, length), F32)],
            [core] + operands,
            scratch=[pltpu.VMEM((length, PAIR), BF)],
            flops=unit * 2,
            prefetch=1,
        )
    operands += list(backward)
    specs += [part, part, full, stat]
    sums = pl.BlockSpec((1, 8, PAIR), lambda i, j, s: (i, 0, j))
    scratch = [
        pltpu.VMEM((2, length, length), BF),
        pltpu.VMEM((2, length, length), BF),
        pltpu.VMEM((length, PAIR), BF),
        pltpu.VMEM((3, length, PAIR), BF),
    ]
    if causal:
        part3 = pl.BlockSpec((3, 1, length // 2, PAIR), lambda i, j, s: (0, i, 0, j))
        outs = [part3, part3, sums]
        shapes = [shape((3, micro, length // 2, width), BF)] * 2
    else:
        part2 = pl.BlockSpec((2, 1, length // 2, PAIR), lambda i, j, s: (0, i, 0, j))
        outs = [part, part, part2, part2, sums]
        shapes = [half_out, half_out] + [shape((2, micro, length // 2, width), BF)] * 2
    return call(
        "attend_back",
        functools.partial(backward_kernel, causal),
        (micro, pairs),
        specs,
        outs,
        shapes + [shape((micro, 8, width), F32)],
        [core] + operands,
        scratch=scratch,
        flops=unit * 5,
        prefetch=1,
    )


def project_kernel(first_scale, ordered, gather, *refs):
    core_ref, refs = refs[0], refs[1:]
    if gather is None:
        a_ref, b_ref, w_ref, bias_ref, out_ref = refs
        mat = w_ref[0]
    else:
        near, rels = gather
        me_ref, a_ref, b_ref = refs[:3]
        parts = refs[3 : 3 + len(near)]
        bias_ref, out_ref, mat_ref = refs[3 + len(near) :]
        assemble_kernel(near, rels, me_ref, *parts, mat_ref)
        mat = mat_ref[0].reshape(a_ref.shape[-1], mat_ref.shape[-1])
    rows = a_ref.shape[1]
    scale = jnp.where(pl.program_id(0) == 0, first_scale, 1.0).astype(F32)
    for m in range(a_ref.shape[0]):
        for slot, ref in enumerate((a_ref, b_ref)):
            low = ((nn(ref[m], mat) + bias_ref[0]) * scale).astype(BF)
            place = (core_ref[0] ^ slot) * rows if ordered else slot * rows
            out_ref[0, m, pl.ds(pl.multiple_of(place, rows), rows), :] = low


def project(core, me, own, other, mats, biases, scale, ordered):
    micro, rows, depth = own.shape
    count, _, width = biases.shape
    tokens = pl.BlockSpec(own.shape, lambda i, *_: (0, 0, 0))
    mat_spec = pl.BlockSpec((1, depth, width), lambda i, *_: (i, 0, 0))
    bias_spec = pl.BlockSpec((1, 1, width), lambda i, *_: (i, 0, 0))
    out_specs = [pl.BlockSpec((1, micro, 2 * rows, width), lambda i, *_: (i, 0, 0, 0))]
    out_shape = [shape((count, micro, 2 * rows, width), BF)]
    flops = 2 * count * micro * 2 * rows * depth * width
    if not isinstance(mats, tuple):
        out = call(
            "project",
            functools.partial(project_kernel, scale, ordered, None),
            (count,),
            [tokens, tokens, mat_spec, bias_spec],
            out_specs,
            out_shape,
            [core, own, other, mats, biases],
            flops=flops,
            prefetch=1,
        )[0]
        return out, mats
    parts, near, rels = mats
    lot = depth // (2 * len(near) * len(rels))
    out, full = call(
        "project",
        functools.partial(project_kernel, scale, ordered, (near, rels)),
        (count,),
        [tokens, tokens] + part_specs(parts, lot) + [bias_spec],
        out_specs + [pl.BlockSpec((1, depth // lot, lot, width), lambda i, *_: (i, 0, 0, 0))],
        out_shape + [shape((count, depth // lot, lot, width), BF)],
        [core, me, own, other] + parts + [biases],
        flops=flops,
        prefetch=2,
    )
    return out, full.reshape(count, depth, width)


def normalise(r):
    mean = jnp.mean(r, axis=-1, keepdims=True)
    centred = r - mean
    rstd = lax.rsqrt(jnp.mean(centred * centred, axis=-1, keepdims=True) + norm_eps)
    return centred * rstd, rstd


def norm_back(dz, xhat, rstd, gain):
    dxhat = dz * gain
    a = jnp.mean(dxhat, axis=-1, keepdims=True)
    b = jnp.mean(dxhat * xhat, axis=-1, keepdims=True)
    return (dxhat - a - xhat * b) * rstd


def col_sum(a):
    return jnp.sum(a.astype(F32), axis=0, keepdims=True)


def own_part(core, swap, width):
    return pl.ds(pl.multiple_of((core ^ swap) * width, width), width)


def join_columns(core, own_ref, oth_ref, scratch):
    width = own_ref.shape[-1]
    scratch[:, own_part(core, 0, width)] = own_ref[...]
    scratch[:, own_part(core, 1, width)] = oth_ref[...]


def after_self_kernel(
    core_ref, own_ref, oth_ref, x_ref, mat_ref, moth_ref, vec_ref, xhat_ref, rstd_ref, low_ref, qa_ref, qb_ref, out_s
):
    core = core_ref[0]
    width = own_ref.shape[1]

    @pl.when(pl.program_id(0) == 0)
    def _():
        join_columns(core, mat_ref.at[0], moth_ref.at[0], out_s)

    mixed = nn(own_ref[...], out_s[own_part(core, 0, width), :]) + nn(oth_ref[...], out_s[own_part(core, 1, width), :])
    r = x_ref[...].astype(F32) + mixed + vec_ref[2:3]
    xhat, rstd = normalise(r)
    xhat_ref[...] = xhat
    rstd_ref[...] = rstd
    low = (xhat * vec_ref[7:8] + vec_ref[8:9]).astype(BF)
    low_ref[...] = low
    qa_ref[...] = ((nn(low, mat_ref[1]) + vec_ref[3:4, own_part(core, 0, width)]) * 0.125).astype(BF)
    qb_ref[...] = ((nn(low, moth_ref[1]) + vec_ref[3:4, own_part(core, 1, width)]) * 0.125).astype(BF)


def first_two(mats):
    return pl.BlockSpec((2,) + mats.shape[1:], lambda *_: (0, 0, 0))


def after_self(core, own, other, x, mats, mats_other, vec, tile):
    tokens, dim = x.shape
    rows = lambda w: pl.BlockSpec((tile, w), lambda i, s: (i, 0))
    half = dim // 2
    return call(
        "after_self",
        after_self_kernel,
        (tokens // tile,),
        [rows(half), rows(half), rows(dim), first_two(mats), first_two(mats), whole(vec)],
        [rows(dim), rows(1), rows(dim), rows(half), rows(half)],
        [
            shape((tokens, dim), F32),
            shape((tokens, 1), F32),
            shape((tokens, dim), BF),
            shape((tokens, half), BF),
            shape((tokens, half), BF),
        ],
        [core, own, other, x, mats, mats_other, vec],
        scratch=[pltpu.VMEM((dim, dim), BF)],
        flops=4 * tokens * dim * dim,
        prefetch=1,
    )


LOTS = 32


def packed_in(pack_ref, n):
    lots, dim = pack_ref.shape[0], pack_ref.shape[2]
    lot = dim // lots
    return pack_ref[:, n * lot : (n + 1) * lot, :].reshape(dim, dim)


def packed_out(pack_ref, n):
    lots, dim = pack_ref.shape[0], pack_ref.shape[2]
    lot, some = dim // lots, lots // 4
    return pack_ref[n * some : (n + 1) * some, 4 * lot : 8 * lot, :].reshape(dim, dim)


def packed_cross(pack_ref, core, swap):
    lots, dim = pack_ref.shape[0], pack_ref.shape[2]
    lot, some = dim // lots, lots // 2
    return pack_ref[own_part(core, swap, some), 8 * lot : 9 * lot, :].reshape(dim // 2, dim)


def middle_kernel(
    core_ref,
    own_ref,
    oth_ref,
    xhat1_ref,
    cot_ref,
    pack_ref,
    vec_ref,
    block_ref,
    act_ref,
    dpre_ref,
    low2_ref,
    e3_ref,
    dr2_ref,
    br2_ref,
    ga_ref,
    gb_ref,
    vsum_ref,
    fsum_ref,
    slope_s,
):
    core = core_ref[0]
    dim = xhat1_ref.shape[1]
    hidden = act_ref.shape[1]
    step = dim
    first = xhat1_ref[...] * vec_ref[7:8] + vec_ref[8:9]
    mixed = nn(own_ref[...], packed_cross(pack_ref, core, 0)) + nn(oth_ref[...], packed_cross(pack_ref, core, 1))
    r2 = first + mixed + vec_ref[5:6]
    xhat2, rstd2 = normalise(r2)
    second = xhat2 * vec_ref[9:10] + vec_ref[10:11]
    low2 = second.astype(BF)
    low2_ref[...] = low2
    r3 = second + vec_ref[6:7]
    for n in range(hidden // step):
        cs = slice(n * step, (n + 1) * step)
        pre = nn(low2, packed_in(pack_ref, n)) + vec_ref[13 + n : 14 + n]
        phi = 0.5 * (1.0 + lax.erf(pre * 0.7071067811865476))
        act = (pre * phi).astype(BF)
        act_ref[:, cs] = act
        slope_s[:, cs] = phi + pre * (jnp.exp(-0.5 * pre * pre) * 0.3989422804014327)
        r3 = r3 + nn(act, packed_out(pack_ref, n))
    xhat3, rstd3 = normalise(r3)
    block_ref[...] = xhat3 * vec_ref[11:12] + vec_ref[12:13]
    dz = cot_ref[...].astype(F32)
    dr3 = norm_back(dz, xhat3, rstd3, vec_ref[11:12])
    e3 = dr3.astype(BF)
    e3_ref[...] = e3
    back = dr3
    fsums = []
    for n in range(hidden // step):
        cs = slice(n * step, (n + 1) * step)
        dpre = (nt(e3, packed_out(pack_ref, n)) * slope_s[:, cs]).astype(BF)
        dpre_ref[:, cs] = dpre
        fsums.append(col_sum(dpre))
        back = back + nt(dpre, packed_in(pack_ref, n))
    dr2 = norm_back(back, xhat2, rstd2, vec_ref[9:10])
    dr2_ref[...] = dr2
    br2 = dr2.astype(BF)
    br2_ref[...] = br2
    ga_ref[...] = nt(br2, packed_cross(pack_ref, core, 0)).astype(BF)
    gb_ref[...] = nt(br2, packed_cross(pack_ref, core, 1)).astype(BF)
    zero = jnp.zeros((2, dim), F32)
    sums = jnp.concatenate(
        [col_sum(br2), col_sum(e3), col_sum(back * xhat2), col_sum(back), col_sum(dz * xhat3), col_sum(dz), zero],
        axis=0,
    )
    fsum = jnp.concatenate(fsums + [jnp.zeros((8 - len(fsums), dim), F32)], axis=0)
    first_step = pl.program_id(0) == 0
    vsum_ref[...] = jnp.where(first_step, 0.0, vsum_ref[...]) + sums
    fsum_ref[...] = jnp.where(first_step, 0.0, fsum_ref[...]) + fsum


def middle(core, own, other, xhat1, cot, pack, vec, tile):
    tokens, dim = xhat1.shape
    hidden = 4 * dim
    half = dim // 2
    rows = lambda w: pl.BlockSpec((tile, w), lambda i, s: (i, 0))
    once = lambda a: pl.BlockSpec(a.shape, lambda *_: (0,) * a.ndim, pipeline_mode=pl.Buffered(1))
    sums = pl.BlockSpec((8, dim), lambda i, s: (0, 0))
    return call(
        "middle",
        middle_kernel,
        (tokens // tile,),
        [rows(half), rows(half), rows(dim), rows(dim), once(pack), once(vec)],
        [
            rows(dim),
            rows(hidden),
            rows(hidden),
            rows(dim),
            rows(dim),
            rows(dim),
            rows(dim),
            rows(half),
            rows(half),
            sums,
            sums,
        ],
        [
            shape((tokens, dim), F32),
            shape((tokens, hidden), BF),
            shape((tokens, hidden), BF),
            shape((tokens, dim), BF),
            shape((tokens, dim), BF),
            shape((tokens, dim), F32),
            shape((tokens, dim), BF),
            shape((tokens, half), BF),
            shape((tokens, half), BF),
            shape((8, dim), F32),
            shape((8, dim), F32),
        ],
        [core, own, other, xhat1, cot, pack, vec],
        scratch=[pltpu.VMEM((tile, hidden), F32)],
        flops=tokens * (4 * dim * dim + 8 * dim * hidden),
        prefetch=1,
    )


def before_self_kernel(
    core_ref,
    own_ref,
    oth_ref,
    dr2_ref,
    xhat_ref,
    rstd_ref,
    mat_ref,
    moth_ref,
    vec_ref,
    dr1_ref,
    br1_ref,
    ga_ref,
    gb_ref,
    vsum_ref,
    out_s,
):
    core = core_ref[0]
    width = own_ref.shape[1]

    @pl.when(pl.program_id(0) == 0)
    def _():
        join_columns(core, mat_ref.at[0], moth_ref.at[0], out_s)

    dfirst = dr2_ref[...] + nt(own_ref[...], mat_ref[1]) + nt(oth_ref[...], moth_ref[1])
    xhat = xhat_ref[...]
    dr1 = norm_back(dfirst, xhat, rstd_ref[...], vec_ref[7:8])
    dr1_ref[...] = dr1
    br1 = dr1.astype(BF)
    br1_ref[...] = br1
    ga_ref[...] = nt(br1, out_s[own_part(core, 0, width), :]).astype(BF)
    gb_ref[...] = nt(br1, out_s[own_part(core, 1, width), :]).astype(BF)
    zero = jnp.zeros((5, xhat.shape[1]), F32)
    sums = jnp.concatenate([col_sum(br1), col_sum(dfirst * xhat), col_sum(dfirst), zero], axis=0)
    vsum_ref[...] = jnp.where(pl.program_id(0) == 0, 0.0, vsum_ref[...]) + sums


def before_self(core, own, other, dr2, xhat, rstd, mats, mats_other, vec, tile):
    tokens, dim = xhat.shape
    half = dim // 2
    rows = lambda w: pl.BlockSpec((tile, w), lambda i, s: (i, 0))
    return call(
        "before_self",
        before_self_kernel,
        (tokens // tile,),
        [rows(half), rows(half), rows(dim), rows(dim), rows(1), first_two(mats), first_two(mats), whole(vec)],
        [rows(dim), rows(dim), rows(half), rows(half), pl.BlockSpec((8, dim), lambda i, s: (0, 0))],
        [
            shape((tokens, dim), F32),
            shape((tokens, dim), BF),
            shape((tokens, half), BF),
            shape((tokens, half), BF),
            shape((8, dim), F32),
        ],
        [core, own, other, dr2, xhat, rstd, mats, mats_other, vec],
        scratch=[pltpu.VMEM((dim, dim), BF)],
        flops=4 * tokens * dim * dim,
        prefetch=1,
    )


def pair_grads_kernel(route, me_ref, xt_ref, yt_ref, a_ref, b_ref, *refs):
    n = pl.program_id(0)
    total = (nn(xt_ref[...], a_ref[0]) + nn(yt_ref[...], b_ref[0])).astype(BF)
    if route is None:
        refs[0][0] = total
        return
    bits, devices = route
    tile_ref, outs, block_s = refs[0], refs[1:-1], refs[-1]
    block_s[...] = total.reshape(block_s.shape)
    lot = block_s.shape[1]
    rows = pl.ds(pl.multiple_of(n * lot, lot), lot)
    last = outs[0].shape[1] - 8

    def store(out):
        def put(j, value):
            out[j, rows, :] = value

        return put

    def store_tile(out):
        def put(j, value):
            out[j, last:, :] = value

        return put

    send_blocks(bits, [], devices, me_ref[0], lambda k: block_s[k], [store(out) for out in outs])

    @pl.when(n == 0)
    def _():
        send_blocks(bits, [], devices, me_ref[0], lambda k: tile_ref[k], [store_tile(out) for out in outs])


def pair_grads(me, xt, yt, own, other, route=None):
    count, tokens, width = own.shape
    dim = xt.shape[0]
    grads = pl.BlockSpec((1, tokens, width), lambda i, *_: (i, 0, 0))
    operands, specs = [me, xt, yt, own, other], [whole(xt), whole(yt), grads, grads]
    if route is None:
        outs = [pl.BlockSpec((1, dim, width), lambda i, *_: (i, 0, 0))]
        shapes, scratch = [shape((count, dim, width), BF)], []
    else:
        bits, tiles = route
        devices = tiles.shape[0]
        lot, blocks = dim // devices, devices >> len(bits)
        shapes = [shape((blocks, count * lot + 8, width), BF)] * (1 << len(bits))
        outs = [whole(one) for one in shapes]
        scratch = [pltpu.VMEM((devices, lot, width), BF)]
        operands, specs, route = operands + [tiles], specs + [whole(tiles)], (bits, devices)
    return call(
        "pair_grads",
        functools.partial(pair_grads_kernel, route),
        (count,),
        specs,
        outs,
        shapes,
        operands,
        scratch=scratch,
        flops=4 * count * tokens * width * dim,
        prefetch=1,
    )


def route_sums(me, mine, received, plain, bits, count):
    lots = count
    _, dim, width = mine.shape
    lot = dim // lots
    total = mine.shape[0] + plain.shape[0]
    view = lambda a: a.reshape(a.shape[0], lots, lot, width)
    out = shape((lots >> len(bits), total, lot, width), BF)
    operands = [view(mine), view(received), view(plain)]

    def kernel(me_ref, a_ref, b_ref, p_ref, *outs):
        def load(k):
            both = (a_ref[:, k].astype(F32) + b_ref[:, k].astype(F32)).astype(BF)
            return both, p_ref[:, k]

        def store(out):
            def put(j, value):
                out[j, : a_ref.shape[0]] = value[0]
                out[j, a_ref.shape[0] :] = value[1]

            return put

        send_blocks(bits, [], count, me_ref[0], load, [store(o) for o in outs])

    return call(
        "route_sums",
        kernel,
        (1,),
        [whole(o) for o in operands],
        [whole(out)] * (1 << len(bits)),
        [out] * (1 << len(bits)),
        [me] + operands,
        prefetch=1,
    )


def token_grads_kernel(core_ref, so_ref, st_ref, br1_ref, low_ref, qo_ref, qt_ref, co_ref, ct_ref, br2_ref, mine_ref, away_ref, full_s):
    core = core_ref[0]
    width = so_ref.shape[1]

    def by_rows(own, other, grad, n):
        full_s[own_part(core, 0, width), :] = tn(own[...], grad[...]).astype(BF)
        full_s[own_part(core, 1, width), :] = tn(other[...], grad[...]).astype(BF)
        mine_ref[n] = full_s[:, own_part(core, 0, width)]
        away_ref[n] = full_s[:, own_part(core, 1, width)]

    by_rows(so_ref, st_ref, br1_ref, 0)
    mine_ref[1] = tn(low_ref[...], qo_ref[...]).astype(BF)
    away_ref[1] = tn(low_ref[...], qt_ref[...]).astype(BF)
    by_rows(co_ref, ct_ref, br2_ref, 2)


def token_grads(core, self_own, self_other, br1, low1, dcq_own, dcq_other, cross_own, cross_other, br2):
    operands = [self_own, self_other, br1, low1, dcq_own, dcq_other, cross_own, cross_other, br2]
    tokens, dim = br1.shape
    out = shape((3, dim, dim // 2), BF)
    return call(
        "token_grads",
        token_grads_kernel,
        (1,),
        [whole(o) for o in operands],
        [whole(out)] * 2,
        [out] * 2,
        [core] + operands,
        scratch=[pltpu.VMEM((dim, dim), BF)],
        flops=6 * tokens * dim * dim,
        prefetch=1,
    )


def feed_grads_kernel(low_ref, dpre_ref, act_ref, e3_ref, out_ref, low_s):
    n = pl.program_id(0)

    @pl.when(n == 0)
    def _():
        low_s[...] = low_ref[...].T

    lots, _, dim = out_ref.shape
    lot, some = dim // lots, lots // 4
    win = nn(low_s[...], dpre_ref[...]).astype(BF)
    out_ref[:, pl.ds(pl.multiple_of(n * lot, lot), lot), :] = win.reshape(lots, lot, dim)
    wout = tn(act_ref[...], e3_ref[...]).astype(BF)
    out_ref[pl.ds(pl.multiple_of(n * some, some), some), 4 * lot : 8 * lot, :] = wout.reshape(some, 4 * lot, dim)


def feed_grads(low2, dpre, act, e3):
    tokens, dim = low2.shape
    out = shape((LOTS, 8 * dim // LOTS, dim), BF)
    block = pl.BlockSpec((tokens, dim), lambda i: (0, i))
    return call(
        "feed_grads",
        feed_grads_kernel,
        (4,),
        [whole(low2), block, block, whole(e3)],
        [whole(out)],
        [out],
        [low2, dpre, act, e3],
        scratch=[pltpu.VMEM((dim, tokens), BF)],
        flops=16 * tokens * dim * dim,
    )[0]


def vec_rows_kernel(core_ref, self_ref, cross_ref, first_ref, mid_ref, ff_ref, out_ref, tiles_ref=None):
    core = core_ref[0]
    width = self_ref.shape[2]
    out_ref[...] = jnp.zeros_like(out_ref)
    self_sum, cross_sum = self_ref[0], cross_ref[0]
    for m in range(1, self_ref.shape[0]):
        self_sum, cross_sum = self_sum + self_ref[m], cross_sum + cross_ref[m]
    own = own_part(core, 0, width)
    out_ref[0:1, own] = self_sum[0:1]
    out_ref[1:2, own] = self_sum[2:3]
    out_ref[3:4, own] = cross_sum[0:1]
    out_ref[4:5, own] = cross_sum[2:3]
    out_ref[2:3, :] = first_ref[0:1]
    out_ref[5:7, :] = mid_ref[0:2]
    out_ref[7:9, :] = first_ref[1:3]
    out_ref[9:13, :] = mid_ref[2:6]
    out_ref[13:17, :] = ff_ref[0:4]
    if tiles_ref is not None:
        lots = tiles_ref.shape[0]
        lot, third = out_ref.shape[1] // lots, tiles_ref.shape[2] // 3
        tiles_ref[...] = jnp.zeros_like(tiles_ref)
        for d in range(lots):
            for n in range(3):
                piece = out_ref[8 * n : 8 * n + 8, d * lot : (d + 1) * lot]
                tiles_ref[d, :, n * third : n * third + lot] = piece.astype(BF)


def vec_rows(core, self_sums, cross_sums, first_sums, mid_sums, ff_sums, devices=None):
    operands = [self_sums, cross_sums, first_sums, mid_sums, ff_sums]
    dim = first_sums.shape[1]
    outs = [shape((24, dim), F32)]
    if devices is not None:
        outs.append(shape((devices, 8, dim // 2), BF))
    return call(
        "vec_rows",
        vec_rows_kernel,
        (1,),
        [whole(o) for o in operands],
        [whole(o) for o in outs],
        outs,
        [core] + operands,
        prefetch=1,
    )


def input_grad_kernel(count, has_start, *refs):
    start = refs[0] if has_start else None
    own, oth, mats_a, mats_b, out = refs[has_start:]
    total = start[...] if has_start else None
    for n in range(count):
        for grads, mats in ((own, mats_a), (oth, mats_b)):
            t = nt(grads[n], mats[n])
            total = t if total is None else total + t
    out[...] = total


def input_grad(own, other, mats_own, mats_other, start, tile):
    count, tokens, half = own.shape
    dim = mats_own.shape[1]
    grads = pl.BlockSpec((count, tile, half), lambda i: (0, i, 0))
    rows = pl.BlockSpec((tile, dim), lambda i: (i, 0))
    has_start = start is not None
    return call(
        "input_grad",
        functools.partial(input_grad_kernel, count, has_start),
        (tokens // tile,),
        ([rows] if has_start else []) + [grads, grads, whole(mats_own), whole(mats_other)],
        [rows],
        [shape((tokens, dim), F32)],
        ([start] if has_start else []) + [own, other, mats_own, mats_other],
        flops=4 * count * tokens * half * dim,
    )[0]


def adam_step(master, first_m, second_m, grad_sum, rate, decay):
    first_new = 0.5 * first_m + 0.5 * grad_sum
    second_new = 0.5 * second_m + 0.5 * grad_sum * grad_sum
    fix_term = 1.0 - 0.5**STEP
    update = first_new / fix_term / (jnp.sqrt(second_new / fix_term) + adam_eps)
    master_new = master - rate * (update + decay * master)
    return (master_new, first_new, second_new, master_new.astype(BF))


def on_device(
    target,
    memory,
    cotangent,
    seg_target,
    seg_memory,
    attn_master,
    attn_first,
    attn_second,
    in_master,
    in_first,
    in_second,
    out_master,
    out_first,
    out_second,
    vec_master,
    vec_first,
    vec_second,
):
    both = ("seq", "fsdp")
    devices = lax.axis_size("seq") * lax.axis_size("fsdp")
    core_at = lax.axis_index("seq") & 1
    core = core_at.astype(jnp.int32).reshape(1)
    is_low = core_at == 0
    place = lax.axis_index("seq") * lax.axis_size("fsdp") + lax.axis_index("fsdp")
    me = place.astype(jnp.int32).reshape(1)
    micro, _, rows, dim = target.shape
    half, hidden = dim // 2, in_master.shape[1]
    tokens = micro * rows
    shard = attn_master.shape[1]
    sets = bit_sets(devices)
    near = flips(sets[0])
    thin = sets[:1] + [[b] for bits in sets[1:] for b in bits]
    chip_bits = [b for bits in sets[::-1] for b in bits[::-1]]
    all_bits = sorted(chip_bits + [1], reverse=True)
    direct = devices == LOTS
    partner = lambda a: moved(a, CORE)

    x_own, m_own = target[:, 0], memory[:, 0]
    seg_own = jnp.concatenate([seg_target[:, 0], seg_memory[:, 0]], axis=0)
    attn_low = attn_master.astype(BF)
    in_low = in_master.astype(BF)
    out_low = out_master.astype(BF)
    vec_low = vec_master.astype(BF)

    def column_halves(mats):
        mine = jnp.where(is_low, mats[:, :, :half], mats[:, :, half:])
        other = partner(jnp.where(is_low, mats[:, :, half:], mats[:, :, :half]))
        return jnp.stack([jnp.where(is_low, mine, other), jnp.where(is_low, other, mine)])

    x_other, seg_other, m_other = partner(x_own), partner(seg_own), partner(m_own)
    if direct:
        halves = column_halves(attn_low[0:7]).reshape(2, 7 * shard, half)
        low_tile = as_tile(vec_low, half)
        far_tile = partner(low_tile)
        tiles = jnp.stack([jnp.where(is_low, low_tile, far_tile), jnp.where(is_low, far_tile, low_tile)])
        attn_far, rels = far_parts(jnp.concatenate([halves, tiles], axis=1), sets)
        feed_low = in_low.reshape(shard, 4, dim).transpose(1, 0, 2).reshape(4 * shard, dim)
        pack = jnp.concatenate([feed_low, out_low, attn_low[7]], axis=0)
        attn_far, x_own, m_own, x_other, m_other, seg_other, pack = lax.optimization_barrier(
            (attn_far, x_own, m_own, x_other, m_other, seg_other, pack)
        )
        pack = lax.all_gather(pack, both, axis=0, tiled=False)
        vec_parts = near_parts(attn_far[:, :, 7 * shard :], sets)
        self_parts = near_parts(attn_far[:, :, : 3 * shard], sets)
        self_mats = (self_parts, near, rels)
        vec_tiles = assemble(me, vec_parts, near, rels, 8)[0].reshape(devices, 8, half)
        vec_all = from_tile(vec_tiles, vec_low.shape[0], vec_low.shape[1])
        late_far = attn_far[:, :, 3 * shard : 7 * shard]
        self_parts[1:], late_far = lax.optimization_barrier((self_parts[1:], late_far))
        late_parts = near_parts(late_far, sets)
    else:

        def gather_half(mats):
            stacked = jnp.moveaxis(column_halves(mats), 0, 1)
            return gather_bits(stacked, chip_bits, [1]).reshape(mats.shape[0], dim, half)

        self_mats = gather_half(attn_low[0:3])
        late_mats = gather_half(attn_low[3:7])
        lots = lambda a: a.reshape(LOTS, -1, dim)
        win = lax.all_gather(in_low, both, axis=0, tiled=True)
        pack = jnp.concatenate(
            [lots(win[:, n * dim : (n + 1) * dim]) for n in range(4)]
            + [lots(lax.all_gather(out_low, both, axis=0, tiled=True))]
            + [lots(lax.all_gather(attn_low[7], both, axis=0, tiled=True))],
            axis=1,
        )
        vec_all = gather_bits(vec_low[None], [1] + chip_bits).reshape(devices, *vec_low.shape)
    vec = vec_all.transpose(1, 0, 2).reshape(vec_low.shape[0], dim).astype(F32)

    seg_t, seg_m = (jnp.concatenate([a, b], axis=1) for a, b in zip(
        (seg_own[:micro], seg_own[micro:]), (seg_other[:micro], seg_other[micro:])
    ))
    seg_t_ordered = jnp.where(is_low, seg_t, jnp.concatenate([seg_other[:micro], seg_own[:micro]], axis=1))
    row = lambda a: a[:, None, :]
    own_cols = lambda n: jnp.where(is_low, vec[n, :half], vec[n, half:])
    zeros = jnp.zeros((half,), F32)
    flat = lambda a: a.reshape(-1, a.shape[-1])
    flat3 = lambda a: a.reshape(a.shape[0], tokens, half)
    tall = lambda a: a.reshape(micro, rows, half)
    across = [flat(a).T for a in (x_own, x_other, m_own, m_other)]
    x_own, across = lax.optimization_barrier((x_own, across))

    qkv, self_mats = project(
        core, me, x_own, x_other, self_mats, jnp.stack([own_cols(0), zeros, own_cols(1)])[:, None], 0.125, True
    )
    self_own, self_send, self_exact, self_log = attention(
        True, core, None, (qkv, 1), row(seg_t_ordered), row(seg_t_ordered)
    )
    if direct:
        self_own, late_parts[0] = lax.optimization_barrier((self_own, late_parts[0]))
        late_mats = assemble(me, late_parts, near, rels, shard)
    late_other = partner(late_mats)
    mem_kv, _ = project(
        core, me, m_own, m_other, late_mats[2:4], jnp.stack([zeros, own_cols(4)])[:, None], 1.0, False
    )
    self_other_mats = partner(self_mats)
    mem_kv, late_other, self_other_mats = lax.optimization_barrier((mem_kv, late_other, self_other_mats))
    self_own, self_other = flat(self_own), flat(partner(self_send))
    xhat1, rstd1, first_low, cq_own, cq_send = after_self(
        core, self_own, self_other, flat(x_own), late_mats, late_other, vec, CHUNK
    )
    cq_own, cq_other = tall(cq_own), tall(partner(cq_send))
    cross_own, cross_send, cross_exact, cross_log = attention(
        False, core, (cq_own, cq_other), (mem_kv, 0), row(seg_t), row(seg_m)
    )
    cross_own, cross_other = flat(cross_own), flat(partner(cross_send))

    (block, act, d_pre, second_low, e3, d_r2, br2, dco_own, dco_send, mid_sums, ff_sums) = middle(
        core, cross_own, cross_other, xhat1, flat(cotangent[:, 0]), pack, vec, CHUNK
    )
    dco_own, dco_other = tall(dco_own), tall(partner(dco_send))
    feed = feed_grads(second_low, d_pre, act, e3)
    if direct:
        feed = lax.psum_scatter(feed, both, scatter_dimension=0, tiled=False)
        sum_in_mat = feed[: 4 * shard].reshape(4, shard, dim).transpose(1, 0, 2).reshape(shard, hidden)
        sum_out_mat = feed[4 * shard :]
    else:
        lot = dim // LOTS
        in_parts = [feed[:, n * lot : (n + 1) * lot].reshape(dim, dim) for n in range(4)]
        sum_in_mat = lax.psum_scatter(jnp.concatenate(in_parts, axis=1), both, scatter_dimension=0, tiled=True)
        sum_out_mat = lax.psum_scatter(
            feed[:, 4 * lot :].reshape(hidden, dim), both, scatter_dimension=0, tiled=True
        )
    dcq_own, dcq_send, d_mem_own, d_mem_other, cross_sums = attention(
        False,
        core,
        (cq_own, cq_other),
        (mem_kv, 0),
        row(seg_t),
        row(seg_m),
        (dco_own, dco_other, cross_exact, cross_log),
    )
    dcq_own, dcq_other = flat(dcq_own), flat(partner(dcq_send))
    d_r1, br1, dso_own, dso_send, first_sums = before_self(
        core, dcq_own, dcq_other, d_r2, xhat1, rstd1, late_mats, late_other, vec, CHUNK
    )
    dso_own, dso_other = tall(dso_own), tall(partner(dso_send))

    def reduce_whole(mats):
        spread = mats.reshape([mats.shape[0]] + [2] * len(all_bits) + [shard, half])
        summed = scatter_bits(spread, chip_bits[::-1], all_bits)
        mine = jnp.where(is_low, summed[:, 0], summed[:, 1])
        other = partner(jnp.where(is_low, summed[:, 1], summed[:, 0]))
        return both_halves(is_low, mine, other)

    d_mem_own, d_mem_other = flat3(d_mem_own), flat3(d_mem_other)
    grads_mine, grads_away = token_grads(
        core, self_own, self_other, br1, first_low, dcq_own, dcq_other, cross_own, cross_other, br2
    )
    grads_mem = pair_grads(me, across[2], across[3], d_mem_own, d_mem_other)[0]
    grads_got = partner(grads_away)
    d_mem_in = partner(d_mem_other)
    if direct:
        routed = list(route_sums(me, grads_mine, grads_got, grads_mem, sets[0], devices))
        dso_own, routed[0], d_mem_in = lax.optimization_barrier((dso_own, routed[0], d_mem_in))
        cross_near, _ = reduce_near(me, routed, thin, devices)
    else:
        summed = (grads_mine.astype(F32) + grads_got.astype(F32)).astype(BF)
        sum_cross = reduce_whole(jnp.concatenate([summed, grads_mem]))

    d_self_own, d_self_away, self_sums = attention(
        True,
        core,
        None,
        (qkv, 1),
        row(seg_t_ordered),
        row(seg_t_ordered),
        (dso_own, dso_other, self_exact, self_log),
    )
    d_self_own, d_self_away = flat3(d_self_own), flat3(d_self_away)
    grad_m = input_grad(d_mem_own, d_mem_in, late_mats[2:4], late_other[2:4], None, CHUNK)
    vec_grad = vec_rows(core, self_sums, cross_sums, first_sums, mid_sums, ff_sums, devices if direct else None)
    if direct:
        routed = list(
            pair_grads(me, across[0], across[1], d_self_own, d_self_away, (sets[0], vec_grad[1]))
        )
        d_self_away, routed, cross_near = lax.optimization_barrier((d_self_away, routed, cross_near))

    d_self_other = partner(d_self_away)
    grad_x = input_grad(d_self_own, d_self_other, self_mats, self_other_mats, d_r1, CHUNK)
    if direct:
        mine, other, (grad_m, grad_x) = reduce_far(me, cross_near, thin, devices, [grad_m, grad_x])
        self_near, (mine, grad_m, grad_x) = reduce_near(me, routed, sets, devices, (mine, grad_m, grad_x))
        sum_cross = both_halves(is_low, mine, other)
        mine, other, _ = reduce_far(me, self_near, sets, devices)
        last = 3 * shard
        sum_self = both_halves(is_low, mine[:last], other[:last]).reshape(3, shard, dim)
        tile = mine[last:].astype(F32) + other[last:].astype(F32)
        sum_vec = from_tile(tile, *vec_master.shape)
    else:
        sum_self = reduce_whole(pair_grads(me, across[0], across[1], d_self_own, d_self_away)[0])
        all_rows = vec_grad[0]
        for bit in [1] + chip_bits[::-1]:
            all_rows = all_rows + moved(all_rows, 1 << bit)
        width = vec_master.shape[1]
        sum_vec = lax.dynamic_slice_in_dim(all_rows[: vec_master.shape[0]], place * width, width, axis=1)

    sum_attn = jnp.concatenate(
        [sum_self, sum_cross[0:2], sum_cross[3:5], sum_cross[2:3]], axis=0
    ).astype(F32)
    attn_new, attn_m, attn_s, attn_w = adam_step(attn_master, attn_first, attn_second, sum_attn, 0.1, 0.01)
    in_new, in_m, in_s, in_w = adam_step(in_master, in_first, in_second, sum_in_mat.astype(F32), 0.05, 0.01)
    out_new, out_m, out_s, out_w = adam_step(out_master, out_first, out_second, sum_out_mat.astype(F32), 0.03, 0.01)
    vec_new, vec_m, vec_s, vec_w = adam_step(vec_master, vec_first, vec_second, sum_vec, 0.3, 0.0)
    return (
        block.reshape(micro, 1, rows, dim),
        grad_x.reshape(micro, 1, rows, dim),
        grad_m.reshape(micro, 1, rows, dim),
        attn_new,
        attn_m,
        attn_s,
        attn_w,
        in_new,
        in_m,
        in_s,
        in_w,
        out_new,
        out_m,
        out_s,
        out_w,
        vec_new,
        vec_m,
        vec_s,
        vec_w,
    )


def solution(mesh):
    tokens = P(None, "fsdp", "seq", None)
    marks = P(None, "fsdp", "seq")
    attn = P(None, ("seq", "fsdp"), None)
    feed = P(("seq", "fsdp"), None)
    rows = P(None, ("seq", "fsdp"))
    return jax.shard_map(
        on_device,
        mesh=mesh,
        in_specs=(tokens,) * 3 + (marks,) * 2 + (attn,) * 3 + (feed,) * 6 + (rows,) * 3,
        out_specs=(tokens,) * 3 + (attn,) * 4 + (feed,) * 8 + (rows,) * 4,
        check_vma=False,
    )
```

```python
import functools

import jax
import jax.numpy as jnp
from jax import lax
from jax.experimental import pallas as pl
from jax.experimental.pallas import tpu as pltpu
from jax.sharding import PartitionSpec as P

HDIM = 64
STEP = 10
PAIR = 2 * HDIM
CHUNK = 256
DOCS = 5
MASKED = -1e30
BOUND = 3000.0

BF = jnp.bfloat16
F32 = jnp.float32

norm_eps = 1e-05
adam_eps = 1e-08
MIB = 2**20
COST = 0.1


def nn(a, b):
    return lax.dot_general(a, b, (((1,), (0,)), ((), ())), preferred_element_type=F32)


def nt(a, b):
    return lax.dot_general(a, b, (((1,), (1,)), ((), ())), preferred_element_type=F32)


def tn(a, b):
    return lax.dot_general(a, b, (((0,), (0,)), ((), ())), preferred_element_type=F32)


def call(name, kernel, grid, in_specs, out_specs, out_shape, operands, scratch=(), flops=0, prefetch=0, room=28):
    size = COST * sum(leaf.size * leaf.dtype.itemsize for leaf in list(operands) + list(out_shape))
    return pl.pallas_call(
        kernel,
        name=name,
        grid_spec=pltpu.PrefetchScalarGridSpec(
            num_scalar_prefetch=prefetch,
            grid=grid,
            in_specs=in_specs,
            out_specs=out_specs,
            scratch_shapes=scratch,
        ),
        out_shape=out_shape,
        compiler_params=pltpu.CompilerParams(vmem_limit_bytes=room * MIB),
        cost_estimate=pl.CostEstimate(flops=int(COST * flops), bytes_accessed=int(size), transcendentals=0),
    )(*operands)


def shape(dims, dtype):
    return jax.ShapeDtypeStruct(tuple(dims), dtype)


def whole(array):
    zeros = (0,) * array.ndim
    return pl.BlockSpec(array.shape, lambda *_: zeros)


CORE = 2


def moved(array, flip):
    count = lax.axis_size("seq") * lax.axis_size("fsdp")
    return lax.ppermute(array, ("seq", "fsdp"), [(i, i ^ flip) for i in range(count)])


def own_bit(bit):
    if bit == 0:
        return lax.axis_index("fsdp")
    return (lax.axis_index("seq") >> (bit - 1)) & 1


def bit_sets(count):
    bits = [0] + list(range(2, count.bit_length() - 1))
    return [bits[i : i + 2] for i in range(0, len(bits), 2)]


def flips(bits):
    out = [0]
    for bit in bits:
        out = out + [f | 1 << bit for f in out]
    return out


def gather_bits(array, order, present=()):
    present = sorted(present, reverse=True)
    for bit in order:
        other = moved(array, 1 << bit)
        place = 1 + sum(b > bit for b in present)
        low = own_bit(bit) == 0
        array = jnp.stack([jnp.where(low, array, other), jnp.where(low, other, array)], axis=place)
        present = sorted(present + [bit], reverse=True)
    return array


def scatter_bits(array, order, present):
    present = sorted(present, reverse=True)
    for bit in order:
        place = 1 + present.index(bit)
        mine = own_bit(bit)
        send = lax.dynamic_index_in_dim(array, 1 - mine, place, keepdims=False)
        keep = lax.dynamic_index_in_dim(array, mine, place, keepdims=False)
        array = (keep.astype(F32) + moved(send, 1 << bit).astype(F32)).astype(BF)
        present.remove(bit)
    return array


def as_tile(rows, width):
    third = width // 3
    full = jnp.pad(rows, ((0, 24 - rows.shape[0]), (0, third - rows.shape[1])))
    return jnp.concatenate([full[0:8], full[8:16], full[16:24]], axis=1)


def from_tile(tile, count, columns):
    third = tile.shape[-1] // 3
    groups = [tile[..., n * third : n * third + columns] for n in range(3)]
    return jnp.concatenate(groups, axis=-2)[..., :count, :]


def far_parts(stacked, sets, cuts):
    rels, array = [0], stacked[None]
    for bits in sets[:1:-1]:
        rels = [f ^ r for f in flips(bits) for r in rels]
        array = jnp.concatenate([array] + [moved(array, f) for f in flips(bits)[1:]], axis=0)
    got = [array] + [moved(array, f) for f in flips(sets[1])[1:]]
    rels = [f ^ r for f in flips(sets[1]) for r in rels]
    many = array.shape[0]

    def join_kernel(*refs):
        ins, outs = refs[: len(got)], refs[len(got) :]
        for out, (a, b) in zip(outs, cuts):
            for n, one in enumerate(ins):
                out[n * many : (n + 1) * many] = one[:, :, a:b]

    outs = [shape((many * len(got), 2, b - a, array.shape[3]), BF) for a, b in cuts]
    joined = call("join", join_kernel, (1,), [whole(one) for one in got], [whole(out) for out in outs], outs, got)
    return joined, rels


def near_parts(array, sets):
    return [array] + [moved(array, f) for f in flips(sets[0])[1:]]


def assemble_kernel(near, rels, me_ref, *refs):
    parts, out = refs[: len(near)], refs[-1]
    for part, f in zip(parts, near):
        for i, r in enumerate(rels):
            for c in range(2):
                out[0, ((me_ref[0] & ~CORE) ^ (f ^ r)) + CORE * c] = part[i, c]


def part_specs(parts, rows):
    return [pl.BlockSpec((p.shape[0], 2, rows, p.shape[3]), lambda i, *_: (0, 0, i, 0)) for p in parts]


def assemble(me, parts, near, rels, rows):
    _, _, total, cols = parts[0].shape
    count = total // rows
    lots = 2 * len(near) * len(rels)
    out = call(
        "assemble",
        functools.partial(assemble_kernel, near, rels),
        (count,),
        part_specs(parts, rows),
        [pl.BlockSpec((1, lots, rows, cols), lambda i, *_: (i, 0, 0, 0))],
        [shape((count, lots, rows, cols), BF)],
        [me] + parts,
        prefetch=1,
    )[0]
    return out.reshape(count, lots * rows, cols)


def compact(number, removed):
    out, place = 0, 0
    for bit in range(number.bit_length()):
        if bit not in removed:
            out |= (number >> bit & 1) << place
            place += 1
    return out


def send_blocks(bits, gone, count, me, load, outs):
    kept = [b for b in range(count.bit_length() - 1) if b not in gone]
    mask = sum(1 << kept.index(b) for b in bits)
    here = 0
    for b in bits:
        here = here + (((me >> b) & 1) << kept.index(b))
    total = 1 << len(kept)
    for f, out in zip(flips(bits), outs):
        small = sum(((f >> b) & 1) << kept.index(b) for b in bits)
        j = 0
        for k in range(total):
            if k & mask == 0:
                out(j, load((here ^ small) + k))
                j += 1


def combine_kernel(bits, gone, count, me_ref, *refs):
    outs = refs[-(1 << len(bits)) :]
    ins = refs[: len(refs) - len(outs)]

    def load(k):
        total = ins[0][k].astype(F32)
        for ref in ins[1:]:
            total = total + ref[k].astype(F32)
        return total.astype(BF)

    def store(out):
        def put(j, value):
            out[j] = value

        return put

    send_blocks(bits, gone, count, me_ref[0], load, [store(out) for out in outs])


def combine(me, arrays, bits, gone, count):
    blocks = arrays[0].shape[0] >> len(bits)
    out = shape((blocks,) + arrays[0].shape[1:], BF)
    return call(
        "combine",
        functools.partial(combine_kernel, bits, gone, count),
        (1,),
        [whole(a) for a in arrays],
        [whole(out)] * (1 << len(bits)),
        [out] * (1 << len(bits)),
        [me] + arrays,
        prefetch=1,
    )


def reduce_near(me, outs, sets, count, beside=None):
    got = [outs[0]] + [moved(out, f) for out, f in zip(outs[1:], flips(sets[0])[1:])]
    if beside is not None:
        got[0], beside = lax.optimization_barrier((got[0], beside))
    return combine(me, got, (sets[1:] + [[1]])[0], sets[0], count), beside


def reduce_far(me, outs, sets, count, beside=()):
    gone, beside = sets[0], list(beside)
    for n, (here, after) in enumerate(zip(sets[1:], sets[2:] + [[1]])):
        gone = gone + here
        got = [outs[0]] + [moved(out, f) for out, f in zip(outs[1:], flips(here)[1:])]
        if n < len(beside):
            got[0], beside[n] = lax.optimization_barrier((got[0], beside[n]))
        outs = combine(me, got, after, gone, count)
    return outs[0][0], moved(outs[1], CORE)[0], beside


def both_halves(is_low, mine, other):
    return jnp.concatenate([jnp.where(is_low, mine, other), jnp.where(is_low, other, mine)], axis=-1)


def with_marks(pair, seg, half, lanes, is_key):
    mark = lanes - (HDIM if half == 0 else 0)
    mine = (lanes < HDIM) if half == 0 else (lanes >= HDIM)
    hit = seg == mark
    if is_key:
        extra = jnp.where(hit, 1.0, 0.0)
    else:
        extra = jnp.where(hit | (mark < 0) | (mark >= DOCS), 0.0, MASKED)
    return jnp.where(mine, pair.astype(F32), extra).astype(BF)


def down(row):
    return jnp.broadcast_to(row, (PAIR, row.shape[1])).T


def causal_tile():
    keys = lax.broadcasted_iota(jnp.int32, (CHUNK, CHUNK), 0)
    places = lax.broadcasted_iota(jnp.int32, (CHUNK, CHUNK), 1)
    return jnp.where(places >= keys, 0.0, MASKED)


def masked_scores(keys, queries, c, causal, tile):
    length = keys.shape[0]
    end = (c + 1) * CHUNK if causal else length
    s = nt(keys[:end], queries[c * CHUNK : (c + 1) * CHUNK])
    if causal:
        last = s[c * CHUNK :] + tile
        s = jnp.concatenate([s[: c * CHUNK], last], axis=0) if c else last
    return s


def halves_in(ref_a, ref_b, core, scratch):
    rows = ref_a.shape[-2]
    if core is None:
        scratch[0:rows, :] = ref_a[...].reshape(rows, PAIR)
        scratch[rows:, :] = ref_b[...].reshape(rows, PAIR)
    else:
        scratch[pl.ds(pl.multiple_of(core * rows, rows), rows), :] = ref_a[...].reshape(rows, PAIR)
        scratch[pl.ds(pl.multiple_of((1 - core) * rows, rows), rows), :] = ref_b[...].reshape(rows, PAIR)


def halves_out(scratch, core, ref_a, ref_b):
    rows = scratch.shape[0] // 2
    if core is None:
        a, b = scratch[0:rows, :], scratch[rows:, :]
    else:
        a = scratch[pl.ds(pl.multiple_of(core * rows, rows), rows), :]
        b = scratch[pl.ds(pl.multiple_of((1 - core) * rows, rows), rows), :]
    ref_a[...] = a.reshape(ref_a.shape)
    ref_b[...] = b.reshape(ref_b.shape)


def head_lanes():
    pick = lax.broadcasted_iota(jnp.int32, (8, PAIR), 1) // HDIM == lax.broadcasted_iota(jnp.int32, (8, PAIR), 0)
    return jnp.where(pick, 1.0, 0.0)


def forward_kernel(causal, core_ref, *refs):
    if causal:
        q_ref, k_ref, v_ref, sq_ref, sk_ref, own_ref, send_ref, exact_ref, log_ref, out_s = refs
        core = core_ref[0]
        q = q_ref[0, 0]
    else:
        qa_ref, qb_ref, k_ref, v_ref, sq_ref, sk_ref, own_ref, send_ref, exact_ref, log_ref, out_s = refs
        core = None
        q = jnp.concatenate([qa_ref[0], qb_ref[0]], axis=0)
    k, v = k_ref[0, 0], v_ref[0, 0]
    sq, sk = down(sq_ref[0]), down(sk_ref[0])
    length = k.shape[0]
    lanes = lax.broadcasted_iota(jnp.int32, (length, PAIR), 1)
    tile = causal_tile() if causal else None
    across = v.astype(F32).T.astype(BF)
    ones = jnp.ones((16, length), BF)
    heads = [
        (
            with_marks(q, sq, half, lanes, False),
            with_marks(k, sk, half, lanes, True),
            jnp.concatenate([across[half * HDIM : (half + 1) * HDIM], ones], axis=0),
        )
        for half in range(2)
    ]
    square = lambda a: jnp.max(nt(head_lanes().astype(BF), (a.astype(F32) * a.astype(F32)).astype(BF)))
    bounded = square(q) * square(k) < BOUND

    def every_chunk(with_top):
        done = {}

        def finish(c, half, s):
            if with_top:
                top = jnp.max(s, axis=0, keepdims=True)
                s = s - top
            p = jnp.exp(s).astype(BF)
            mixed = nn(heads[half][2][:, : s.shape[0]], p)
            total = mixed[HDIM : HDIM + 1]
            log = jnp.log(total)
            done[half] = (mixed[:HDIM] * (1.0 / total), log + top if with_top else log)
            if half == 1:
                cs = slice(c * CHUNK, (c + 1) * CHUNK)
                both = jnp.concatenate([done[0][0], done[1][0]], axis=0).T
                exact_ref[0, cs, :] = both
                out_s[cs, :] = both.astype(BF)
                log_ref[0, 0, 0:1, cs] = done[0][1]
                log_ref[0, 0, 1:2, cs] = done[1][1]

        waiting = None
        for c in reversed(range(length // CHUNK)):
            for half in range(2):
                s = masked_scores(heads[half][1], heads[half][0], c, causal, tile)
                if waiting is not None:
                    finish(*waiting)
                waiting = (c, half, s)
        finish(*waiting)

    @pl.when(bounded)
    def _():
        every_chunk(False)

    @pl.when(jnp.logical_not(bounded))
    def _():
        every_chunk(True)

    halves_out(out_s, core, own_ref, send_ref)


def backward_kernel(causal, core_ref, *refs):
    if causal:
        q_ref, k_ref, v_ref, sq_ref, sk_ref, ga_ref, gb_ref, exact_ref, log_ref = refs[:9]
        own_ref, send_ref, sum_ref, p_s, ds_s, g_s, out_s = refs[9:]
        core = core_ref[0]
        q = q_ref[0, 0]
    else:
        qa_ref, qb_ref, k_ref, v_ref, sq_ref, sk_ref, ga_ref, gb_ref, exact_ref, log_ref = refs[:10]
        own_ref, send_ref, kv_own_ref, kv_oth_ref, sum_ref, p_s, ds_s, g_s, out_s = refs[10:]
        core = None
        q = jnp.concatenate([qa_ref[0], qb_ref[0]], axis=0)
    k, v = k_ref[0, 0], v_ref[0, 0]
    sq, sk = down(sq_ref[0]), down(sk_ref[0])
    length = k.shape[0]
    chunks = length // CHUNK
    halves_in(ga_ref, gb_ref, core, g_s)
    grad = g_s[...]
    lanes = lax.broadcasted_iota(jnp.int32, (length, PAIR), 1)
    tile = causal_tile() if causal else None
    pick = lax.broadcasted_iota(jnp.int32, (8, PAIR), 1) // HDIM == lax.broadcasted_iota(jnp.int32, (8, PAIR), 0)
    delta = lax.dot_general(
        jnp.where(pick, 1.0, 0.0),
        grad.astype(F32) * exact_ref[0],
        (((1,), (1,)), ((), ())),
        precision=lax.Precision.HIGHEST,
        preferred_element_type=F32,
    )
    heads = []
    for half in range(2):
        mine = (lanes < HDIM) if half == 0 else (lanes >= HDIM)
        only = lambda a: jnp.where(mine, a.astype(F32), 0.0)
        heads.append(
            dict(
                q=with_marks(q, sq, half, lanes, False),
                k=with_marks(k, sk, half, lanes, True),
                qm=only(q).astype(BF),
                kt=only(k).T.astype(BF),
                gm=only(grad).astype(BF),
                log=log_ref[0, 0, half : half + 1, :],
                delta=delta[half : half + 1, :],
            )
        )
    dq, dk, dv = {}, {}, {}

    def products(c, half):
        h = heads[half]
        cs = slice(c * CHUNK, (c + 1) * CHUNK)
        s = masked_scores(h["k"], h["q"], c, causal, tile)
        return s, nt(v[: s.shape[0]], h["gm"][cs])

    def finish(c, half, s, dp):
        h = heads[half]
        cs = slice(c * CHUNK, (c + 1) * CHUNK)
        end = s.shape[0]
        p = jnp.exp(s - h["log"][:, cs])
        ds = (p * (dp - h["delta"][:, cs])).astype(BF)
        p_s[half, :end, cs] = p.astype(BF)
        ds_s[half, :end, cs] = ds
        t = nn(h["kt"][:, :end], ds)
        dq[c] = t if half == 0 else dq[c] + t

    def keys_side(kb, half):
        h = heads[half]
        q0 = kb * CHUNK if causal else 0
        ks = slice(kb * CHUNK, (kb + 1) * CHUNK)
        a = nn(p_s[half, ks, q0:], h["gm"][q0:])
        b = nn(ds_s[half, ks, q0:], h["qm"][q0:])
        dv[kb] = a if half == 0 else dv[kb] + a
        dk[kb] = b if half == 0 else dk[kb] + b

    waiting = None
    for half in range(2):
        for c in range(chunks):
            pair = products(c, half)
            if waiting is not None:
                finish(*waiting)
            waiting = (c, half, *pair)
            if half == 1 and c > 0:
                keys_side(c - 1, 0)
    finish(*waiting)
    keys_side(chunks - 1, 0)
    for kb in range(chunks):
        keys_side(kb, 1)

    def put(n, parts):
        low = [part.astype(BF) for part in parts]
        for c in range(chunks):
            out_s[n, c * CHUNK : (c + 1) * CHUNK, :] = low[c]
        return sum(jnp.sum(one.astype(F32), axis=0, keepdims=True) for one in low)

    sum_q = put(0, [dq[c].T.astype(BF).astype(F32) * 0.125 for c in range(chunks)])
    sum_k = put(1, [dk[c] for c in range(chunks)])
    sum_v = put(2, [dv[c] for c in range(chunks)])
    pad = jnp.zeros((5, PAIR), F32)
    sum_ref[0] = jnp.concatenate([sum_q, sum_k, sum_v, pad], axis=0)
    if causal:
        for n in range(3):
            halves_out(out_s.at[n], core, own_ref.at[n], send_ref.at[n])
    else:
        halves_out(out_s.at[0], core, own_ref, send_ref)
        for n in range(2):
            halves_out(out_s.at[1 + n], None, kv_own_ref.at[n], kv_oth_ref.at[n])


def attention(causal, core, queries, keys, seg_q, seg_k, backward=None):
    source, k_at = keys
    _, micro, length, width = source.shape
    pairs = width // PAIR
    part = pl.BlockSpec((1, length // 2, PAIR), lambda i, j, s: (i, 0, j))
    full = pl.BlockSpec((1, length, PAIR), lambda i, j, s: (i, 0, j))
    at = lambda n: pl.BlockSpec((1, 1, length, PAIR), lambda i, j, s: (n, i, 0, j))
    seg = pl.BlockSpec((1, 1, length), lambda i, j, s: (i, 0, 0))
    stat = pl.BlockSpec((1, 1, 8, length), lambda i, j, s: (i, j, 0, 0))
    if causal:
        operands, specs = [source], [at(0)]
    else:
        operands, specs = list(queries), [part, part]
    operands += [source, source, seg_q, seg_k]
    specs += [at(k_at), at(k_at + 1), seg, seg]
    share = 0.625 if causal else 1.0
    unit = 2 * micro * pairs * 2 * length * length * PAIR * share
    half_out = shape((micro, length // 2, width), BF)
    if backward is None:
        return call(
            "attend",
            functools.partial(forward_kernel, causal),
            (micro, pairs),
            specs,
            [part, part, full, stat],
            [half_out, half_out, shape((micro, length, width), F32), shape((micro, pairs, 8, length), F32)],
            [core] + operands,
            scratch=[pltpu.VMEM((length, PAIR), BF)],
            flops=unit * 2,
            prefetch=1,
        )
    operands += list(backward)
    specs += [part, part, full, stat]
    sums = pl.BlockSpec((1, 8, PAIR), lambda i, j, s: (i, 0, j))
    scratch = [
        pltpu.VMEM((2, length, length), BF),
        pltpu.VMEM((2, length, length), BF),
        pltpu.VMEM((length, PAIR), BF),
        pltpu.VMEM((3, length, PAIR), BF),
    ]
    if causal:
        part3 = pl.BlockSpec((3, 1, length // 2, PAIR), lambda i, j, s: (0, i, 0, j))
        outs = [part3, part3, sums]
        shapes = [shape((3, micro, length // 2, width), BF)] * 2
    else:
        part2 = pl.BlockSpec((2, 1, length // 2, PAIR), lambda i, j, s: (0, i, 0, j))
        outs = [part, part, part2, part2, sums]
        shapes = [half_out, half_out] + [shape((2, micro, length // 2, width), BF)] * 2
    return call(
        "attend_back",
        functools.partial(backward_kernel, causal),
        (micro, pairs),
        specs,
        outs,
        shapes + [shape((micro, 8, width), F32)],
        [core] + operands,
        scratch=scratch,
        room=36,
        flops=unit * 5,
        prefetch=1,
    )


def project_kernel(first_scale, ordered, gather, *refs):
    core_ref, refs = refs[0], refs[1:]
    if gather is None:
        a_ref, b_ref, w_ref, bias_ref, out_ref = refs
        mat = w_ref[0]
    else:
        near, rels = gather
        me_ref, a_ref, b_ref = refs[:3]
        parts = refs[3 : 3 + len(near)]
        bias_ref, out_ref, mat_ref = refs[3 + len(near) :]
        assemble_kernel(near, rels, me_ref, *parts, mat_ref)
        mat = mat_ref[0].reshape(a_ref.shape[-1], mat_ref.shape[-1])
    rows = a_ref.shape[1]
    scale = jnp.where(pl.program_id(0) == 0, first_scale, 1.0).astype(F32)
    for m in range(a_ref.shape[0]):
        for slot, ref in enumerate((a_ref, b_ref)):
            low = ((nn(ref[m], mat) + bias_ref[0]) * scale).astype(BF)
            place = (core_ref[0] ^ slot) * rows if ordered else slot * rows
            out_ref[0, m, pl.ds(pl.multiple_of(place, rows), rows), :] = low


def project(core, me, own, other, mats, biases, scale, ordered):
    micro, rows, depth = own.shape
    count, _, width = biases.shape
    tokens = pl.BlockSpec(own.shape, lambda i, *_: (0, 0, 0))
    mat_spec = pl.BlockSpec((1, depth, width), lambda i, *_: (i, 0, 0))
    bias_spec = pl.BlockSpec((1, 1, width), lambda i, *_: (i, 0, 0))
    out_specs = [pl.BlockSpec((1, micro, 2 * rows, width), lambda i, *_: (i, 0, 0, 0))]
    out_shape = [shape((count, micro, 2 * rows, width), BF)]
    flops = 2 * count * micro * 2 * rows * depth * width
    if not isinstance(mats, tuple):
        out = call(
            "project",
            functools.partial(project_kernel, scale, ordered, None),
            (count,),
            [tokens, tokens, mat_spec, bias_spec],
            out_specs,
            out_shape,
            [core, own, other, mats, biases],
            flops=flops,
            prefetch=1,
        )[0]
        return out, mats
    parts, near, rels = mats
    lot = depth // (2 * len(near) * len(rels))
    out, full = call(
        "project",
        functools.partial(project_kernel, scale, ordered, (near, rels)),
        (count,),
        [tokens, tokens] + part_specs(parts, lot) + [bias_spec],
        out_specs + [pl.BlockSpec((1, depth // lot, lot, width), lambda i, *_: (i, 0, 0, 0))],
        out_shape + [shape((count, depth // lot, lot, width), BF)],
        [core, me, own, other] + parts + [biases],
        flops=flops,
        prefetch=2,
    )
    return out, full.reshape(count, depth, width)


def normalise(r):
    mean = jnp.mean(r, axis=-1, keepdims=True)
    centred = r - mean
    rstd = lax.rsqrt(jnp.mean(centred * centred, axis=-1, keepdims=True) + norm_eps)
    return centred * rstd, rstd


def norm_back(dz, xhat, rstd, gain):
    dxhat = dz * gain
    a = jnp.mean(dxhat, axis=-1, keepdims=True)
    b = jnp.mean(dxhat * xhat, axis=-1, keepdims=True)
    return (dxhat - a - xhat * b) * rstd


def col_sum(a):
    return jnp.sum(a.astype(F32), axis=0, keepdims=True)


def own_part(core, swap, width):
    return pl.ds(pl.multiple_of((core ^ swap) * width, width), width)


def join_columns(core, own_ref, oth_ref, scratch):
    width = own_ref.shape[-1]
    scratch[:, own_part(core, 0, width)] = own_ref[...]
    scratch[:, own_part(core, 1, width)] = oth_ref[...]


def after_self_kernel(
    core_ref, own_ref, oth_ref, x_ref, mat_ref, moth_ref, vec_ref, xhat_ref, rstd_ref, low_ref, qa_ref, qb_ref, out_s
):
    core = core_ref[0]
    width = own_ref.shape[1]

    @pl.when(pl.program_id(0) == 0)
    def _():
        join_columns(core, mat_ref.at[0], moth_ref.at[0], out_s)

    parts = [slice(i, i + CHUNK) for i in range(0, own_ref.shape[0], CHUNK)]
    mixed = [
        nn(own_ref[r, :], out_s[own_part(core, 0, width), :]) + nn(oth_ref[r, :], out_s[own_part(core, 1, width), :])
        for r in parts
    ]
    for r, one in zip(parts, mixed):
        xhat, rstd = normalise(x_ref[r, :].astype(F32) + one + vec_ref[2:3])
        xhat_ref[r, :] = xhat
        rstd_ref[r, :] = rstd
        low = (xhat * vec_ref[7:8] + vec_ref[8:9]).astype(BF)
        low_ref[r, :] = low
        qa_ref[r, :] = ((nn(low, mat_ref[1]) + vec_ref[3:4, own_part(core, 0, width)]) * 0.125).astype(BF)
        qb_ref[r, :] = ((nn(low, moth_ref[1]) + vec_ref[3:4, own_part(core, 1, width)]) * 0.125).astype(BF)


def first_two(mats):
    return pl.BlockSpec((2,) + mats.shape[1:], lambda *_: (0, 0, 0))


def after_self(core, own, other, x, mats, mats_other, vec, tile):
    tokens, dim = x.shape
    rows = lambda w: pl.BlockSpec((tile, w), lambda i, s: (i, 0))
    half = dim // 2
    return call(
        "after_self",
        after_self_kernel,
        (tokens // tile,),
        [rows(half), rows(half), rows(dim), first_two(mats), first_two(mats), whole(vec)],
        [rows(dim), rows(1), rows(dim), rows(half), rows(half)],
        [
            shape((tokens, dim), F32),
            shape((tokens, 1), F32),
            shape((tokens, dim), BF),
            shape((tokens, half), BF),
            shape((tokens, half), BF),
        ],
        [core, own, other, x, mats, mats_other, vec],
        scratch=[pltpu.VMEM((dim, dim), BF)],
        flops=4 * tokens * dim * dim,
        prefetch=1,
    )


LOTS = 32


def packed_in(pack_ref, n):
    lots, dim = pack_ref.shape[0], pack_ref.shape[2]
    lot = dim // lots
    return pack_ref[:, n * lot : (n + 1) * lot, :].reshape(dim, dim)


def packed_out(pack_ref, n):
    lots, dim = pack_ref.shape[0], pack_ref.shape[2]
    lot, some = dim // lots, lots // 4
    return pack_ref[n * some : (n + 1) * some, 4 * lot : 8 * lot, :].reshape(dim, dim)


def packed_cross(pack_ref, core, swap):
    lots, dim = pack_ref.shape[0], pack_ref.shape[2]
    lot, some = dim // lots, lots // 2
    return pack_ref[own_part(core, swap, some), 8 * lot : 9 * lot, :].reshape(dim // 2, dim)


def middle_kernel(
    core_ref,
    own_ref,
    oth_ref,
    xhat1_ref,
    cot_ref,
    pack_ref,
    vec_ref,
    block_ref,
    act_ref,
    dpre_ref,
    low2_ref,
    e3_ref,
    dr2_ref,
    br2_ref,
    ga_ref,
    gb_ref,
    vsum_ref,
    fsum_ref,
    slope_s,
):
    core = core_ref[0]
    rows, dim = xhat1_ref.shape
    hidden = act_ref.shape[1]
    parts = [slice(i, i + CHUNK) for i in range(0, rows, CHUNK)]
    jobs = [(i, n) for n in range(hidden // dim) for i in range(len(parts))]
    state = [{} for _ in parts]

    def in_turn(make, use):
        waiting = None
        for job in jobs:
            made = make(*job)
            if waiting is not None:
                use(*waiting)
            waiting = (*job, made)
        use(*waiting)

    for at, r in zip(state, parts):
        first = xhat1_ref[r, :] * vec_ref[7:8] + vec_ref[8:9]
        mixed = nn(own_ref[r, :], packed_cross(pack_ref, core, 0)) + nn(oth_ref[r, :], packed_cross(pack_ref, core, 1))
        at["r2"] = first + mixed + vec_ref[5:6]
    for at, r in zip(state, parts):
        at["xhat2"], at["rstd2"] = normalise(at["r2"])
        second = at["xhat2"] * vec_ref[9:10] + vec_ref[10:11]
        at["low2"] = second.astype(BF)
        low2_ref[r, :] = at["low2"]
        at["r3"] = second + vec_ref[6:7]

    def before_gelu(i, n):
        return nn(state[i]["low2"], packed_in(pack_ref, n)) + vec_ref[13 + n : 14 + n]

    def gelu(i, n, pre):
        r, cs = parts[i], slice(n * dim, (n + 1) * dim)
        phi = 0.5 * (1.0 + lax.erf(pre * 0.7071067811865476))
        act = (pre * phi).astype(BF)
        act_ref[r, cs] = act
        slope_s[r, cs] = phi + pre * (jnp.exp(-0.5 * pre * pre) * 0.3989422804014327)
        state[i]["r3"] = state[i]["r3"] + nn(act, packed_out(pack_ref, n))

    in_turn(before_gelu, gelu)
    for at, r in zip(state, parts):
        xhat3, rstd3 = normalise(at["r3"])
        block_ref[r, :] = xhat3 * vec_ref[11:12] + vec_ref[12:13]
        dz = cot_ref[r, :].astype(F32)
        dr3 = norm_back(dz, xhat3, rstd3, vec_ref[11:12])
        at["e3"] = dr3.astype(BF)
        e3_ref[r, :] = at["e3"]
        at["back"] = dr3
        at["sums"] = [col_sum(at["e3"]), col_sum(dz * xhat3), col_sum(dz)]
        at["ff"] = []

    def act_grad(i, n):
        return nt(state[i]["e3"], packed_out(pack_ref, n))

    def gelu_back(i, n, grad):
        r, cs = parts[i], slice(n * dim, (n + 1) * dim)
        low = (grad * slope_s[r, cs]).astype(BF)
        dpre_ref[r, cs] = low
        state[i]["ff"].append(col_sum(low))
        state[i]["back"] = state[i]["back"] + nt(low, packed_in(pack_ref, n))

    in_turn(act_grad, gelu_back)
    first_step = pl.program_id(0) == 0
    total = jnp.where(first_step, 0.0, vsum_ref[...])
    ff_total = jnp.where(first_step, 0.0, fsum_ref[...])
    for at, r in zip(state, parts):
        back = at["back"]
        dr2 = norm_back(back, at["xhat2"], at["rstd2"], vec_ref[9:10])
        dr2_ref[r, :] = dr2
        br2 = dr2.astype(BF)
        br2_ref[r, :] = br2
        ga_ref[r, :] = nt(br2, packed_cross(pack_ref, core, 0)).astype(BF)
        gb_ref[r, :] = nt(br2, packed_cross(pack_ref, core, 1)).astype(BF)
        e3_sum, gain3, shift3 = at["sums"]
        sums = [col_sum(br2), e3_sum, col_sum(back * at["xhat2"]), col_sum(back), gain3, shift3]
        total = total + jnp.concatenate(sums + [jnp.zeros((2, dim), F32)], axis=0)
        ff_total = ff_total + jnp.concatenate(at["ff"] + [jnp.zeros((8 - len(at["ff"]), dim), F32)], axis=0)
    vsum_ref[...] = total
    fsum_ref[...] = ff_total


def middle(core, own, other, xhat1, cot, pack, vec, tile):
    tokens, dim = xhat1.shape
    hidden = 4 * dim
    half = dim // 2
    rows = lambda w: pl.BlockSpec((tile, w), lambda i, s: (i, 0))
    once = lambda a: pl.BlockSpec(a.shape, lambda *_: (0,) * a.ndim, pipeline_mode=pl.Buffered(1))
    sums = pl.BlockSpec((8, dim), lambda i, s: (0, 0))
    return call(
        "middle",
        middle_kernel,
        (tokens // tile,),
        [rows(half), rows(half), rows(dim), rows(dim), once(pack), once(vec)],
        [
            rows(dim),
            rows(hidden),
            rows(hidden),
            rows(dim),
            rows(dim),
            rows(dim),
            rows(dim),
            rows(half),
            rows(half),
            sums,
            sums,
        ],
        [
            shape((tokens, dim), F32),
            shape((tokens, hidden), BF),
            shape((tokens, hidden), BF),
            shape((tokens, dim), BF),
            shape((tokens, dim), BF),
            shape((tokens, dim), F32),
            shape((tokens, dim), BF),
            shape((tokens, half), BF),
            shape((tokens, half), BF),
            shape((8, dim), F32),
            shape((8, dim), F32),
        ],
        [core, own, other, xhat1, cot, pack, vec],
        scratch=[pltpu.VMEM((tile, hidden), F32)],
        room=56,
        flops=tokens * (4 * dim * dim + 8 * dim * hidden),
        prefetch=1,
    )


def before_self_kernel(
    core_ref,
    own_ref,
    oth_ref,
    dr2_ref,
    xhat_ref,
    rstd_ref,
    mat_ref,
    moth_ref,
    vec_ref,
    dr1_ref,
    br1_ref,
    ga_ref,
    gb_ref,
    vsum_ref,
    out_s,
):
    core = core_ref[0]
    width = own_ref.shape[1]

    @pl.when(pl.program_id(0) == 0)
    def _():
        join_columns(core, mat_ref.at[0], moth_ref.at[0], out_s)

    parts = [slice(i, i + CHUNK) for i in range(0, own_ref.shape[0], CHUNK)]
    grads = [dr2_ref[r, :] + nt(own_ref[r, :], mat_ref[1]) + nt(oth_ref[r, :], moth_ref[1]) for r in parts]
    total = jnp.where(pl.program_id(0) == 0, 0.0, vsum_ref[...])
    zero = jnp.zeros((5, xhat_ref.shape[1]), F32)
    for r, dfirst in zip(parts, grads):
        xhat = xhat_ref[r, :]
        dr1 = norm_back(dfirst, xhat, rstd_ref[r, :], vec_ref[7:8])
        dr1_ref[r, :] = dr1
        br1 = dr1.astype(BF)
        br1_ref[r, :] = br1
        ga_ref[r, :] = nt(br1, out_s[own_part(core, 0, width), :]).astype(BF)
        gb_ref[r, :] = nt(br1, out_s[own_part(core, 1, width), :]).astype(BF)
        total = total + jnp.concatenate([col_sum(br1), col_sum(dfirst * xhat), col_sum(dfirst), zero], axis=0)
    vsum_ref[...] = total


def before_self(core, own, other, dr2, xhat, rstd, mats, mats_other, vec, tile):
    tokens, dim = xhat.shape
    half = dim // 2
    rows = lambda w: pl.BlockSpec((tile, w), lambda i, s: (i, 0))
    return call(
        "before_self",
        before_self_kernel,
        (tokens // tile,),
        [rows(half), rows(half), rows(dim), rows(dim), rows(1), first_two(mats), first_two(mats), whole(vec)],
        [rows(dim), rows(dim), rows(half), rows(half), pl.BlockSpec((8, dim), lambda i, s: (0, 0))],
        [
            shape((tokens, dim), F32),
            shape((tokens, dim), BF),
            shape((tokens, half), BF),
            shape((tokens, half), BF),
            shape((8, dim), F32),
        ],
        [core, own, other, dr2, xhat, rstd, mats, mats_other, vec],
        scratch=[pltpu.VMEM((dim, dim), BF)],
        flops=4 * tokens * dim * dim,
        prefetch=1,
    )


def pair_grads_kernel(route, me_ref, xt_ref, yt_ref, a_ref, b_ref, *refs):
    n = pl.program_id(0)
    total = (nn(xt_ref[...], a_ref[0]) + nn(yt_ref[...], b_ref[0])).astype(BF)
    if route is None:
        refs[0][0] = total
        return
    bits, devices = route
    tile_ref, outs, block_s = refs[0], refs[1:-1], refs[-1]
    block_s[...] = total.reshape(block_s.shape)
    lot = block_s.shape[1]
    rows = pl.ds(pl.multiple_of(n * lot, lot), lot)
    last = outs[0].shape[1] - 8

    def store(out):
        def put(j, value):
            out[j, rows, :] = value

        return put

    def store_tile(out):
        def put(j, value):
            out[j, last:, :] = value

        return put

    send_blocks(bits, [], devices, me_ref[0], lambda k: block_s[k], [store(out) for out in outs])

    @pl.when(n == 0)
    def _():
        send_blocks(bits, [], devices, me_ref[0], lambda k: tile_ref[k], [store_tile(out) for out in outs])


def pair_grads(me, xt, yt, own, other, route=None):
    count, tokens, width = own.shape
    dim = xt.shape[0]
    grads = pl.BlockSpec((1, tokens, width), lambda i, *_: (i, 0, 0))
    operands, specs = [me, xt, yt, own, other], [whole(xt), whole(yt), grads, grads]
    if route is None:
        outs = [pl.BlockSpec((1, dim, width), lambda i, *_: (i, 0, 0))]
        shapes, scratch = [shape((count, dim, width), BF)], []
    else:
        bits, tiles = route
        devices = tiles.shape[0]
        lot, blocks = dim // devices, devices >> len(bits)
        shapes = [shape((blocks, count * lot + 8, width), BF)] * (1 << len(bits))
        outs = [whole(one) for one in shapes]
        scratch = [pltpu.VMEM((devices, lot, width), BF)]
        operands, specs, route = operands + [tiles], specs + [whole(tiles)], (bits, devices)
    return call(
        "pair_grads",
        functools.partial(pair_grads_kernel, route),
        (count,),
        specs,
        outs,
        shapes,
        operands,
        scratch=scratch,
        flops=4 * count * tokens * width * dim,
        prefetch=1,
    )


def route_sums(me, mine, received, plain, bits, count):
    lots = count
    _, dim, width = mine.shape
    lot = dim // lots
    total = mine.shape[0] + plain.shape[0]
    view = lambda a: a.reshape(a.shape[0], lots, lot, width)
    out = shape((lots >> len(bits), total, lot, width), BF)
    operands = [view(mine), view(received), view(plain)]

    def kernel(me_ref, a_ref, b_ref, p_ref, *outs):
        def load(k):
            both = (a_ref[:, k].astype(F32) + b_ref[:, k].astype(F32)).astype(BF)
            return both, p_ref[:, k]

        def store(out):
            def put(j, value):
                out[j, : a_ref.shape[0]] = value[0]
                out[j, a_ref.shape[0] :] = value[1]

            return put

        send_blocks(bits, [], count, me_ref[0], load, [store(o) for o in outs])

    return call(
        "route_sums",
        kernel,
        (1,),
        [whole(o) for o in operands],
        [whole(out)] * (1 << len(bits)),
        [out] * (1 << len(bits)),
        [me] + operands,
        prefetch=1,
    )


def token_grads_kernel(core_ref, so_ref, st_ref, br1_ref, low_ref, qo_ref, qt_ref, co_ref, ct_ref, br2_ref, mine_ref, away_ref, full_s):
    core = core_ref[0]
    width = so_ref.shape[1]

    def by_rows(own, other, grad, n):
        full_s[own_part(core, 0, width), :] = tn(own[...], grad[...]).astype(BF)
        full_s[own_part(core, 1, width), :] = tn(other[...], grad[...]).astype(BF)
        mine_ref[n] = full_s[:, own_part(core, 0, width)]
        away_ref[n] = full_s[:, own_part(core, 1, width)]

    by_rows(so_ref, st_ref, br1_ref, 0)
    mine_ref[1] = tn(low_ref[...], qo_ref[...]).astype(BF)
    away_ref[1] = tn(low_ref[...], qt_ref[...]).astype(BF)
    by_rows(co_ref, ct_ref, br2_ref, 2)


def token_grads(core, self_own, self_other, br1, low1, dcq_own, dcq_other, cross_own, cross_other, br2):
    operands = [self_own, self_other, br1, low1, dcq_own, dcq_other, cross_own, cross_other, br2]
    tokens, dim = br1.shape
    out = shape((3, dim, dim // 2), BF)
    return call(
        "token_grads",
        token_grads_kernel,
        (1,),
        [whole(o) for o in operands],
        [whole(out)] * 2,
        [out] * 2,
        [core] + operands,
        scratch=[pltpu.VMEM((dim, dim), BF)],
        flops=6 * tokens * dim * dim,
        prefetch=1,
    )


def feed_grads_kernel(low_ref, dpre_ref, act_ref, e3_ref, out_ref, low_s):
    n = pl.program_id(0)

    @pl.when(n == 0)
    def _():
        low_s[...] = low_ref[...].T

    lots, _, dim = out_ref.shape
    lot, some = dim // lots, lots // 4
    win = nn(low_s[...], dpre_ref[...]).astype(BF)
    out_ref[:, pl.ds(pl.multiple_of(n * lot, lot), lot), :] = win.reshape(lots, lot, dim)
    wout = tn(act_ref[...], e3_ref[...]).astype(BF)
    out_ref[pl.ds(pl.multiple_of(n * some, some), some), 4 * lot : 8 * lot, :] = wout.reshape(some, 4 * lot, dim)


def feed_grads(low2, dpre, act, e3):
    tokens, dim = low2.shape
    out = shape((LOTS, 8 * dim // LOTS, dim), BF)
    block = pl.BlockSpec((tokens, dim), lambda i: (0, i))
    return call(
        "feed_grads",
        feed_grads_kernel,
        (4,),
        [whole(low2), block, block, whole(e3)],
        [whole(out)],
        [out],
        [low2, dpre, act, e3],
        scratch=[pltpu.VMEM((dim, tokens), BF)],
        room=44,
        flops=16 * tokens * dim * dim,
    )[0]


def vec_rows_kernel(core_ref, self_ref, cross_ref, first_ref, mid_ref, ff_ref, out_ref, tiles_ref=None):
    core = core_ref[0]
    width = self_ref.shape[2]
    out_ref[...] = jnp.zeros_like(out_ref)
    self_sum, cross_sum = self_ref[0], cross_ref[0]
    for m in range(1, self_ref.shape[0]):
        self_sum, cross_sum = self_sum + self_ref[m], cross_sum + cross_ref[m]
    own = own_part(core, 0, width)
    out_ref[0:1, own] = self_sum[0:1]
    out_ref[1:2, own] = self_sum[2:3]
    out_ref[3:4, own] = cross_sum[0:1]
    out_ref[4:5, own] = cross_sum[2:3]
    out_ref[2:3, :] = first_ref[0:1]
    out_ref[5:7, :] = mid_ref[0:2]
    out_ref[7:9, :] = first_ref[1:3]
    out_ref[9:13, :] = mid_ref[2:6]
    out_ref[13:17, :] = ff_ref[0:4]
    if tiles_ref is not None:
        lots = tiles_ref.shape[0]
        lot, third = out_ref.shape[1] // lots, tiles_ref.shape[2] // 3
        tiles_ref[...] = jnp.zeros_like(tiles_ref)
        for d in range(lots):
            for n in range(3):
                piece = out_ref[8 * n : 8 * n + 8, d * lot : (d + 1) * lot]
                tiles_ref[d, :, n * third : n * third + lot] = piece.astype(BF)


def vec_rows(core, self_sums, cross_sums, first_sums, mid_sums, ff_sums, devices=None):
    operands = [self_sums, cross_sums, first_sums, mid_sums, ff_sums]
    dim = first_sums.shape[1]
    outs = [shape((24, dim), F32)]
    if devices is not None:
        outs.append(shape((devices, 8, dim // 2), BF))
    return call(
        "vec_rows",
        vec_rows_kernel,
        (1,),
        [whole(o) for o in operands],
        [whole(o) for o in outs],
        outs,
        [core] + operands,
        prefetch=1,
    )


def input_grad_kernel(count, has_start, *refs):
    start = refs[0] if has_start else None
    own, oth, mats_a, mats_b, out = refs[has_start:]
    total = start[...] if has_start else None
    for n in range(count):
        for grads, mats in ((own, mats_a), (oth, mats_b)):
            t = nt(grads[n], mats[n])
            total = t if total is None else total + t
    out[...] = total


def input_grad(own, other, mats_own, mats_other, start, tile):
    count, tokens, half = own.shape
    dim = mats_own.shape[1]
    grads = pl.BlockSpec((count, tile, half), lambda i: (0, i, 0))
    rows = pl.BlockSpec((tile, dim), lambda i: (i, 0))
    has_start = start is not None
    return call(
        "input_grad",
        functools.partial(input_grad_kernel, count, has_start),
        (tokens // tile,),
        ([rows] if has_start else []) + [grads, grads, whole(mats_own), whole(mats_other)],
        [rows],
        [shape((tokens, dim), F32)],
        ([start] if has_start else []) + [own, other, mats_own, mats_other],
        flops=4 * count * tokens * half * dim,
    )[0]


def adam_step(master, first_m, second_m, grad_sum, rate, decay):
    first_new = 0.5 * first_m + 0.5 * grad_sum
    second_new = 0.5 * second_m + 0.5 * grad_sum * grad_sum
    fix_term = 1.0 - 0.5**STEP
    update = first_new / fix_term / (jnp.sqrt(second_new / fix_term) + adam_eps)
    master_new = master - rate * (update + decay * master)
    return (master_new, first_new, second_new, master_new.astype(BF))


def on_device(
    target,
    memory,
    cotangent,
    seg_target,
    seg_memory,
    attn_master,
    attn_first,
    attn_second,
    in_master,
    in_first,
    in_second,
    out_master,
    out_first,
    out_second,
    vec_master,
    vec_first,
    vec_second,
):
    both = ("seq", "fsdp")
    devices = lax.axis_size("seq") * lax.axis_size("fsdp")
    core_at = lax.axis_index("seq") & 1
    core = core_at.astype(jnp.int32).reshape(1)
    is_low = core_at == 0
    place = lax.axis_index("seq") * lax.axis_size("fsdp") + lax.axis_index("fsdp")
    me = place.astype(jnp.int32).reshape(1)
    micro, _, rows, dim = target.shape
    half, hidden = dim // 2, in_master.shape[1]
    tokens = micro * rows
    shard = attn_master.shape[1]
    sets = bit_sets(devices)
    near = flips(sets[0])
    thin = sets[:1] + [[b] for bits in sets[1:] for b in bits]
    chip_bits = [b for bits in sets[::-1] for b in bits[::-1]]
    all_bits = sorted(chip_bits + [1], reverse=True)
    direct = devices == LOTS
    partner = lambda a: moved(a, CORE)

    x_own, m_own = target[:, 0], memory[:, 0]
    seg_own = jnp.concatenate([seg_target[:, 0], seg_memory[:, 0]], axis=0)
    attn_low = attn_master.astype(BF)
    in_low = in_master.astype(BF)
    out_low = out_master.astype(BF)
    vec_low = vec_master.astype(BF)

    def column_halves(mats):
        mine = jnp.where(is_low, mats[:, :, :half], mats[:, :, half:])
        other = partner(jnp.where(is_low, mats[:, :, half:], mats[:, :, :half]))
        return jnp.stack([jnp.where(is_low, mine, other), jnp.where(is_low, other, mine)])

    x_other, seg_other, m_other = partner(x_own), partner(seg_own), partner(m_own)
    if direct:
        halves = column_halves(attn_low[0:7]).reshape(2, 7 * shard, half)
        low_tile = as_tile(vec_low, half)
        far_tile = partner(low_tile)
        tiles = jnp.stack([jnp.where(is_low, low_tile, far_tile), jnp.where(is_low, far_tile, low_tile)])
        ends = (3 * shard, 7 * shard, 7 * shard + 8)
        cuts = list(zip((0,) + ends[:2], ends))
        (self_far, late_far, vec_far), rels = far_parts(jnp.concatenate([halves, tiles], axis=1), sets, cuts)
        feed_low = in_low.reshape(shard, 4, dim).transpose(1, 0, 2).reshape(4 * shard, dim)
        pack = jnp.concatenate([feed_low, out_low, attn_low[7]], axis=0)
        self_far, x_own, m_own, x_other, m_other, seg_other, pack, vec_far = lax.optimization_barrier(
            (self_far, x_own, m_own, x_other, m_other, seg_other, pack, vec_far)
        )
        pack = lax.all_gather(pack, both, axis=0, tiled=False)
        self_parts = near_parts(self_far, sets)
        vec_parts = near_parts(vec_far, sets)
        self_mats = (self_parts, near, rels)
        vec_tiles = assemble(me, vec_parts, near, rels, 8)[0].reshape(devices, 8, half)
        vec_all = from_tile(vec_tiles, vec_low.shape[0], vec_low.shape[1])
        vec_all, x_own, m_own = lax.optimization_barrier((vec_all, x_own, m_own))
        self_parts[1:], late_far = lax.optimization_barrier((self_parts[1:], late_far))
        late_parts = near_parts(late_far, sets)
    else:

        def gather_half(mats):
            stacked = jnp.moveaxis(column_halves(mats), 0, 1)
            return gather_bits(stacked, chip_bits, [1]).reshape(mats.shape[0], dim, half)

        self_mats = gather_half(attn_low[0:3])
        late_mats = gather_half(attn_low[3:7])
        lots = lambda a: a.reshape(LOTS, -1, dim)
        win = lax.all_gather(in_low, both, axis=0, tiled=True)
        pack = jnp.concatenate(
            [lots(win[:, n * dim : (n + 1) * dim]) for n in range(4)]
            + [lots(lax.all_gather(out_low, both, axis=0, tiled=True))]
            + [lots(lax.all_gather(attn_low[7], both, axis=0, tiled=True))],
            axis=1,
        )
        vec_all = gather_bits(vec_low[None], [1] + chip_bits).reshape(devices, *vec_low.shape)
    vec = vec_all.transpose(1, 0, 2).reshape(vec_low.shape[0], dim).astype(F32)

    seg_t, seg_m = (jnp.concatenate([a, b], axis=1) for a, b in zip(
        (seg_own[:micro], seg_own[micro:]), (seg_other[:micro], seg_other[micro:])
    ))
    seg_t_ordered = jnp.where(is_low, seg_t, jnp.concatenate([seg_other[:micro], seg_own[:micro]], axis=1))
    row = lambda a: a[:, None, :]
    own_cols = lambda n: jnp.where(is_low, vec[n, :half], vec[n, half:])
    zeros = jnp.zeros((half,), F32)
    flat = lambda a: a.reshape(-1, a.shape[-1])
    flat3 = lambda a: a.reshape(a.shape[0], tokens, half)
    tall = lambda a: a.reshape(micro, rows, half)
    across = [flat(a).T for a in (x_own, x_other, m_own, m_other)]
    x_own, across = lax.optimization_barrier((x_own, across))

    qkv, self_mats = project(
        core, me, x_own, x_other, self_mats, jnp.stack([own_cols(0), zeros, own_cols(1)])[:, None], 0.125, True
    )
    self_own, self_send, self_exact, self_log = attention(
        True, core, None, (qkv, 1), row(seg_t_ordered), row(seg_t_ordered)
    )
    if direct:
        self_own, late_parts[0] = lax.optimization_barrier((self_own, late_parts[0]))
        late_mats = assemble(me, late_parts, near, rels, shard)
    late_other = partner(late_mats)
    mem_kv, _ = project(
        core, me, m_own, m_other, late_mats[2:4], jnp.stack([zeros, own_cols(4)])[:, None], 1.0, False
    )
    self_other_mats = partner(self_mats)
    mem_kv, late_other, self_other_mats = lax.optimization_barrier((mem_kv, late_other, self_other_mats))
    self_own, self_other = flat(self_own), flat(partner(self_send))
    xhat1, rstd1, first_low, cq_own, cq_send = after_self(
        core, self_own, self_other, flat(x_own), late_mats, late_other, vec, 2 * CHUNK
    )
    cq_own, cq_other = tall(cq_own), tall(partner(cq_send))
    cross_own, cross_send, cross_exact, cross_log = attention(
        False, core, (cq_own, cq_other), (mem_kv, 0), row(seg_t), row(seg_m)
    )
    cross_own, cross_other = flat(cross_own), flat(partner(cross_send))

    (block, act, d_pre, second_low, e3, d_r2, br2, dco_own, dco_send, mid_sums, ff_sums) = middle(
        core, cross_own, cross_other, xhat1, flat(cotangent[:, 0]), pack, vec, 2 * CHUNK
    )
    dco_own, dco_other = tall(dco_own), tall(partner(dco_send))
    feed = feed_grads(second_low, d_pre, act, e3)
    if direct:
        feed = lax.psum_scatter(feed, both, scatter_dimension=0, tiled=False)
        sum_in_mat = feed[: 4 * shard].reshape(4, shard, dim).transpose(1, 0, 2).reshape(shard, hidden)
        sum_out_mat = feed[4 * shard :]
    else:
        lot = dim // LOTS
        in_parts = [feed[:, n * lot : (n + 1) * lot].reshape(dim, dim) for n in range(4)]
        sum_in_mat = lax.psum_scatter(jnp.concatenate(in_parts, axis=1), both, scatter_dimension=0, tiled=True)
        sum_out_mat = lax.psum_scatter(
            feed[:, 4 * lot :].reshape(hidden, dim), both, scatter_dimension=0, tiled=True
        )
    dcq_own, dcq_send, d_mem_own, d_mem_other, cross_sums = attention(
        False,
        core,
        (cq_own, cq_other),
        (mem_kv, 0),
        row(seg_t),
        row(seg_m),
        (dco_own, dco_other, cross_exact, cross_log),
    )
    dcq_own, dcq_other = flat(dcq_own), flat(partner(dcq_send))
    d_r1, br1, dso_own, dso_send, first_sums = before_self(
        core, dcq_own, dcq_other, d_r2, xhat1, rstd1, late_mats, late_other, vec, 2 * CHUNK
    )
    dso_own, dso_other = tall(dso_own), tall(partner(dso_send))

    def reduce_whole(mats):
        spread = mats.reshape([mats.shape[0]] + [2] * len(all_bits) + [shard, half])
        summed = scatter_bits(spread, chip_bits[::-1], all_bits)
        mine = jnp.where(is_low, summed[:, 0], summed[:, 1])
        other = partner(jnp.where(is_low, summed[:, 1], summed[:, 0]))
        return both_halves(is_low, mine, other)

    d_mem_own, d_mem_other = flat3(d_mem_own), flat3(d_mem_other)
    grads_mine, grads_away = token_grads(
        core, self_own, self_other, br1, first_low, dcq_own, dcq_other, cross_own, cross_other, br2
    )
    grads_mem = pair_grads(me, across[2], across[3], d_mem_own, d_mem_other)[0]
    grads_got = partner(grads_away)
    d_mem_in = partner(d_mem_other)
    if direct:
        routed = list(route_sums(me, grads_mine, grads_got, grads_mem, sets[0], devices))
        dso_own, routed[0], d_mem_in = lax.optimization_barrier((dso_own, routed[0], d_mem_in))
        cross_near, _ = reduce_near(me, routed, thin, devices)
    else:
        summed = (grads_mine.astype(F32) + grads_got.astype(F32)).astype(BF)
        sum_cross = reduce_whole(jnp.concatenate([summed, grads_mem]))

    d_self_own, d_self_away, self_sums = attention(
        True,
        core,
        None,
        (qkv, 1),
        row(seg_t_ordered),
        row(seg_t_ordered),
        (dso_own, dso_other, self_exact, self_log),
    )
    d_self_own, d_self_away = flat3(d_self_own), flat3(d_self_away)
    grad_m = input_grad(d_mem_own, d_mem_in, late_mats[2:4], late_other[2:4], None, 2 * CHUNK)
    vec_grad = vec_rows(core, self_sums, cross_sums, first_sums, mid_sums, ff_sums, devices if direct else None)
    if direct:
        routed = list(
            pair_grads(me, across[0], across[1], d_self_own, d_self_away, (sets[0], vec_grad[1]))
        )
        d_self_away, routed, cross_near = lax.optimization_barrier((d_self_away, routed, cross_near))

    d_self_other = partner(d_self_away)
    grad_x = input_grad(d_self_own, d_self_other, self_mats, self_other_mats, d_r1, 2 * CHUNK)
    if direct:
        mine, other, (grad_m, grad_x) = reduce_far(me, cross_near, thin, devices, [grad_m, grad_x])
        self_near, (mine, grad_m, grad_x) = reduce_near(me, routed, sets, devices, (mine, grad_m, grad_x))
        sum_cross = both_halves(is_low, mine, other)
        mine, other, _ = reduce_far(me, self_near, sets, devices)
        last = 3 * shard
        sum_self = both_halves(is_low, mine[:last], other[:last]).reshape(3, shard, dim)
        tile = mine[last:].astype(F32) + other[last:].astype(F32)
        sum_vec = from_tile(tile, *vec_master.shape)
    else:
        sum_self = reduce_whole(pair_grads(me, across[0], across[1], d_self_own, d_self_away)[0])
        all_rows = vec_grad[0]
        for bit in [1] + chip_bits[::-1]:
            all_rows = all_rows + moved(all_rows, 1 << bit)
        width = vec_master.shape[1]
        sum_vec = lax.dynamic_slice_in_dim(all_rows[: vec_master.shape[0]], place * width, width, axis=1)

    sum_attn = jnp.concatenate(
        [sum_self, sum_cross[0:2], sum_cross[3:5], sum_cross[2:3]], axis=0
    ).astype(F32)
    attn_new, attn_m, attn_s, attn_w = adam_step(attn_master, attn_first, attn_second, sum_attn, 0.1, 0.01)
    in_new, in_m, in_s, in_w = adam_step(in_master, in_first, in_second, sum_in_mat.astype(F32), 0.05, 0.01)
    out_new, out_m, out_s, out_w = adam_step(out_master, out_first, out_second, sum_out_mat.astype(F32), 0.03, 0.01)
    vec_new, vec_m, vec_s, vec_w = adam_step(vec_master, vec_first, vec_second, sum_vec, 0.3, 0.0)
    return (
        block.reshape(micro, 1, rows, dim),
        grad_x.reshape(micro, 1, rows, dim),
        grad_m.reshape(micro, 1, rows, dim),
        attn_new,
        attn_m,
        attn_s,
        attn_w,
        in_new,
        in_m,
        in_s,
        in_w,
        out_new,
        out_m,
        out_s,
        out_w,
        vec_new,
        vec_m,
        vec_s,
        vec_w,
    )


def solution(mesh):
    tokens = P(None, "fsdp", "seq", None)
    marks = P(None, "fsdp", "seq")
    attn = P(None, ("seq", "fsdp"), None)
    feed = P(("seq", "fsdp"), None)
    rows = P(None, ("seq", "fsdp"))
    return jax.shard_map(
        on_device,
        mesh=mesh,
        in_specs=(tokens,) * 3 + (marks,) * 2 + (attn,) * 3 + (feed,) * 6 + (rows,) * 3,
        out_specs=(tokens,) * 3 + (attn,) * 4 + (feed,) * 8 + (rows,) * 4,
        check_vma=False,
    )
```

```python
import functools

import jax
import jax.numpy as jnp
from jax import lax
from jax.experimental import pallas as pl
from jax.experimental.pallas import tpu as pltpu
from jax.sharding import PartitionSpec as P

HDIM = 64
STEP = 10
PAIR = 2 * HDIM
CHUNK = 256
DOCS = 5
MASKED = -1e30
BOUND = 3000.0

BF = jnp.bfloat16
F32 = jnp.float32

norm_eps = 1e-05
adam_eps = 1e-08
MIB = 2**20


def nn(a, b):
    return lax.dot_general(a, b, (((1,), (0,)), ((), ())), preferred_element_type=F32)


def nt(a, b):
    return lax.dot_general(a, b, (((1,), (1,)), ((), ())), preferred_element_type=F32)


def tn(a, b):
    return lax.dot_general(a, b, (((0,), (0,)), ((), ())), preferred_element_type=F32)


def call(name, kernel, grid, in_specs, out_specs, out_shape, operands, scratch=(), flops=0, prefetch=0, room=28, cost=0.01):
    size = cost * sum(leaf.size * leaf.dtype.itemsize for leaf in list(operands) + list(out_shape))
    return pl.pallas_call(
        kernel,
        name=name,
        grid_spec=pltpu.PrefetchScalarGridSpec(
            num_scalar_prefetch=prefetch,
            grid=grid,
            in_specs=in_specs,
            out_specs=out_specs,
            scratch_shapes=scratch,
        ),
        out_shape=out_shape,
        compiler_params=pltpu.CompilerParams(vmem_limit_bytes=room * MIB),
        cost_estimate=pl.CostEstimate(flops=int(cost * flops), bytes_accessed=int(size), transcendentals=0),
    )(*operands)


def shape(dims, dtype):
    return jax.ShapeDtypeStruct(tuple(dims), dtype)


def whole(array):
    zeros = (0,) * array.ndim
    return pl.BlockSpec(array.shape, lambda *_: zeros)


CORE = 2


def moved(array, flip):
    count = lax.axis_size("seq") * lax.axis_size("fsdp")
    return lax.ppermute(array, ("seq", "fsdp"), [(i, i ^ flip) for i in range(count)])


def own_bit(bit):
    if bit == 0:
        return lax.axis_index("fsdp")
    return (lax.axis_index("seq") >> (bit - 1)) & 1


def bit_sets(count):
    bits = [0] + list(range(2, count.bit_length() - 1))
    return [bits[i : i + 2] for i in range(0, len(bits), 2)]


def flips(bits):
    out = [0]
    for bit in bits:
        out = out + [f | 1 << bit for f in out]
    return out


def gather_bits(array, order, present=()):
    present = sorted(present, reverse=True)
    for bit in order:
        other = moved(array, 1 << bit)
        place = 1 + sum(b > bit for b in present)
        low = own_bit(bit) == 0
        array = jnp.stack([jnp.where(low, array, other), jnp.where(low, other, array)], axis=place)
        present = sorted(present + [bit], reverse=True)
    return array


def scatter_bits(array, order, present):
    present = sorted(present, reverse=True)
    for bit in order:
        place = 1 + present.index(bit)
        mine = own_bit(bit)
        send = lax.dynamic_index_in_dim(array, 1 - mine, place, keepdims=False)
        keep = lax.dynamic_index_in_dim(array, mine, place, keepdims=False)
        array = (keep.astype(F32) + moved(send, 1 << bit).astype(F32)).astype(BF)
        present.remove(bit)
    return array


def as_tile(rows, width):
    third = width // 3
    full = jnp.pad(rows, ((0, 24 - rows.shape[0]), (0, third - rows.shape[1])))
    return jnp.concatenate([full[0:8], full[8:16], full[16:24]], axis=1)


def from_tile(tile, count, columns):
    third = tile.shape[-1] // 3
    groups = [tile[..., n * third : n * third + columns] for n in range(3)]
    return jnp.concatenate(groups, axis=-2)[..., :count, :]


def far_parts(stacked, sets, cuts):
    rels, array = [0], stacked[None]
    for bits in sets[:1:-1]:
        rels = [f ^ r for f in flips(bits) for r in rels]
        array = jnp.concatenate([array] + [moved(array, f) for f in flips(bits)[1:]], axis=0)
    got = [array] + [moved(array, f) for f in flips(sets[1])[1:]]
    rels = [f ^ r for f in flips(sets[1]) for r in rels]
    many = array.shape[0]

    def join_kernel(*refs):
        ins, outs = refs[: len(got)], refs[len(got) :]
        for out, (a, b) in zip(outs, cuts):
            for n, one in enumerate(ins):
                out[n * many : (n + 1) * many] = one[:, :, a:b]

    outs = [shape((many * len(got), 2, b - a, array.shape[3]), BF) for a, b in cuts]
    joined = call("join", join_kernel, (1,), [whole(one) for one in got], [whole(out) for out in outs], outs, got)
    return joined, rels


def near_parts(array, sets):
    return [array] + [moved(array, f) for f in flips(sets[0])[1:]]


def assemble_kernel(near, rels, me_ref, *refs):
    parts, out = refs[: len(near)], refs[-1]
    for part, f in zip(parts, near):
        for i, r in enumerate(rels):
            for c in range(2):
                out[0, ((me_ref[0] & ~CORE) ^ (f ^ r)) + CORE * c] = part[i, c]


def part_specs(parts, rows):
    return [pl.BlockSpec((p.shape[0], 2, rows, p.shape[3]), lambda i, *_: (0, 0, i, 0)) for p in parts]


def assemble(me, parts, near, rels, rows):
    _, _, total, cols = parts[0].shape
    count = total // rows
    lots = 2 * len(near) * len(rels)
    out = call(
        "assemble",
        functools.partial(assemble_kernel, near, rels),
        (count,),
        part_specs(parts, rows),
        [pl.BlockSpec((1, lots, rows, cols), lambda i, *_: (i, 0, 0, 0))],
        [shape((count, lots, rows, cols), BF)],
        [me] + parts,
        prefetch=1,
    )[0]
    return out.reshape(count, lots * rows, cols)


def compact(number, removed):
    out, place = 0, 0
    for bit in range(number.bit_length()):
        if bit not in removed:
            out |= (number >> bit & 1) << place
            place += 1
    return out


def send_blocks(bits, gone, count, me, load, outs):
    kept = [b for b in range(count.bit_length() - 1) if b not in gone]
    mask = sum(1 << kept.index(b) for b in bits)
    here = 0
    for b in bits:
        here = here + (((me >> b) & 1) << kept.index(b))
    total = 1 << len(kept)
    for f, out in zip(flips(bits), outs):
        small = sum(((f >> b) & 1) << kept.index(b) for b in bits)
        j = 0
        for k in range(total):
            if k & mask == 0:
                out(j, load((here ^ small) + k))
                j += 1


def combine_kernel(bits, gone, count, me_ref, *refs):
    outs = refs[-(1 << len(bits)) :]
    ins = refs[: len(refs) - len(outs)]

    def load(k):
        total = ins[0][k].astype(F32)
        for ref in ins[1:]:
            total = total + ref[k].astype(F32)
        return total.astype(BF)

    def store(out):
        def put(j, value):
            out[j] = value

        return put

    send_blocks(bits, gone, count, me_ref[0], load, [store(out) for out in outs])


def combine(me, arrays, bits, gone, count):
    blocks = arrays[0].shape[0] >> len(bits)
    out = shape((blocks,) + arrays[0].shape[1:], BF)
    return call(
        "combine",
        functools.partial(combine_kernel, bits, gone, count),
        (1,),
        [whole(a) for a in arrays],
        [whole(out)] * (1 << len(bits)),
        [out] * (1 << len(bits)),
        [me] + arrays,
        prefetch=1,
    )


def reduce_near(me, outs, sets, count, beside=None):
    got = [outs[0]] + [moved(out, f) for out, f in zip(outs[1:], flips(sets[0])[1:])]
    if beside is not None:
        got[0], beside = lax.optimization_barrier((got[0], beside))
    return combine(me, got, (sets[1:] + [[1]])[0], sets[0], count), beside


def reduce_step(me, outs, sets, n, count, behind=None):
    got = [outs[0]] + [moved(out, f) for out, f in zip(outs[1:], flips(sets[n])[1:])]
    if behind is not None:
        got, behind = lax.optimization_barrier((got, behind))
    return combine(me, got, (sets + [[1]])[n + 1], sum(sets[: n + 1], []), count), behind


def reduce_far(me, outs, sets, count, beside=()):
    gone, beside = sets[0], list(beside)
    for n, (here, after) in enumerate(zip(sets[1:], sets[2:] + [[1]])):
        gone = gone + here
        got = [outs[0]] + [moved(out, f) for out, f in zip(outs[1:], flips(here)[1:])]
        if n < len(beside):
            got[0], beside[n] = lax.optimization_barrier((got[0], beside[n]))
        outs = combine(me, got, after, gone, count)
    return outs[0][0], moved(outs[1], CORE)[0], beside


def both_halves(is_low, mine, other):
    return jnp.concatenate([jnp.where(is_low, mine, other), jnp.where(is_low, other, mine)], axis=-1)


def with_marks(pair, seg, half, lanes, is_key):
    mark = lanes - (HDIM if half == 0 else 0)
    mine = (lanes < HDIM) if half == 0 else (lanes >= HDIM)
    hit = seg == mark
    if is_key:
        extra = jnp.where(hit, 1.0, 0.0)
    else:
        extra = jnp.where(hit | (mark < 0) | (mark >= DOCS), 0.0, MASKED)
    return jnp.where(mine, pair.astype(F32), extra).astype(BF)


def down(row):
    return jnp.broadcast_to(row, (PAIR, row.shape[1])).T


def causal_tile():
    keys = lax.broadcasted_iota(jnp.int32, (CHUNK, CHUNK), 0)
    places = lax.broadcasted_iota(jnp.int32, (CHUNK, CHUNK), 1)
    return jnp.where(places >= keys, 0.0, MASKED)


def masked_scores(keys, queries, c, causal, tile):
    length = keys.shape[0]
    end = (c + 1) * CHUNK if causal else length
    s = nt(keys[:end], queries[c * CHUNK : (c + 1) * CHUNK])
    if causal:
        last = s[c * CHUNK :] + tile
        s = jnp.concatenate([s[: c * CHUNK], last], axis=0) if c else last
    return s


def halves_in(ref_a, ref_b, core, scratch):
    rows = ref_a.shape[-2]
    if core is None:
        scratch[0:rows, :] = ref_a[...].reshape(rows, PAIR)
        scratch[rows:, :] = ref_b[...].reshape(rows, PAIR)
    else:
        scratch[pl.ds(pl.multiple_of(core * rows, rows), rows), :] = ref_a[...].reshape(rows, PAIR)
        scratch[pl.ds(pl.multiple_of((1 - core) * rows, rows), rows), :] = ref_b[...].reshape(rows, PAIR)


def halves_out(scratch, core, ref_a, ref_b):
    rows = scratch.shape[0] // 2
    if core is None:
        a, b = scratch[0:rows, :], scratch[rows:, :]
    else:
        a = scratch[pl.ds(pl.multiple_of(core * rows, rows), rows), :]
        b = scratch[pl.ds(pl.multiple_of((1 - core) * rows, rows), rows), :]
    ref_a[...] = a.reshape(ref_a.shape)
    ref_b[...] = b.reshape(ref_b.shape)


def head_lanes():
    pick = lax.broadcasted_iota(jnp.int32, (8, PAIR), 1) // HDIM == lax.broadcasted_iota(jnp.int32, (8, PAIR), 0)
    return jnp.where(pick, 1.0, 0.0)


def forward_kernel(causal, core_ref, *refs):
    if causal:
        q_ref, k_ref, v_ref, sq_ref, sk_ref, own_ref, send_ref, exact_ref, log_ref, out_s = refs
        core = core_ref[0]
        q = q_ref[0, 0]
    else:
        qa_ref, qb_ref, k_ref, v_ref, sq_ref, sk_ref, own_ref, send_ref, exact_ref, log_ref, out_s = refs
        core = None
        q = jnp.concatenate([qa_ref[0], qb_ref[0]], axis=0)
    k, v = k_ref[0, 0], v_ref[0, 0]
    sq, sk = down(sq_ref[0]), down(sk_ref[0])
    length = k.shape[0]
    lanes = lax.broadcasted_iota(jnp.int32, (length, PAIR), 1)
    tile = causal_tile() if causal else None
    across = v.astype(F32).T.astype(BF)
    ones = jnp.ones((16, length), BF)
    heads = [
        (
            with_marks(q, sq, half, lanes, False),
            with_marks(k, sk, half, lanes, True),
            jnp.concatenate([across[half * HDIM : (half + 1) * HDIM], ones], axis=0),
        )
        for half in range(2)
    ]
    square = lambda a: jnp.max(nt(head_lanes().astype(BF), (a.astype(F32) * a.astype(F32)).astype(BF)))
    bounded = square(q) * square(k) < BOUND

    def every_chunk(with_top):
        done = {}

        def finish(c, half, s):
            if with_top:
                top = jnp.max(s, axis=0, keepdims=True)
                s = s - top
            p = jnp.exp(s).astype(BF)
            mixed = nn(heads[half][2][:, : s.shape[0]], p)
            total = mixed[HDIM : HDIM + 1]
            log = jnp.log(total)
            done[half] = (mixed[:HDIM] * (1.0 / total), log + top if with_top else log)
            if half == 1:
                cs = slice(c * CHUNK, (c + 1) * CHUNK)
                both = jnp.concatenate([done[0][0], done[1][0]], axis=0).T
                exact_ref[0, cs, :] = both
                out_s[cs, :] = both.astype(BF)
                log_ref[0, 0, 0:1, cs] = done[0][1]
                log_ref[0, 0, 1:2, cs] = done[1][1]

        waiting = None
        for c in reversed(range(length // CHUNK)):
            for half in range(2):
                s = masked_scores(heads[half][1], heads[half][0], c, causal, tile)
                if waiting is not None:
                    finish(*waiting)
                waiting = (c, half, s)
        finish(*waiting)

    @pl.when(bounded)
    def _():
        every_chunk(False)

    @pl.when(jnp.logical_not(bounded))
    def _():
        every_chunk(True)

    halves_out(out_s, core, own_ref, send_ref)


def backward_kernel(causal, core_ref, *refs):
    if causal:
        q_ref, k_ref, v_ref, sq_ref, sk_ref, ga_ref, gb_ref, exact_ref, log_ref = refs[:9]
        own_ref, send_ref, sum_ref, p_s, ds_s, g_s, out_s = refs[9:]
        core = core_ref[0]
        q = q_ref[0, 0]
    else:
        qa_ref, qb_ref, k_ref, v_ref, sq_ref, sk_ref, ga_ref, gb_ref, exact_ref, log_ref = refs[:10]
        own_ref, send_ref, kv_own_ref, kv_oth_ref, sum_ref, p_s, ds_s, g_s, out_s = refs[10:]
        core = None
        q = jnp.concatenate([qa_ref[0], qb_ref[0]], axis=0)
    k, v = k_ref[0, 0], v_ref[0, 0]
    sq, sk = down(sq_ref[0]), down(sk_ref[0])
    length = k.shape[0]
    chunks = length // CHUNK
    halves_in(ga_ref, gb_ref, core, g_s)
    grad = g_s[...]
    lanes = lax.broadcasted_iota(jnp.int32, (length, PAIR), 1)
    tile = causal_tile() if causal else None
    pick = lax.broadcasted_iota(jnp.int32, (8, PAIR), 1) // HDIM == lax.broadcasted_iota(jnp.int32, (8, PAIR), 0)
    delta = lax.dot_general(
        jnp.where(pick, 1.0, 0.0),
        grad.astype(F32) * exact_ref[0],
        (((1,), (1,)), ((), ())),
        precision=lax.Precision.HIGHEST,
        preferred_element_type=F32,
    )
    heads = []
    for half in range(2):
        mine = (lanes < HDIM) if half == 0 else (lanes >= HDIM)
        only = lambda a: jnp.where(mine, a.astype(F32), 0.0)
        heads.append(
            dict(
                q=with_marks(q, sq, half, lanes, False),
                k=with_marks(k, sk, half, lanes, True),
                qm=only(q).astype(BF),
                kt=only(k).T.astype(BF),
                gm=only(grad).astype(BF),
                log=log_ref[0, 0, half : half + 1, :],
                delta=delta[half : half + 1, :],
            )
        )
    dq, dk, dv = {}, {}, {}

    def products(c, half):
        h = heads[half]
        cs = slice(c * CHUNK, (c + 1) * CHUNK)
        s = masked_scores(h["k"], h["q"], c, causal, tile)
        return s, nt(v[: s.shape[0]], h["gm"][cs])

    def finish(c, half, s, dp):
        h = heads[half]
        cs = slice(c * CHUNK, (c + 1) * CHUNK)
        end = s.shape[0]
        p = jnp.exp(s - h["log"][:, cs])
        ds = (p * (dp - h["delta"][:, cs])).astype(BF)
        p_s[half, :end, cs] = p.astype(BF)
        ds_s[half, :end, cs] = ds
        t = nn(h["kt"][:, :end], ds)
        dq[c] = t if half == 0 else dq[c] + t

    def keys_side(kb, half):
        h = heads[half]
        q0 = kb * CHUNK if causal else 0
        ks = slice(kb * CHUNK, (kb + 1) * CHUNK)
        a = nn(p_s[half, ks, q0:], h["gm"][q0:])
        b = nn(ds_s[half, ks, q0:], h["qm"][q0:])
        dv[kb] = a if half == 0 else dv[kb] + a
        dk[kb] = b if half == 0 else dk[kb] + b

    waiting = None
    for half in range(2):
        for c in range(chunks):
            pair = products(c, half)
            if waiting is not None:
                finish(*waiting)
            waiting = (c, half, *pair)
            if half == 1 and c > 0:
                keys_side(c - 1, 0)
    finish(*waiting)
    keys_side(chunks - 1, 0)
    for kb in range(chunks):
        keys_side(kb, 1)

    def put(n, parts):
        low = [part.astype(BF) for part in parts]
        for c in range(chunks):
            out_s[n, c * CHUNK : (c + 1) * CHUNK, :] = low[c]
        return sum(jnp.sum(one.astype(F32), axis=0, keepdims=True) for one in low)

    sum_q = put(0, [dq[c].T.astype(BF).astype(F32) * 0.125 for c in range(chunks)])
    sum_k = put(1, [dk[c] for c in range(chunks)])
    sum_v = put(2, [dv[c] for c in range(chunks)])
    pad = jnp.zeros((5, PAIR), F32)
    sum_ref[0] = jnp.concatenate([sum_q, sum_k, sum_v, pad], axis=0)
    if causal:
        for n in range(3):
            halves_out(out_s.at[n], core, own_ref.at[n], send_ref.at[n])
    else:
        halves_out(out_s.at[0], core, own_ref, send_ref)
        for n in range(2):
            halves_out(out_s.at[1 + n], None, kv_own_ref.at[n], kv_oth_ref.at[n])


def attention(causal, core, queries, keys, seg_q, seg_k, backward=None):
    source, k_at = keys
    _, micro, length, width = source.shape
    pairs = width // PAIR
    part = pl.BlockSpec((1, length // 2, PAIR), lambda i, j, s: (i, 0, j))
    full = pl.BlockSpec((1, length, PAIR), lambda i, j, s: (i, 0, j))
    at = lambda n: pl.BlockSpec((1, 1, length, PAIR), lambda i, j, s: (n, i, 0, j))
    seg = pl.BlockSpec((1, 1, length), lambda i, j, s: (i, 0, 0))
    stat = pl.BlockSpec((1, 1, 8, length), lambda i, j, s: (i, j, 0, 0))
    if causal:
        operands, specs = [source], [at(0)]
    else:
        operands, specs = list(queries), [part, part]
    operands += [source, source, seg_q, seg_k]
    specs += [at(k_at), at(k_at + 1), seg, seg]
    share = 0.625 if causal else 1.0
    unit = 2 * micro * pairs * 2 * length * length * PAIR * share
    half_out = shape((micro, length // 2, width), BF)
    if backward is None:
        return call(
            "attend",
            functools.partial(forward_kernel, causal),
            (micro, pairs),
            specs,
            [part, part, full, stat],
            [half_out, half_out, shape((micro, length, width), F32), shape((micro, pairs, 8, length), F32)],
            [core] + operands,
            scratch=[pltpu.VMEM((length, PAIR), BF)],
            cost=0.1,
            flops=unit * 2,
            prefetch=1,
        )
    operands += list(backward)
    specs += [part, part, full, stat]
    sums = pl.BlockSpec((1, 8, PAIR), lambda i, j, s: (i, 0, j))
    scratch = [
        pltpu.VMEM((2, length, length), BF),
        pltpu.VMEM((2, length, length), BF),
        pltpu.VMEM((length, PAIR), BF),
        pltpu.VMEM((3, length, PAIR), BF),
    ]
    if causal:
        part3 = pl.BlockSpec((3, 1, length // 2, PAIR), lambda i, j, s: (0, i, 0, j))
        outs = [part3, part3, sums]
        shapes = [shape((3, micro, length // 2, width), BF)] * 2
    else:
        part2 = pl.BlockSpec((2, 1, length // 2, PAIR), lambda i, j, s: (0, i, 0, j))
        outs = [part, part, part2, part2, sums]
        shapes = [half_out, half_out] + [shape((2, micro, length // 2, width), BF)] * 2
    return call(
        "attend_back",
        functools.partial(backward_kernel, causal),
        (micro, pairs),
        specs,
        outs,
        shapes + [shape((micro, 8, width), F32)],
        [core] + operands,
        scratch=scratch,
        room=36,
        cost=0.1,
        flops=unit * 5,
        prefetch=1,
    )


def project_kernel(first_scale, ordered, gather, *refs):
    core_ref, refs = refs[0], refs[1:]
    if gather is None:
        a_ref, b_ref, w_ref, bias_ref, out_ref = refs
        mat = w_ref[0]
    else:
        near, rels = gather
        me_ref, a_ref, b_ref = refs[:3]
        parts = refs[3 : 3 + len(near)]
        bias_ref, out_ref, mat_ref = refs[3 + len(near) :]
        assemble_kernel(near, rels, me_ref, *parts, mat_ref)
        mat = mat_ref[0].reshape(a_ref.shape[-1], mat_ref.shape[-1])
    rows = a_ref.shape[1]
    scale = jnp.where(pl.program_id(0) == 0, first_scale, 1.0).astype(F32)
    for m in range(a_ref.shape[0]):
        for slot, ref in enumerate((a_ref, b_ref)):
            low = ((nn(ref[m], mat) + bias_ref[0]) * scale).astype(BF)
            place = (core_ref[0] ^ slot) * rows if ordered else slot * rows
            out_ref[0, m, pl.ds(pl.multiple_of(place, rows), rows), :] = low


def project(core, me, own, other, mats, biases, scale, ordered):
    micro, rows, depth = own.shape
    count, _, width = biases.shape
    tokens = pl.BlockSpec(own.shape, lambda i, *_: (0, 0, 0))
    mat_spec = pl.BlockSpec((1, depth, width), lambda i, *_: (i, 0, 0))
    bias_spec = pl.BlockSpec((1, 1, width), lambda i, *_: (i, 0, 0))
    out_specs = [pl.BlockSpec((1, micro, 2 * rows, width), lambda i, *_: (i, 0, 0, 0))]
    out_shape = [shape((count, micro, 2 * rows, width), BF)]
    flops = 2 * count * micro * 2 * rows * depth * width
    if not isinstance(mats, tuple):
        out = call(
            "project",
            functools.partial(project_kernel, scale, ordered, None),
            (count,),
            [tokens, tokens, mat_spec, bias_spec],
            out_specs,
            out_shape,
            [core, own, other, mats, biases],
            flops=flops,
            prefetch=1,
        )[0]
        return out, mats
    parts, near, rels = mats
    lot = depth // (2 * len(near) * len(rels))
    out, full = call(
        "project",
        functools.partial(project_kernel, scale, ordered, (near, rels)),
        (count,),
        [tokens, tokens] + part_specs(parts, lot) + [bias_spec],
        out_specs + [pl.BlockSpec((1, depth // lot, lot, width), lambda i, *_: (i, 0, 0, 0))],
        out_shape + [shape((count, depth // lot, lot, width), BF)],
        [core, me, own, other] + parts + [biases],
        flops=flops,
        prefetch=2,
    )
    return out, full.reshape(count, depth, width)


def normalise(r):
    mean = jnp.mean(r, axis=-1, keepdims=True)
    centred = r - mean
    rstd = lax.rsqrt(jnp.mean(centred * centred, axis=-1, keepdims=True) + norm_eps)
    return centred * rstd, rstd


def norm_back(dz, xhat, rstd, gain):
    dxhat = dz * gain
    a = jnp.mean(dxhat, axis=-1, keepdims=True)
    b = jnp.mean(dxhat * xhat, axis=-1, keepdims=True)
    return (dxhat - a - xhat * b) * rstd


def col_sum(a):
    return jnp.sum(a.astype(F32), axis=0, keepdims=True)


def own_part(core, swap, width):
    return pl.ds(pl.multiple_of((core ^ swap) * width, width), width)


def join_columns(core, own_ref, oth_ref, scratch):
    width = own_ref.shape[-1]
    scratch[:, own_part(core, 0, width)] = own_ref[...]
    scratch[:, own_part(core, 1, width)] = oth_ref[...]


def after_self_kernel(
    core_ref, own_ref, oth_ref, x_ref, mat_ref, moth_ref, vec_ref, xhat_ref, rstd_ref, low_ref, qa_ref, qb_ref, out_s
):
    core = core_ref[0]
    width = own_ref.shape[1]

    @pl.when(pl.program_id(0) == 0)
    def _():
        join_columns(core, mat_ref.at[0], moth_ref.at[0], out_s)

    parts = [slice(i, i + CHUNK) for i in range(0, own_ref.shape[0], CHUNK)]
    mixed = [
        nn(own_ref[r, :], out_s[own_part(core, 0, width), :]) + nn(oth_ref[r, :], out_s[own_part(core, 1, width), :])
        for r in parts
    ]
    for r, one in zip(parts, mixed):
        xhat, rstd = normalise(x_ref[r, :].astype(F32) + one + vec_ref[2:3])
        xhat_ref[r, :] = xhat
        rstd_ref[r, :] = rstd
        low = (xhat * vec_ref[7:8] + vec_ref[8:9]).astype(BF)
        low_ref[r, :] = low
        qa_ref[r, :] = ((nn(low, mat_ref[1]) + vec_ref[3:4, own_part(core, 0, width)]) * 0.125).astype(BF)
        qb_ref[r, :] = ((nn(low, moth_ref[1]) + vec_ref[3:4, own_part(core, 1, width)]) * 0.125).astype(BF)


def first_two(mats):
    return pl.BlockSpec((2,) + mats.shape[1:], lambda *_: (0, 0, 0))


def after_self(core, own, other, x, mats, mats_other, vec, tile):
    tokens, dim = x.shape
    rows = lambda w: pl.BlockSpec((tile, w), lambda i, s: (i, 0))
    half = dim // 2
    return call(
        "after_self",
        after_self_kernel,
        (tokens // tile,),
        [rows(half), rows(half), rows(dim), first_two(mats), first_two(mats), whole(vec)],
        [rows(dim), rows(1), rows(dim), rows(half), rows(half)],
        [
            shape((tokens, dim), F32),
            shape((tokens, 1), F32),
            shape((tokens, dim), BF),
            shape((tokens, half), BF),
            shape((tokens, half), BF),
        ],
        [core, own, other, x, mats, mats_other, vec],
        scratch=[pltpu.VMEM((dim, dim), BF)],
        flops=4 * tokens * dim * dim,
        prefetch=1,
    )


LOTS = 32


def packed_in(pack_ref, n):
    lots, dim = pack_ref.shape[0], pack_ref.shape[2]
    lot = dim // lots
    return pack_ref[:, n * lot : (n + 1) * lot, :].reshape(dim, dim)


def packed_out(pack_ref, n):
    lots, dim = pack_ref.shape[0], pack_ref.shape[2]
    lot, some = dim // lots, lots // 4
    return pack_ref[n * some : (n + 1) * some, 4 * lot : 8 * lot, :].reshape(dim, dim)


def packed_cross(pack_ref, core, swap):
    lots, dim = pack_ref.shape[0], pack_ref.shape[2]
    lot, some = dim // lots, lots // 2
    return pack_ref[own_part(core, swap, some), 8 * lot : 9 * lot, :].reshape(dim // 2, dim)


def middle_kernel(
    core_ref,
    own_ref,
    oth_ref,
    xhat1_ref,
    cot_ref,
    pack_ref,
    vec_ref,
    block_ref,
    act_ref,
    dpre_ref,
    low2_ref,
    e3_ref,
    dr2_ref,
    br2_ref,
    ga_ref,
    gb_ref,
    vsum_ref,
    fsum_ref,
    slope_s,
):
    core = core_ref[0]
    rows, dim = xhat1_ref.shape
    hidden = act_ref.shape[1]
    parts = [slice(i, i + CHUNK) for i in range(0, rows, CHUNK)]
    jobs = [(i, n) for n in range(hidden // dim) for i in range(len(parts))]
    state = [{} for _ in parts]

    def in_turn(make, use):
        waiting = None
        for job in jobs:
            made = make(*job)
            if waiting is not None:
                use(*waiting)
            waiting = (*job, made)
        use(*waiting)

    for at, r in zip(state, parts):
        first = xhat1_ref[r, :] * vec_ref[7:8] + vec_ref[8:9]
        mixed = nn(own_ref[r, :], packed_cross(pack_ref, core, 0)) + nn(oth_ref[r, :], packed_cross(pack_ref, core, 1))
        at["r2"] = first + mixed + vec_ref[5:6]
    for at, r in zip(state, parts):
        at["xhat2"], at["rstd2"] = normalise(at["r2"])
        second = at["xhat2"] * vec_ref[9:10] + vec_ref[10:11]
        at["low2"] = second.astype(BF)
        low2_ref[r, :] = at["low2"]
        at["r3"] = second + vec_ref[6:7]

    def before_gelu(i, n):
        return nn(state[i]["low2"], packed_in(pack_ref, n)) + vec_ref[13 + n : 14 + n]

    def gelu(i, n, pre):
        r, cs = parts[i], slice(n * dim, (n + 1) * dim)
        phi = 0.5 * (1.0 + lax.erf(pre * 0.7071067811865476))
        act = (pre * phi).astype(BF)
        act_ref[r, cs] = act
        slope_s[r, cs] = phi + pre * (jnp.exp(-0.5 * pre * pre) * 0.3989422804014327)
        state[i]["r3"] = state[i]["r3"] + nn(act, packed_out(pack_ref, n))

    in_turn(before_gelu, gelu)
    for at, r in zip(state, parts):
        xhat3, rstd3 = normalise(at["r3"])
        block_ref[r, :] = xhat3 * vec_ref[11:12] + vec_ref[12:13]
        dz = cot_ref[r, :].astype(F32)
        dr3 = norm_back(dz, xhat3, rstd3, vec_ref[11:12])
        at["e3"] = dr3.astype(BF)
        e3_ref[r, :] = at["e3"]
        at["back"] = dr3
        at["sums"] = [col_sum(at["e3"]), col_sum(dz * xhat3), col_sum(dz)]
        at["ff"] = []

    def act_grad(i, n):
        return nt(state[i]["e3"], packed_out(pack_ref, n))

    def gelu_back(i, n, grad):
        r, cs = parts[i], slice(n * dim, (n + 1) * dim)
        low = (grad * slope_s[r, cs]).astype(BF)
        dpre_ref[r, cs] = low
        state[i]["ff"].append(col_sum(low))
        state[i]["back"] = state[i]["back"] + nt(low, packed_in(pack_ref, n))

    in_turn(act_grad, gelu_back)
    first_step = pl.program_id(0) == 0
    total = jnp.where(first_step, 0.0, vsum_ref[...])
    ff_total = jnp.where(first_step, 0.0, fsum_ref[...])
    for at, r in zip(state, parts):
        back = at["back"]
        dr2 = norm_back(back, at["xhat2"], at["rstd2"], vec_ref[9:10])
        dr2_ref[r, :] = dr2
        br2 = dr2.astype(BF)
        br2_ref[r, :] = br2
        ga_ref[r, :] = nt(br2, packed_cross(pack_ref, core, 0)).astype(BF)
        gb_ref[r, :] = nt(br2, packed_cross(pack_ref, core, 1)).astype(BF)
        e3_sum, gain3, shift3 = at["sums"]
        sums = [col_sum(br2), e3_sum, col_sum(back * at["xhat2"]), col_sum(back), gain3, shift3]
        total = total + jnp.concatenate(sums + [jnp.zeros((2, dim), F32)], axis=0)
        ff_total = ff_total + jnp.concatenate(at["ff"] + [jnp.zeros((8 - len(at["ff"]), dim), F32)], axis=0)
    vsum_ref[...] = total
    fsum_ref[...] = ff_total


def middle(core, own, other, xhat1, cot, pack, vec, tile):
    tokens, dim = xhat1.shape
    hidden = 4 * dim
    half = dim // 2
    rows = lambda w: pl.BlockSpec((tile, w), lambda i, s: (i, 0))
    once = lambda a: pl.BlockSpec(a.shape, lambda *_: (0,) * a.ndim, pipeline_mode=pl.Buffered(1))
    sums = pl.BlockSpec((8, dim), lambda i, s: (0, 0))
    return call(
        "middle",
        middle_kernel,
        (tokens // tile,),
        [rows(half), rows(half), rows(dim), rows(dim), once(pack), once(vec)],
        [
            rows(dim),
            rows(hidden),
            rows(hidden),
            rows(dim),
            rows(dim),
            rows(dim),
            rows(dim),
            rows(half),
            rows(half),
            sums,
            sums,
        ],
        [
            shape((tokens, dim), F32),
            shape((tokens, hidden), BF),
            shape((tokens, hidden), BF),
            shape((tokens, dim), BF),
            shape((tokens, dim), BF),
            shape((tokens, dim), F32),
            shape((tokens, dim), BF),
            shape((tokens, half), BF),
            shape((tokens, half), BF),
            shape((8, dim), F32),
            shape((8, dim), F32),
        ],
        [core, own, other, xhat1, cot, pack, vec],
        scratch=[pltpu.VMEM((tile, hidden), F32)],
        room=56,
        flops=tokens * (4 * dim * dim + 8 * dim * hidden),
        prefetch=1,
    )


def before_self_kernel(
    core_ref,
    own_ref,
    oth_ref,
    dr2_ref,
    xhat_ref,
    rstd_ref,
    mat_ref,
    moth_ref,
    vec_ref,
    dr1_ref,
    br1_ref,
    ga_ref,
    gb_ref,
    vsum_ref,
    out_s,
):
    core = core_ref[0]
    width = own_ref.shape[1]

    @pl.when(pl.program_id(0) == 0)
    def _():
        join_columns(core, mat_ref.at[0], moth_ref.at[0], out_s)

    parts = [slice(i, i + CHUNK) for i in range(0, own_ref.shape[0], CHUNK)]
    grads = [dr2_ref[r, :] + nt(own_ref[r, :], mat_ref[1]) + nt(oth_ref[r, :], moth_ref[1]) for r in parts]
    total = jnp.where(pl.program_id(0) == 0, 0.0, vsum_ref[...])
    zero = jnp.zeros((5, xhat_ref.shape[1]), F32)
    for r, dfirst in zip(parts, grads):
        xhat = xhat_ref[r, :]
        dr1 = norm_back(dfirst, xhat, rstd_ref[r, :], vec_ref[7:8])
        dr1_ref[r, :] = dr1
        br1 = dr1.astype(BF)
        br1_ref[r, :] = br1
        ga_ref[r, :] = nt(br1, out_s[own_part(core, 0, width), :]).astype(BF)
        gb_ref[r, :] = nt(br1, out_s[own_part(core, 1, width), :]).astype(BF)
        total = total + jnp.concatenate([col_sum(br1), col_sum(dfirst * xhat), col_sum(dfirst), zero], axis=0)
    vsum_ref[...] = total


def before_self(core, own, other, dr2, xhat, rstd, mats, mats_other, vec, tile):
    tokens, dim = xhat.shape
    half = dim // 2
    rows = lambda w: pl.BlockSpec((tile, w), lambda i, s: (i, 0))
    return call(
        "before_self",
        before_self_kernel,
        (tokens // tile,),
        [rows(half), rows(half), rows(dim), rows(dim), rows(1), first_two(mats), first_two(mats), whole(vec)],
        [rows(dim), rows(dim), rows(half), rows(half), pl.BlockSpec((8, dim), lambda i, s: (0, 0))],
        [
            shape((tokens, dim), F32),
            shape((tokens, dim), BF),
            shape((tokens, half), BF),
            shape((tokens, half), BF),
            shape((8, dim), F32),
        ],
        [core, own, other, dr2, xhat, rstd, mats, mats_other, vec],
        scratch=[pltpu.VMEM((dim, dim), BF)],
        flops=4 * tokens * dim * dim,
        prefetch=1,
    )


def pair_grads_kernel(route, me_ref, xt_ref, yt_ref, a_ref, b_ref, *refs):
    n = pl.program_id(0)
    total = (nn(xt_ref[...], a_ref[0]) + nn(yt_ref[...], b_ref[0])).astype(BF)
    if route is None:
        refs[0][0] = total
        return
    bits, devices = route
    tile_ref, outs, block_s = refs[0], refs[1:-1], refs[-1]
    block_s[...] = total.reshape(block_s.shape)
    lot = block_s.shape[1]
    rows = pl.ds(pl.multiple_of(n * lot, lot), lot)
    last = outs[0].shape[1] - 8

    def store(out):
        def put(j, value):
            out[j, rows, :] = value

        return put

    def store_tile(out):
        def put(j, value):
            out[j, last:, :] = value

        return put

    send_blocks(bits, [], devices, me_ref[0], lambda k: block_s[k], [store(out) for out in outs])

    @pl.when(n == 0)
    def _():
        send_blocks(bits, [], devices, me_ref[0], lambda k: tile_ref[k], [store_tile(out) for out in outs])


def pair_grads(me, xt, yt, own, other, route=None):
    count, tokens, width = own.shape
    dim = xt.shape[0]
    grads = pl.BlockSpec((1, tokens, width), lambda i, *_: (i, 0, 0))
    operands, specs = [me, xt, yt, own, other], [whole(xt), whole(yt), grads, grads]
    if route is None:
        outs = [pl.BlockSpec((1, dim, width), lambda i, *_: (i, 0, 0))]
        shapes, scratch = [shape((count, dim, width), BF)], []
    else:
        bits, tiles = route
        devices = tiles.shape[0]
        lot, blocks = dim // devices, devices >> len(bits)
        shapes = [shape((blocks, count * lot + 8, width), BF)] * (1 << len(bits))
        outs = [whole(one) for one in shapes]
        scratch = [pltpu.VMEM((devices, lot, width), BF)]
        operands, specs, route = operands + [tiles], specs + [whole(tiles)], (bits, devices)
    return call(
        "pair_grads",
        functools.partial(pair_grads_kernel, route),
        (count,),
        specs,
        outs,
        shapes,
        operands,
        scratch=scratch,
        flops=4 * count * tokens * width * dim,
        prefetch=1,
    )


def route_sums(me, mine, received, plain, bits, count):
    lots = count
    _, dim, width = mine.shape
    lot = dim // lots
    total = mine.shape[0] + plain.shape[0]
    view = lambda a: a.reshape(a.shape[0], lots, lot, width)
    out = shape((lots >> len(bits), total, lot, width), BF)
    operands = [view(mine), view(received), view(plain)]

    def kernel(me_ref, a_ref, b_ref, p_ref, *outs):
        def load(k):
            both = (a_ref[:, k].astype(F32) + b_ref[:, k].astype(F32)).astype(BF)
            return both, p_ref[:, k]

        def store(out):
            def put(j, value):
                out[j, : a_ref.shape[0]] = value[0]
                out[j, a_ref.shape[0] :] = value[1]

            return put

        send_blocks(bits, [], count, me_ref[0], load, [store(o) for o in outs])

    return call(
        "route_sums",
        kernel,
        (1,),
        [whole(o) for o in operands],
        [whole(out)] * (1 << len(bits)),
        [out] * (1 << len(bits)),
        [me] + operands,
        prefetch=1,
    )


def token_grads_kernel(core_ref, so_ref, st_ref, br1_ref, low_ref, qo_ref, qt_ref, co_ref, ct_ref, br2_ref, mine_ref, away_ref, full_s):
    core = core_ref[0]
    width = so_ref.shape[1]

    def by_rows(own, other, grad, n):
        full_s[own_part(core, 0, width), :] = tn(own[...], grad[...]).astype(BF)
        full_s[own_part(core, 1, width), :] = tn(other[...], grad[...]).astype(BF)
        mine_ref[n] = full_s[:, own_part(core, 0, width)]
        away_ref[n] = full_s[:, own_part(core, 1, width)]

    by_rows(so_ref, st_ref, br1_ref, 0)
    mine_ref[1] = tn(low_ref[...], qo_ref[...]).astype(BF)
    away_ref[1] = tn(low_ref[...], qt_ref[...]).astype(BF)
    by_rows(co_ref, ct_ref, br2_ref, 2)


def token_grads(core, self_own, self_other, br1, low1, dcq_own, dcq_other, cross_own, cross_other, br2):
    operands = [self_own, self_other, br1, low1, dcq_own, dcq_other, cross_own, cross_other, br2]
    tokens, dim = br1.shape
    out = shape((3, dim, dim // 2), BF)
    return call(
        "token_grads",
        token_grads_kernel,
        (1,),
        [whole(o) for o in operands],
        [whole(out)] * 2,
        [out] * 2,
        [core] + operands,
        scratch=[pltpu.VMEM((dim, dim), BF)],
        flops=6 * tokens * dim * dim,
        prefetch=1,
    )


def feed_in_kernel(core_ref, low_ref, dpre_ref, mine_ref, away_ref, low_s, full_s):
    n = pl.program_id(0)

    @pl.when(n == 0)
    def _():
        low_s[...] = low_ref[...].T

    lots, _, half = mine_ref.shape
    lot = low_s.shape[0] // lots
    full_s[...] = nn(low_s[...], dpre_ref[...]).astype(BF)
    rows = pl.ds(pl.multiple_of(n * lot, lot), lot)
    mine_ref[:, rows, :] = full_s[:, own_part(core_ref[0], 0, half)].reshape(lots, lot, half)
    away_ref[:, rows, :] = full_s[:, own_part(core_ref[0], 1, half)].reshape(lots, lot, half)


def feed_out_kernel(core_ref, act_ref, e3_ref, mine_ref, away_ref, full_s):
    full_s[...] = tn(act_ref[...], e3_ref[...]).astype(BF)
    half = mine_ref.shape[2]
    mine_ref[...] = full_s[:, own_part(core_ref[0], 0, half)].reshape(mine_ref.shape)
    away_ref[...] = full_s[:, own_part(core_ref[0], 1, half)].reshape(away_ref.shape)


def feed_in_grads(core, low2, dpre):
    tokens, dim = low2.shape
    out = shape((LOTS, 4 * dim // LOTS, dim // 2), BF)
    return call(
        "feed_in_grads",
        feed_in_kernel,
        (4,),
        [whole(low2), pl.BlockSpec((tokens, dim), lambda i, s: (0, i))],
        [whole(out)] * 2,
        [out] * 2,
        [core, low2, dpre],
        scratch=[pltpu.VMEM((dim, tokens), BF), pltpu.VMEM((dim, dim), BF)],
        flops=8 * tokens * dim * dim,
        prefetch=1,
    )


def feed_out_grads(core, act, e3):
    tokens, dim = e3.shape
    lots = 4 * dim // LOTS
    out = shape((LOTS, lots, dim // 2), BF)
    return call(
        "feed_out_grads",
        feed_out_kernel,
        (4,),
        [pl.BlockSpec((tokens, dim), lambda i, s: (0, i)), whole(e3)],
        [pl.BlockSpec((LOTS // 4, lots, dim // 2), lambda i, s: (i, 0, 0))] * 2,
        [out] * 2,
        [core, act, e3],
        scratch=[pltpu.VMEM((dim, dim), BF)],
        flops=8 * tokens * dim * dim,
        prefetch=1,
    )


def route_feed(me, first, second, bits, count):
    rows = first[0].shape[1]
    out = shape((count >> len(bits), 2 * rows, first[0].shape[2]), BF)
    operands = list(first) + list(second)

    def kernel(me_ref, a_ref, b_ref, c_ref, d_ref, *outs):
        def load(k):
            one = (a_ref[k].astype(F32) + b_ref[k].astype(F32)).astype(BF)
            return one, (c_ref[k].astype(F32) + d_ref[k].astype(F32)).astype(BF)

        def store(out):
            def put(j, value):
                out[j, :rows] = value[0]
                out[j, rows:] = value[1]

            return put

        send_blocks(bits, [], count, me_ref[0], load, [store(o) for o in outs])

    return call(
        "route_feed",
        kernel,
        (1,),
        [whole(o) for o in operands],
        [whole(out)] * (1 << len(bits)),
        [out] * (1 << len(bits)),
        [me] + operands,
        prefetch=1,
        room=36,
    )


def vec_rows_kernel(core_ref, self_ref, cross_ref, first_ref, mid_ref, ff_ref, out_ref, tiles_ref=None):
    core = core_ref[0]
    width = self_ref.shape[2]
    out_ref[...] = jnp.zeros_like(out_ref)
    self_sum, cross_sum = self_ref[0], cross_ref[0]
    for m in range(1, self_ref.shape[0]):
        self_sum, cross_sum = self_sum + self_ref[m], cross_sum + cross_ref[m]
    own = own_part(core, 0, width)
    out_ref[0:1, own] = self_sum[0:1]
    out_ref[1:2, own] = self_sum[2:3]
    out_ref[3:4, own] = cross_sum[0:1]
    out_ref[4:5, own] = cross_sum[2:3]
    out_ref[2:3, :] = first_ref[0:1]
    out_ref[5:7, :] = mid_ref[0:2]
    out_ref[7:9, :] = first_ref[1:3]
    out_ref[9:13, :] = mid_ref[2:6]
    out_ref[13:17, :] = ff_ref[0:4]
    if tiles_ref is not None:
        lots = tiles_ref.shape[0]
        lot, third = out_ref.shape[1] // lots, tiles_ref.shape[2] // 3
        tiles_ref[...] = jnp.zeros_like(tiles_ref)
        for d in range(lots):
            for n in range(3):
                piece = out_ref[8 * n : 8 * n + 8, d * lot : (d + 1) * lot]
                tiles_ref[d, :, n * third : n * third + lot] = piece.astype(BF)


def vec_rows(core, self_sums, cross_sums, first_sums, mid_sums, ff_sums, devices=None):
    operands = [self_sums, cross_sums, first_sums, mid_sums, ff_sums]
    dim = first_sums.shape[1]
    outs = [shape((24, dim), F32)]
    if devices is not None:
        outs.append(shape((devices, 8, dim // 2), BF))
    return call(
        "vec_rows",
        vec_rows_kernel,
        (1,),
        [whole(o) for o in operands],
        [whole(o) for o in outs],
        outs,
        [core] + operands,
        prefetch=1,
    )


def input_grad_kernel(count, has_start, *refs):
    start = refs[0] if has_start else None
    own, oth, mats_a, mats_b, out = refs[has_start:]
    total = start[...] if has_start else None
    for n in range(count):
        for grads, mats in ((own, mats_a), (oth, mats_b)):
            t = nt(grads[n], mats[n])
            total = t if total is None else total + t
    out[...] = total


def input_grad(own, other, mats_own, mats_other, start, tile):
    count, tokens, half = own.shape
    dim = mats_own.shape[1]
    grads = pl.BlockSpec((count, tile, half), lambda i: (0, i, 0))
    rows = pl.BlockSpec((tile, dim), lambda i: (i, 0))
    has_start = start is not None
    return call(
        "input_grad",
        functools.partial(input_grad_kernel, count, has_start),
        (tokens // tile,),
        ([rows] if has_start else []) + [grads, grads, whole(mats_own), whole(mats_other)],
        [rows],
        [shape((tokens, dim), F32)],
        ([start] if has_start else []) + [own, other, mats_own, mats_other],
        flops=4 * count * tokens * half * dim,
    )[0]


def adam_step(master, first_m, second_m, grad_sum, rate, decay):
    first_new = 0.5 * first_m + 0.5 * grad_sum
    second_new = 0.5 * second_m + 0.5 * grad_sum * grad_sum
    fix_term = 1.0 - 0.5**STEP
    update = first_new / fix_term / (jnp.sqrt(second_new / fix_term) + adam_eps)
    master_new = master - rate * (update + decay * master)
    return (master_new, first_new, second_new, master_new.astype(BF))


def on_device(
    target,
    memory,
    cotangent,
    seg_target,
    seg_memory,
    attn_master,
    attn_first,
    attn_second,
    in_master,
    in_first,
    in_second,
    out_master,
    out_first,
    out_second,
    vec_master,
    vec_first,
    vec_second,
):
    both = ("seq", "fsdp")
    devices = lax.axis_size("seq") * lax.axis_size("fsdp")
    core_at = lax.axis_index("seq") & 1
    core = core_at.astype(jnp.int32).reshape(1)
    is_low = core_at == 0
    place = lax.axis_index("seq") * lax.axis_size("fsdp") + lax.axis_index("fsdp")
    me = place.astype(jnp.int32).reshape(1)
    micro, _, rows, dim = target.shape
    half, hidden = dim // 2, in_master.shape[1]
    tokens = micro * rows
    shard = attn_master.shape[1]
    sets = bit_sets(devices)
    near = flips(sets[0])
    thin = sets[:1] + [[b] for bits in sets[1:] for b in bits]
    chip_bits = [b for bits in sets[::-1] for b in bits[::-1]]
    all_bits = sorted(chip_bits + [1], reverse=True)
    direct = devices == LOTS
    partner = lambda a: moved(a, CORE)

    x_own, m_own = target[:, 0], memory[:, 0]
    seg_own = jnp.concatenate([seg_target[:, 0], seg_memory[:, 0]], axis=0)
    attn_low = attn_master.astype(BF)
    in_low = in_master.astype(BF)
    out_low = out_master.astype(BF)
    vec_low = vec_master.astype(BF)

    def column_halves(mats):
        mine = jnp.where(is_low, mats[:, :, :half], mats[:, :, half:])
        other = partner(jnp.where(is_low, mats[:, :, half:], mats[:, :, :half]))
        return jnp.stack([jnp.where(is_low, mine, other), jnp.where(is_low, other, mine)])

    x_other, seg_other, m_other = partner(x_own), partner(seg_own), partner(m_own)
    if direct:
        halves = column_halves(attn_low[0:7]).reshape(2, 7 * shard, half)
        low_tile = as_tile(vec_low, half)
        far_tile = partner(low_tile)
        tiles = jnp.stack([jnp.where(is_low, low_tile, far_tile), jnp.where(is_low, far_tile, low_tile)])
        ends = (3 * shard, 7 * shard, 7 * shard + 8)
        cuts = list(zip((0,) + ends[:2], ends))
        (self_far, late_far, vec_far), rels = far_parts(jnp.concatenate([halves, tiles], axis=1), sets, cuts)
        feed_low = in_low.reshape(shard, 4, dim).transpose(1, 0, 2).reshape(4 * shard, dim)
        pack = jnp.concatenate([feed_low, out_low, attn_low[7]], axis=0)
        self_far, x_own, m_own, x_other, m_other, seg_other, pack, vec_far = lax.optimization_barrier(
            (self_far, x_own, m_own, x_other, m_other, seg_other, pack, vec_far)
        )
        pack = lax.all_gather(pack, both, axis=0, tiled=False)
        self_parts = near_parts(self_far, sets)
        vec_parts = near_parts(vec_far, sets)
        self_mats = (self_parts, near, rels)
        vec_tiles = assemble(me, vec_parts, near, rels, 8)[0].reshape(devices, 8, half)
        vec_all = from_tile(vec_tiles, vec_low.shape[0], vec_low.shape[1])
        vec_all, x_own, m_own = lax.optimization_barrier((vec_all, x_own, m_own))
        self_parts[1:], late_far = lax.optimization_barrier((self_parts[1:], late_far))
        late_parts = near_parts(late_far, sets)
    else:

        def gather_half(mats):
            stacked = jnp.moveaxis(column_halves(mats), 0, 1)
            return gather_bits(stacked, chip_bits, [1]).reshape(mats.shape[0], dim, half)

        self_mats = gather_half(attn_low[0:3])
        late_mats = gather_half(attn_low[3:7])
        lots = lambda a: a.reshape(LOTS, -1, dim)
        win = lax.all_gather(in_low, both, axis=0, tiled=True)
        pack = jnp.concatenate(
            [lots(win[:, n * dim : (n + 1) * dim]) for n in range(4)]
            + [lots(lax.all_gather(out_low, both, axis=0, tiled=True))]
            + [lots(lax.all_gather(attn_low[7], both, axis=0, tiled=True))],
            axis=1,
        )
        vec_all = gather_bits(vec_low[None], [1] + chip_bits).reshape(devices, *vec_low.shape)
    vec = vec_all.transpose(1, 0, 2).reshape(vec_low.shape[0], dim).astype(F32)

    seg_t, seg_m = (jnp.concatenate([a, b], axis=1) for a, b in zip(
        (seg_own[:micro], seg_own[micro:]), (seg_other[:micro], seg_other[micro:])
    ))
    seg_t_ordered = jnp.where(is_low, seg_t, jnp.concatenate([seg_other[:micro], seg_own[:micro]], axis=1))
    row = lambda a: a[:, None, :]
    own_cols = lambda n: jnp.where(is_low, vec[n, :half], vec[n, half:])
    zeros = jnp.zeros((half,), F32)
    flat = lambda a: a.reshape(-1, a.shape[-1])
    flat3 = lambda a: a.reshape(a.shape[0], tokens, half)
    tall = lambda a: a.reshape(micro, rows, half)
    across = [flat(a).T for a in (x_own, x_other, m_own, m_other)]
    x_own, across = lax.optimization_barrier((x_own, across))

    qkv, self_mats = project(
        core, me, x_own, x_other, self_mats, jnp.stack([own_cols(0), zeros, own_cols(1)])[:, None], 0.125, True
    )
    self_own, self_send, self_exact, self_log = attention(
        True, core, None, (qkv, 1), row(seg_t_ordered), row(seg_t_ordered)
    )
    if direct:
        self_own, late_parts[0] = lax.optimization_barrier((self_own, late_parts[0]))
        late_mats = assemble(me, late_parts, near, rels, shard)
    late_other = partner(late_mats)
    mem_kv, _ = project(
        core, me, m_own, m_other, late_mats[2:4], jnp.stack([zeros, own_cols(4)])[:, None], 1.0, False
    )
    self_other_mats = partner(self_mats)
    mem_kv, late_other, self_other_mats = lax.optimization_barrier((mem_kv, late_other, self_other_mats))
    self_own, self_other = flat(self_own), flat(partner(self_send))
    xhat1, rstd1, first_low, cq_own, cq_send = after_self(
        core, self_own, self_other, flat(x_own), late_mats, late_other, vec, 2 * CHUNK
    )
    cq_own, cq_other = tall(cq_own), tall(partner(cq_send))
    cross_own, cross_send, cross_exact, cross_log = attention(
        False, core, (cq_own, cq_other), (mem_kv, 0), row(seg_t), row(seg_m)
    )
    cross_own, cross_other = flat(cross_own), flat(partner(cross_send))

    (block, act, d_pre, second_low, e3, d_r2, br2, dco_own, dco_send, mid_sums, ff_sums) = middle(
        core, cross_own, cross_other, xhat1, flat(cotangent[:, 0]), pack, vec, 2 * CHUNK
    )
    dco_own, dco_other = tall(dco_own), tall(partner(dco_send))
    feed_in, feed_in_away = feed_in_grads(core, second_low, d_pre)
    feed_out, feed_out_away = feed_out_grads(core, act, e3)
    feed_in_got, feed_out_got = partner(feed_in_away), partner(feed_out_away)
    if direct:
        feed = list(route_feed(me, (feed_in, feed_in_got), (feed_out, feed_out_got), sets[0], devices))
        dco_own, feed[0] = lax.optimization_barrier((dco_own, feed[0]))
        feed_near, _ = reduce_near(me, feed, thin, devices)
    else:
        lot = dim // LOTS
        halves_of = lambda a, b: both_halves(is_low, (a.astype(F32) + b.astype(F32)).astype(BF), partner((a.astype(F32) + b.astype(F32)).astype(BF)))
        win_grad, wout_grad = halves_of(feed_in, feed_in_got), halves_of(feed_out, feed_out_got)
        in_parts = [win_grad[:, n * lot : (n + 1) * lot].reshape(dim, dim) for n in range(4)]
        keep = jnp.where(is_low, 1.0, 0.0).astype(BF)
        sum_in_mat = lax.psum_scatter(keep * jnp.concatenate(in_parts, axis=1), both, scatter_dimension=0, tiled=True)
        sum_out_mat = lax.psum_scatter(keep * wout_grad.reshape(hidden, dim), both, scatter_dimension=0, tiled=True)
    dcq_own, dcq_send, d_mem_own, d_mem_other, cross_sums = attention(
        False,
        core,
        (cq_own, cq_other),
        (mem_kv, 0),
        row(seg_t),
        row(seg_m),
        (dco_own, dco_other, cross_exact, cross_log),
    )
    dcq_own, dcq_other = flat(dcq_own), flat(partner(dcq_send))
    d_r1, br1, dso_own, dso_send, first_sums = before_self(
        core, dcq_own, dcq_other, d_r2, xhat1, rstd1, late_mats, late_other, vec, 2 * CHUNK
    )
    dso_own, dso_other = tall(dso_own), tall(partner(dso_send))
    if direct:
        br1, feed_near = lax.optimization_barrier((br1, feed_near))

    def reduce_whole(mats):
        spread = mats.reshape([mats.shape[0]] + [2] * len(all_bits) + [shard, half])
        summed = scatter_bits(spread, chip_bits[::-1], all_bits)
        mine = jnp.where(is_low, summed[:, 0], summed[:, 1])
        other = partner(jnp.where(is_low, summed[:, 1], summed[:, 0]))
        return both_halves(is_low, mine, other)

    d_mem_own, d_mem_other = flat3(d_mem_own), flat3(d_mem_other)
    grads_mine, grads_away = token_grads(
        core, self_own, self_other, br1, first_low, dcq_own, dcq_other, cross_own, cross_other, br2
    )
    grads_mem = pair_grads(me, across[2], across[3], d_mem_own, d_mem_other)[0]
    grads_got = partner(grads_away)
    d_mem_in = partner(d_mem_other)
    if direct:
        routed = list(route_sums(me, grads_mine, grads_got, grads_mem, sets[0], devices))
        dso_own, routed[0], d_mem_in = lax.optimization_barrier((dso_own, routed[0], d_mem_in))
        cross_near, _ = reduce_near(me, routed, thin, devices)
    else:
        summed = (grads_mine.astype(F32) + grads_got.astype(F32)).astype(BF)
        sum_cross = reduce_whole(jnp.concatenate([summed, grads_mem]))

    d_self_own, d_self_away, self_sums = attention(
        True,
        core,
        None,
        (qkv, 1),
        row(seg_t_ordered),
        row(seg_t_ordered),
        (dso_own, dso_other, self_exact, self_log),
    )
    d_self_own, d_self_away = flat3(d_self_own), flat3(d_self_away)
    grad_m = input_grad(d_mem_own, d_mem_in, late_mats[2:4], late_other[2:4], None, 2 * CHUNK)
    vec_grad = vec_rows(core, self_sums, cross_sums, first_sums, mid_sums, ff_sums, devices if direct else None)
    if direct:
        feed_near, d_self_own = reduce_step(me, feed_near, thin, 1, devices, d_self_own)
        d_self_own, feed_near = lax.optimization_barrier((d_self_own, feed_near))
        routed = list(
            pair_grads(me, across[0], across[1], d_self_own, d_self_away, (sets[0], vec_grad[1]))
        )
        d_self_away, routed, cross_near = lax.optimization_barrier((d_self_away, routed, cross_near))

    d_self_other = partner(d_self_away)
    grad_x = input_grad(d_self_own, d_self_other, self_mats, self_other_mats, d_r1, 2 * CHUNK)
    if direct:
        mine, other, (grad_m, grad_x) = reduce_far(me, cross_near, thin, devices, [grad_m, grad_x])
        self_near, (mine, grad_m, grad_x) = reduce_near(me, routed, sets, devices, (mine, grad_m, grad_x))
        sum_cross = both_halves(is_low, mine, other)
        self_near = list(self_near)
        feed_near, self_near[0] = reduce_step(me, feed_near, thin, 2, devices, self_near[0])
        feed_mine, feed_other = feed_near[0][0], partner(feed_near[1])[0]
        feed_sum = both_halves(is_low, feed_mine, feed_other)
        sum_in_mat = feed_sum[: 4 * shard].reshape(4, shard, dim).transpose(1, 0, 2).reshape(shard, hidden)
        sum_out_mat = feed_sum[4 * shard :]
        mine, other, _ = reduce_far(me, self_near, sets, devices)
        last = 3 * shard
        sum_self = both_halves(is_low, mine[:last], other[:last]).reshape(3, shard, dim)
        tile = mine[last:].astype(F32) + other[last:].astype(F32)
        sum_vec = from_tile(tile, *vec_master.shape)
    else:
        sum_self = reduce_whole(pair_grads(me, across[0], across[1], d_self_own, d_self_away)[0])
        all_rows = vec_grad[0]
        for bit in [1] + chip_bits[::-1]:
            all_rows = all_rows + moved(all_rows, 1 << bit)
        width = vec_master.shape[1]
        sum_vec = lax.dynamic_slice_in_dim(all_rows[: vec_master.shape[0]], place * width, width, axis=1)

    sum_attn = jnp.concatenate(
        [sum_self, sum_cross[0:2], sum_cross[3:5], sum_cross[2:3]], axis=0
    ).astype(F32)
    attn_new, attn_m, attn_s, attn_w = adam_step(attn_master, attn_first, attn_second, sum_attn, 0.1, 0.01)
    in_new, in_m, in_s, in_w = adam_step(in_master, in_first, in_second, sum_in_mat.astype(F32), 0.05, 0.01)
    out_new, out_m, out_s, out_w = adam_step(out_master, out_first, out_second, sum_out_mat.astype(F32), 0.03, 0.01)
    vec_new, vec_m, vec_s, vec_w = adam_step(vec_master, vec_first, vec_second, sum_vec, 0.3, 0.0)
    return (
        block.reshape(micro, 1, rows, dim),
        grad_x.reshape(micro, 1, rows, dim),
        grad_m.reshape(micro, 1, rows, dim),
        attn_new,
        attn_m,
        attn_s,
        attn_w,
        in_new,
        in_m,
        in_s,
        in_w,
        out_new,
        out_m,
        out_s,
        out_w,
        vec_new,
        vec_m,
        vec_s,
        vec_w,
    )


def solution(mesh):
    tokens = P(None, "fsdp", "seq", None)
    marks = P(None, "fsdp", "seq")
    attn = P(None, ("seq", "fsdp"), None)
    feed = P(("seq", "fsdp"), None)
    rows = P(None, ("seq", "fsdp"))
    return jax.shard_map(
        on_device,
        mesh=mesh,
        in_specs=(tokens,) * 3 + (marks,) * 2 + (attn,) * 3 + (feed,) * 6 + (rows,) * 3,
        out_specs=(tokens,) * 3 + (attn,) * 4 + (feed,) * 8 + (rows,) * 4,
        check_vma=False,
    )
```

```python
import functools

import jax
import jax.numpy as jnp
from jax import lax
from jax.experimental import pallas as pl
from jax.experimental.pallas import tpu as pltpu
from jax.sharding import PartitionSpec as P

HDIM = 64
STEP = 10
PAIR = 2 * HDIM
CHUNK = 256
DOCS = 5
MASKED = -1e30
BOUND = 3000.0

BF = jnp.bfloat16
F32 = jnp.float32

norm_eps = 1e-05
adam_eps = 1e-08
MIB = 2**20


def nn(a, b):
    return lax.dot_general(a, b, (((1,), (0,)), ((), ())), preferred_element_type=F32)


def nt(a, b):
    return lax.dot_general(a, b, (((1,), (1,)), ((), ())), preferred_element_type=F32)


def tn(a, b):
    return lax.dot_general(a, b, (((0,), (0,)), ((), ())), preferred_element_type=F32)


def call(name, kernel, grid, in_specs, out_specs, out_shape, operands, scratch=(), flops=0, prefetch=0, room=28, cost=0.01):
    size = cost * sum(leaf.size * leaf.dtype.itemsize for leaf in list(operands) + list(out_shape))
    return pl.pallas_call(
        kernel,
        name=name,
        grid_spec=pltpu.PrefetchScalarGridSpec(
            num_scalar_prefetch=prefetch,
            grid=grid,
            in_specs=in_specs,
            out_specs=out_specs,
            scratch_shapes=scratch,
        ),
        out_shape=out_shape,
        compiler_params=pltpu.CompilerParams(vmem_limit_bytes=room * MIB),
        cost_estimate=pl.CostEstimate(flops=int(cost * flops), bytes_accessed=int(size), transcendentals=0),
    )(*operands)


def shape(dims, dtype):
    return jax.ShapeDtypeStruct(tuple(dims), dtype)


def whole(array):
    zeros = (0,) * array.ndim
    return pl.BlockSpec(array.shape, lambda *_: zeros)


CORE = 2


def moved(array, flip):
    count = lax.axis_size("seq") * lax.axis_size("fsdp")
    return lax.ppermute(array, ("seq", "fsdp"), [(i, i ^ flip) for i in range(count)])


def own_bit(bit):
    if bit == 0:
        return lax.axis_index("fsdp")
    return (lax.axis_index("seq") >> (bit - 1)) & 1


def bit_sets(count):
    bits = [0] + list(range(2, count.bit_length() - 1))
    return [bits[i : i + 2] for i in range(0, len(bits), 2)]


def flips(bits):
    out = [0]
    for bit in bits:
        out = out + [f | 1 << bit for f in out]
    return out


def gather_bits(array, order, present=()):
    present = sorted(present, reverse=True)
    for bit in order:
        other = moved(array, 1 << bit)
        place = 1 + sum(b > bit for b in present)
        low = own_bit(bit) == 0
        array = jnp.stack([jnp.where(low, array, other), jnp.where(low, other, array)], axis=place)
        present = sorted(present + [bit], reverse=True)
    return array


def scatter_bits(array, order, present):
    present = sorted(present, reverse=True)
    for bit in order:
        place = 1 + present.index(bit)
        mine = own_bit(bit)
        send = lax.dynamic_index_in_dim(array, 1 - mine, place, keepdims=False)
        keep = lax.dynamic_index_in_dim(array, mine, place, keepdims=False)
        array = (keep.astype(F32) + moved(send, 1 << bit).astype(F32)).astype(BF)
        present.remove(bit)
    return array


def as_tile(rows, width):
    third = width // 3
    full = jnp.pad(rows, ((0, 24 - rows.shape[0]), (0, third - rows.shape[1])))
    return jnp.concatenate([full[0:8], full[8:16], full[16:24]], axis=1)


def from_tile(tile, count, columns):
    third = tile.shape[-1] // 3
    groups = [tile[..., n * third : n * third + columns] for n in range(3)]
    return jnp.concatenate(groups, axis=-2)[..., :count, :]


def far_parts(stacked, sets, cuts, beside):
    rels, array = [0], stacked[None]
    for bits in sets[:1:-1]:
        rels = [f ^ r for f in flips(bits) for r in rels]
        array = jnp.concatenate([array] + [moved(array, f) for f in flips(bits)[1:]], axis=0)
    got = [array] + [moved(array, f) for f in flips(sets[1])[1:]]
    rels = [f ^ r for f in flips(sets[1]) for r in rels]
    got[1:], beside = lax.optimization_barrier((got[1:], beside))
    many = array.shape[0]

    def join_kernel(*refs):
        ins, outs = refs[: len(got)], refs[len(got) :]
        for out, (a, b) in zip(outs, cuts):
            for n, one in enumerate(ins):
                out[n * many : (n + 1) * many] = one[:, :, a:b]

    outs = [shape((many * len(got), 2, b - a, array.shape[3]), BF) for a, b in cuts]
    joined = call("join", join_kernel, (1,), [whole(one) for one in got], [whole(out) for out in outs], outs, got)
    return joined, rels, beside


def near_parts(array, sets):
    return [array] + [moved(array, f) for f in flips(sets[0])[1:]]


def assemble_kernel(near, rels, me_ref, *refs):
    parts, out = refs[: len(near)], refs[-1]
    for part, f in zip(parts, near):
        for i, r in enumerate(rels):
            for c in range(2):
                out[0, ((me_ref[0] & ~CORE) ^ (f ^ r)) + CORE * c] = part[i, c]


def part_specs(parts, rows):
    return [pl.BlockSpec((p.shape[0], 2, rows, p.shape[3]), lambda i, *_: (0, 0, i, 0)) for p in parts]


def assemble(me, parts, near, rels, rows):
    _, _, total, cols = parts[0].shape
    count = total // rows
    lots = 2 * len(near) * len(rels)
    out = call(
        "assemble",
        functools.partial(assemble_kernel, near, rels),
        (count,),
        part_specs(parts, rows),
        [pl.BlockSpec((1, lots, rows, cols), lambda i, *_: (i, 0, 0, 0))],
        [shape((count, lots, rows, cols), BF)],
        [me] + parts,
        prefetch=1,
    )[0]
    return out.reshape(count, lots * rows, cols)


def compact(number, removed):
    out, place = 0, 0
    for bit in range(number.bit_length()):
        if bit not in removed:
            out |= (number >> bit & 1) << place
            place += 1
    return out


def send_blocks(bits, gone, count, me, load, outs):
    kept = [b for b in range(count.bit_length() - 1) if b not in gone]
    mask = sum(1 << kept.index(b) for b in bits)
    here = 0
    for b in bits:
        here = here + (((me >> b) & 1) << kept.index(b))
    total = 1 << len(kept)
    for f, out in zip(flips(bits), outs):
        small = sum(((f >> b) & 1) << kept.index(b) for b in bits)
        j = 0
        for k in range(total):
            if k & mask == 0:
                out(j, load((here ^ small) + k))
                j += 1


def combine_kernel(bits, gone, count, me_ref, *refs):
    outs = refs[-(1 << len(bits)) :]
    ins = refs[: len(refs) - len(outs)]

    def load(k):
        total = ins[0][k].astype(F32)
        for ref in ins[1:]:
            total = total + ref[k].astype(F32)
        return total.astype(BF)

    def store(out):
        def put(j, value):
            out[j] = value

        return put

    send_blocks(bits, gone, count, me_ref[0], load, [store(out) for out in outs])


def combine(me, arrays, bits, gone, count):
    blocks = arrays[0].shape[0] >> len(bits)
    out = shape((blocks,) + arrays[0].shape[1:], BF)
    return call(
        "combine",
        functools.partial(combine_kernel, bits, gone, count),
        (1,),
        [whole(a) for a in arrays],
        [whole(out)] * (1 << len(bits)),
        [out] * (1 << len(bits)),
        [me] + arrays,
        prefetch=1,
    )


def reduce_near(me, outs, sets, count, beside=None):
    got = [outs[0]] + [moved(out, f) for out, f in zip(outs[1:], flips(sets[0])[1:])]
    if beside is not None:
        got[0], beside = lax.optimization_barrier((got[0], beside))
    return combine(me, got, (sets[1:] + [[1]])[0], sets[0], count), beside


def reduce_step(me, outs, sets, n, count, behind=None):
    got = [outs[0]] + [moved(out, f) for out, f in zip(outs[1:], flips(sets[n])[1:])]
    if behind is not None:
        got, behind = lax.optimization_barrier((got, behind))
    return combine(me, got, (sets + [[1]])[n + 1], sum(sets[: n + 1], []), count), behind


def reduce_far(me, outs, sets, count, beside=()):
    gone, beside = sets[0], list(beside)
    for n, (here, after) in enumerate(zip(sets[1:], sets[2:] + [[1]])):
        gone = gone + here
        got = [outs[0]] + [moved(out, f) for out, f in zip(outs[1:], flips(here)[1:])]
        if n < len(beside):
            got[0], beside[n] = lax.optimization_barrier((got[0], beside[n]))
        outs = combine(me, got, after, gone, count)
    return outs[0][0], moved(outs[1], CORE)[0], beside


def both_halves(is_low, mine, other):
    return jnp.concatenate([jnp.where(is_low, mine, other), jnp.where(is_low, other, mine)], axis=-1)


def with_marks(pair, seg, half, lanes, is_key):
    mark = lanes - (HDIM if half == 0 else 0)
    mine = (lanes < HDIM) if half == 0 else (lanes >= HDIM)
    hit = seg == mark
    if is_key:
        extra = jnp.where(hit, 1.0, 0.0)
    else:
        extra = jnp.where(hit | (mark < 0) | (mark >= DOCS), 0.0, MASKED)
    return jnp.where(mine, pair.astype(F32), extra).astype(BF)


def down(row):
    return jnp.broadcast_to(row, (PAIR, row.shape[1])).T


def causal_tile():
    keys = lax.broadcasted_iota(jnp.int32, (CHUNK, CHUNK), 0)
    places = lax.broadcasted_iota(jnp.int32, (CHUNK, CHUNK), 1)
    return jnp.where(places >= keys, 0.0, MASKED)


def masked_scores(keys, queries, c, causal, tile):
    length = keys.shape[0]
    end = (c + 1) * CHUNK if causal else length
    s = nt(keys[:end], queries[c * CHUNK : (c + 1) * CHUNK])
    if causal:
        last = s[c * CHUNK :] + tile
        s = jnp.concatenate([s[: c * CHUNK], last], axis=0) if c else last
    return s


def halves_in(ref_a, ref_b, core, scratch):
    rows = ref_a.shape[-2]
    if core is None:
        scratch[0:rows, :] = ref_a[...].reshape(rows, PAIR)
        scratch[rows:, :] = ref_b[...].reshape(rows, PAIR)
    else:
        scratch[pl.ds(pl.multiple_of(core * rows, rows), rows), :] = ref_a[...].reshape(rows, PAIR)
        scratch[pl.ds(pl.multiple_of((1 - core) * rows, rows), rows), :] = ref_b[...].reshape(rows, PAIR)


def halves_out(scratch, core, ref_a, ref_b):
    rows = scratch.shape[0] // 2
    if core is None:
        a, b = scratch[0:rows, :], scratch[rows:, :]
    else:
        a = scratch[pl.ds(pl.multiple_of(core * rows, rows), rows), :]
        b = scratch[pl.ds(pl.multiple_of((1 - core) * rows, rows), rows), :]
    ref_a[...] = a.reshape(ref_a.shape)
    ref_b[...] = b.reshape(ref_b.shape)


def head_lanes():
    pick = lax.broadcasted_iota(jnp.int32, (8, PAIR), 1) // HDIM == lax.broadcasted_iota(jnp.int32, (8, PAIR), 0)
    return jnp.where(pick, 1.0, 0.0)


def forward_kernel(causal, core_ref, *refs):
    if causal:
        q_ref, k_ref, v_ref, sq_ref, sk_ref, own_ref, send_ref, exact_ref, log_ref, out_s = refs
        core = core_ref[0]
        q = q_ref[0, 0]
    else:
        qa_ref, qb_ref, k_ref, v_ref, sq_ref, sk_ref, own_ref, send_ref, exact_ref, log_ref, out_s = refs
        core = None
        q = jnp.concatenate([qa_ref[0], qb_ref[0]], axis=0)
    k, v = k_ref[0, 0], v_ref[0, 0]
    sq, sk = down(sq_ref[0]), down(sk_ref[0])
    length = k.shape[0]
    lanes = lax.broadcasted_iota(jnp.int32, (length, PAIR), 1)
    tile = causal_tile() if causal else None
    across = v.astype(F32).T.astype(BF)
    ones = jnp.ones((16, length), BF)
    heads = [
        (
            with_marks(q, sq, half, lanes, False),
            with_marks(k, sk, half, lanes, True),
            jnp.concatenate([across[half * HDIM : (half + 1) * HDIM], ones], axis=0),
        )
        for half in range(2)
    ]
    square = lambda a: jnp.max(nt(head_lanes().astype(BF), (a.astype(F32) * a.astype(F32)).astype(BF)))
    bounded = square(q) * square(k) < BOUND

    def every_chunk(with_top):
        done = {}

        def finish(c, half, s):
            if with_top:
                top = jnp.max(s, axis=0, keepdims=True)
                s = s - top
            p = jnp.exp(s).astype(BF)
            mixed = nn(heads[half][2][:, : s.shape[0]], p)
            total = mixed[HDIM : HDIM + 1]
            log = jnp.log(total)
            done[half] = (mixed[:HDIM] * (1.0 / total), log + top if with_top else log)
            if half == 1:
                cs = slice(c * CHUNK, (c + 1) * CHUNK)
                both = jnp.concatenate([done[0][0], done[1][0]], axis=0).T
                exact_ref[0, cs, :] = both
                out_s[cs, :] = both.astype(BF)
                log_ref[0, 0, 0:1, cs] = done[0][1]
                log_ref[0, 0, 1:2, cs] = done[1][1]

        waiting = None
        for c in reversed(range(length // CHUNK)):
            for half in range(2):
                s = masked_scores(heads[half][1], heads[half][0], c, causal, tile)
                if waiting is not None:
                    finish(*waiting)
                waiting = (c, half, s)
        finish(*waiting)

    @pl.when(bounded)
    def _():
        every_chunk(False)

    @pl.when(jnp.logical_not(bounded))
    def _():
        every_chunk(True)

    halves_out(out_s, core, own_ref, send_ref)


def backward_kernel(causal, core_ref, *refs):
    if causal:
        q_ref, k_ref, v_ref, sq_ref, sk_ref, ga_ref, gb_ref, exact_ref, log_ref = refs[:9]
        own_ref, send_ref, sum_ref, p_s, ds_s, g_s, out_s = refs[9:]
        core = core_ref[0]
        q = q_ref[0, 0]
    else:
        qa_ref, qb_ref, k_ref, v_ref, sq_ref, sk_ref, ga_ref, gb_ref, exact_ref, log_ref = refs[:10]
        own_ref, send_ref, kv_own_ref, kv_oth_ref, sum_ref, p_s, ds_s, g_s, out_s = refs[10:]
        core = None
        q = jnp.concatenate([qa_ref[0], qb_ref[0]], axis=0)
    k, v = k_ref[0, 0], v_ref[0, 0]
    sq, sk = down(sq_ref[0]), down(sk_ref[0])
    length = k.shape[0]
    chunks = length // CHUNK
    halves_in(ga_ref, gb_ref, core, g_s)
    grad = g_s[...]
    lanes = lax.broadcasted_iota(jnp.int32, (length, PAIR), 1)
    tile = causal_tile() if causal else None
    pick = lax.broadcasted_iota(jnp.int32, (8, PAIR), 1) // HDIM == lax.broadcasted_iota(jnp.int32, (8, PAIR), 0)
    delta = lax.dot_general(
        jnp.where(pick, 1.0, 0.0),
        grad.astype(F32) * exact_ref[0],
        (((1,), (1,)), ((), ())),
        precision=lax.Precision.HIGHEST,
        preferred_element_type=F32,
    )
    heads = []
    for half in range(2):
        mine = (lanes < HDIM) if half == 0 else (lanes >= HDIM)
        only = lambda a: jnp.where(mine, a.astype(F32), 0.0)
        heads.append(
            dict(
                q=with_marks(q, sq, half, lanes, False),
                k=with_marks(k, sk, half, lanes, True),
                qm=only(q).astype(BF),
                kt=only(k).T.astype(BF),
                gm=only(grad).astype(BF),
                log=log_ref[0, 0, half : half + 1, :],
                delta=delta[half : half + 1, :],
            )
        )
    dq, dk, dv = {}, {}, {}

    def products(c, half):
        h = heads[half]
        cs = slice(c * CHUNK, (c + 1) * CHUNK)
        s = masked_scores(h["k"], h["q"], c, causal, tile)
        return s, nt(v[: s.shape[0]], h["gm"][cs])

    def finish(c, half, s, dp):
        h = heads[half]
        cs = slice(c * CHUNK, (c + 1) * CHUNK)
        end = s.shape[0]
        p = jnp.exp(s - h["log"][:, cs])
        ds = (p * (dp - h["delta"][:, cs])).astype(BF)
        p_s[half, :end, cs] = p.astype(BF)
        ds_s[half, :end, cs] = ds
        t = nn(h["kt"][:, :end], ds)
        dq[c] = t if half == 0 else dq[c] + t

    def keys_side(kb, half):
        h = heads[half]
        q0 = kb * CHUNK if causal else 0
        ks = slice(kb * CHUNK, (kb + 1) * CHUNK)
        a = nn(p_s[half, ks, q0:], h["gm"][q0:])
        b = nn(ds_s[half, ks, q0:], h["qm"][q0:])
        dv[kb] = a if half == 0 else dv[kb] + a
        dk[kb] = b if half == 0 else dk[kb] + b

    waiting = None
    for half in range(2):
        for c in range(chunks):
            pair = products(c, half)
            if waiting is not None:
                finish(*waiting)
            waiting = (c, half, *pair)
            if half == 1 and c > 0:
                keys_side(c - 1, 0)
    finish(*waiting)
    keys_side(chunks - 1, 0)
    for kb in range(chunks):
        keys_side(kb, 1)

    def put(n, parts):
        low = [part.astype(BF) for part in parts]
        for c in range(chunks):
            out_s[n, c * CHUNK : (c + 1) * CHUNK, :] = low[c]
        return sum(jnp.sum(one.astype(F32), axis=0, keepdims=True) for one in low)

    sum_q = put(0, [dq[c].T.astype(BF).astype(F32) * 0.125 for c in range(chunks)])
    sum_k = put(1, [dk[c] for c in range(chunks)])
    sum_v = put(2, [dv[c] for c in range(chunks)])
    pad = jnp.zeros((5, PAIR), F32)
    sum_ref[0] = jnp.concatenate([sum_q, sum_k, sum_v, pad], axis=0)
    if causal:
        for n in range(3):
            halves_out(out_s.at[n], core, own_ref.at[n], send_ref.at[n])
    else:
        halves_out(out_s.at[0], core, own_ref, send_ref)
        for n in range(2):
            halves_out(out_s.at[1 + n], None, kv_own_ref.at[n], kv_oth_ref.at[n])


def attention(causal, core, queries, keys, seg_q, seg_k, backward=None):
    source, k_at = keys
    _, micro, length, width = source.shape
    pairs = width // PAIR
    part = pl.BlockSpec((1, length // 2, PAIR), lambda i, j, s: (i, 0, j))
    full = pl.BlockSpec((1, length, PAIR), lambda i, j, s: (i, 0, j))
    at = lambda n: pl.BlockSpec((1, 1, length, PAIR), lambda i, j, s: (n, i, 0, j))
    seg = pl.BlockSpec((1, 1, length), lambda i, j, s: (i, 0, 0))
    stat = pl.BlockSpec((1, 1, 8, length), lambda i, j, s: (i, j, 0, 0))
    if causal:
        operands, specs = [source], [at(0)]
    else:
        operands, specs = list(queries), [part, part]
    operands += [source, source, seg_q, seg_k]
    specs += [at(k_at), at(k_at + 1), seg, seg]
    share = 0.625 if causal else 1.0
    unit = 2 * micro * pairs * 2 * length * length * PAIR * share
    half_out = shape((micro, length // 2, width), BF)
    if backward is None:
        return call(
            "attend",
            functools.partial(forward_kernel, causal),
            (micro, pairs),
            specs,
            [part, part, full, stat],
            [half_out, half_out, shape((micro, length, width), F32), shape((micro, pairs, 8, length), F32)],
            [core] + operands,
            scratch=[pltpu.VMEM((length, PAIR), BF)],
            cost=0.1,
            room=20,
            flops=unit * 2,
            prefetch=1,
        )
    operands += list(backward)
    specs += [part, part, full, stat]
    sums = pl.BlockSpec((1, 8, PAIR), lambda i, j, s: (i, 0, j))
    scratch = [
        pltpu.VMEM((2, length, length), BF),
        pltpu.VMEM((2, length, length), BF),
        pltpu.VMEM((length, PAIR), BF),
        pltpu.VMEM((3, length, PAIR), BF),
    ]
    if causal:
        part3 = pl.BlockSpec((3, 1, length // 2, PAIR), lambda i, j, s: (0, i, 0, j))
        outs = [part3, part3, sums]
        shapes = [shape((3, micro, length // 2, width), BF)] * 2
    else:
        part2 = pl.BlockSpec((2, 1, length // 2, PAIR), lambda i, j, s: (0, i, 0, j))
        outs = [part, part, part2, part2, sums]
        shapes = [half_out, half_out] + [shape((2, micro, length // 2, width), BF)] * 2
    return call(
        "attend_back",
        functools.partial(backward_kernel, causal),
        (micro, pairs),
        specs,
        outs,
        shapes + [shape((micro, 8, width), F32)],
        [core] + operands,
        scratch=scratch,
        room=30,
        cost=0.1,
        flops=unit * 5,
        prefetch=1,
    )


def project_kernel(first_scale, ordered, gather, *refs):
    core_ref, refs = refs[0], refs[1:]
    if gather is None:
        a_ref, b_ref, w_ref, bias_ref, out_ref = refs
        mat = w_ref[0]
    else:
        near, rels = gather
        me_ref, a_ref, b_ref = refs[:3]
        parts = refs[3 : 3 + len(near)]
        bias_ref, out_ref, mat_ref = refs[3 + len(near) :]
        assemble_kernel(near, rels, me_ref, *parts, mat_ref)
        mat = mat_ref[0].reshape(a_ref.shape[-1], mat_ref.shape[-1])
    rows = a_ref.shape[1]
    scale = jnp.where(pl.program_id(0) == 0, first_scale, 1.0).astype(F32)
    for m in range(a_ref.shape[0]):
        for slot, ref in enumerate((a_ref, b_ref)):
            low = ((nn(ref[m], mat) + bias_ref[0]) * scale).astype(BF)
            place = (core_ref[0] ^ slot) * rows if ordered else slot * rows
            out_ref[0, m, pl.ds(pl.multiple_of(place, rows), rows), :] = low


def project(core, me, own, other, mats, biases, scale, ordered):
    micro, rows, depth = own.shape
    count, _, width = biases.shape
    tokens = pl.BlockSpec(own.shape, lambda i, *_: (0, 0, 0))
    mat_spec = pl.BlockSpec((1, depth, width), lambda i, *_: (i, 0, 0))
    bias_spec = pl.BlockSpec((1, 1, width), lambda i, *_: (i, 0, 0))
    out_specs = [pl.BlockSpec((1, micro, 2 * rows, width), lambda i, *_: (i, 0, 0, 0))]
    out_shape = [shape((count, micro, 2 * rows, width), BF)]
    flops = 2 * count * micro * 2 * rows * depth * width
    if not isinstance(mats, tuple):
        out = call(
            "project",
            functools.partial(project_kernel, scale, ordered, None),
            (count,),
            [tokens, tokens, mat_spec, bias_spec],
            out_specs,
            out_shape,
            [core, own, other, mats, biases],
            flops=flops,
            prefetch=1,
        )[0]
        return out, mats
    parts, near, rels = mats
    lot = depth // (2 * len(near) * len(rels))
    out, full = call(
        "project",
        functools.partial(project_kernel, scale, ordered, (near, rels)),
        (count,),
        [tokens, tokens] + part_specs(parts, lot) + [bias_spec],
        out_specs + [pl.BlockSpec((1, depth // lot, lot, width), lambda i, *_: (i, 0, 0, 0))],
        out_shape + [shape((count, depth // lot, lot, width), BF)],
        [core, me, own, other] + parts + [biases],
        flops=flops,
        prefetch=2,
    )
    return out, full.reshape(count, depth, width)


def normalise(r):
    mean = jnp.mean(r, axis=-1, keepdims=True)
    centred = r - mean
    rstd = lax.rsqrt(jnp.mean(centred * centred, axis=-1, keepdims=True) + norm_eps)
    return centred * rstd, rstd


def norm_back(dz, xhat, rstd, gain):
    dxhat = dz * gain
    a = jnp.mean(dxhat, axis=-1, keepdims=True)
    b = jnp.mean(dxhat * xhat, axis=-1, keepdims=True)
    return (dxhat - a - xhat * b) * rstd


def col_sum(a):
    return jnp.sum(a.astype(F32), axis=0, keepdims=True)


def own_part(core, swap, width):
    return pl.ds(pl.multiple_of((core ^ swap) * width, width), width)


def join_columns(core, own_ref, oth_ref, scratch):
    width = own_ref.shape[-1]
    scratch[:, own_part(core, 0, width)] = own_ref[...]
    scratch[:, own_part(core, 1, width)] = oth_ref[...]


def after_self_kernel(
    core_ref, own_ref, oth_ref, x_ref, mat_ref, moth_ref, vec_ref, xhat_ref, rstd_ref, low_ref, qa_ref, qb_ref, out_s
):
    core = core_ref[0]
    width = own_ref.shape[1]

    @pl.when(pl.program_id(0) == 0)
    def _():
        join_columns(core, mat_ref.at[0], moth_ref.at[0], out_s)

    parts = [slice(i, i + CHUNK) for i in range(0, own_ref.shape[0], CHUNK)]
    mixed = [
        nn(own_ref[r, :], out_s[own_part(core, 0, width), :]) + nn(oth_ref[r, :], out_s[own_part(core, 1, width), :])
        for r in parts
    ]
    for r, one in zip(parts, mixed):
        xhat, rstd = normalise(x_ref[r, :].astype(F32) + one + vec_ref[2:3])
        xhat_ref[r, :] = xhat
        rstd_ref[r, :] = rstd
        low = (xhat * vec_ref[7:8] + vec_ref[8:9]).astype(BF)
        low_ref[r, :] = low
        qa_ref[r, :] = ((nn(low, mat_ref[1]) + vec_ref[3:4, own_part(core, 0, width)]) * 0.125).astype(BF)
        qb_ref[r, :] = ((nn(low, moth_ref[1]) + vec_ref[3:4, own_part(core, 1, width)]) * 0.125).astype(BF)


def first_two(mats):
    return pl.BlockSpec((2,) + mats.shape[1:], lambda *_: (0, 0, 0))


def after_self(core, own, other, x, mats, mats_other, vec, tile):
    tokens, dim = x.shape
    rows = lambda w: pl.BlockSpec((tile, w), lambda i, s: (i, 0))
    half = dim // 2
    return call(
        "after_self",
        after_self_kernel,
        (tokens // tile,),
        [rows(half), rows(half), rows(dim), first_two(mats), first_two(mats), whole(vec)],
        [rows(dim), rows(1), rows(dim), rows(half), rows(half)],
        [
            shape((tokens, dim), F32),
            shape((tokens, 1), F32),
            shape((tokens, dim), BF),
            shape((tokens, half), BF),
            shape((tokens, half), BF),
        ],
        [core, own, other, x, mats, mats_other, vec],
        scratch=[pltpu.VMEM((dim, dim), BF)],
        flops=4 * tokens * dim * dim,
        prefetch=1,
    )


LOTS = 32


def packed_in(pack_ref, n):
    lots, dim = pack_ref.shape[0], pack_ref.shape[2]
    lot = dim // lots
    return pack_ref[:, n * lot : (n + 1) * lot, :].reshape(dim, dim)


def packed_out(pack_ref, n):
    lots, dim = pack_ref.shape[0], pack_ref.shape[2]
    lot, some = dim // lots, lots // 4
    return pack_ref[n * some : (n + 1) * some, 4 * lot : 8 * lot, :].reshape(dim, dim)


def packed_cross(pack_ref, core, swap):
    lots, dim = pack_ref.shape[0], pack_ref.shape[2]
    lot, some = dim // lots, lots // 2
    return pack_ref[own_part(core, swap, some), 8 * lot : 9 * lot, :].reshape(dim // 2, dim)


def middle_kernel(
    core_ref,
    own_ref,
    oth_ref,
    xhat1_ref,
    cot_ref,
    pack_ref,
    vec_ref,
    block_ref,
    act_ref,
    dpre_ref,
    low2_ref,
    e3_ref,
    dr2_ref,
    br2_ref,
    ga_ref,
    gb_ref,
    vsum_ref,
    fsum_ref,
    slope_s,
):
    core = core_ref[0]
    rows, dim = xhat1_ref.shape
    hidden = act_ref.shape[1]
    parts = [slice(i, i + CHUNK) for i in range(0, rows, CHUNK)]
    jobs = [(i, n) for n in range(hidden // dim) for i in range(len(parts))]
    state = [{} for _ in parts]

    def in_turn(make, use):
        waiting = None
        for job in jobs:
            made = make(*job)
            if waiting is not None:
                use(*waiting)
            waiting = (*job, made)
        use(*waiting)

    for at, r in zip(state, parts):
        first = xhat1_ref[r, :] * vec_ref[7:8] + vec_ref[8:9]
        mixed = nn(own_ref[r, :], packed_cross(pack_ref, core, 0)) + nn(oth_ref[r, :], packed_cross(pack_ref, core, 1))
        at["r2"] = first + mixed + vec_ref[5:6]
    for at, r in zip(state, parts):
        at["xhat2"], at["rstd2"] = normalise(at["r2"])
        second = at["xhat2"] * vec_ref[9:10] + vec_ref[10:11]
        at["low2"] = second.astype(BF)
        low2_ref[r, :] = at["low2"]
        at["r3"] = second + vec_ref[6:7]

    def before_gelu(i, n):
        return nn(state[i]["low2"], packed_in(pack_ref, n)) + vec_ref[13 + n : 14 + n]

    def gelu(i, n, pre):
        r, cs = parts[i], slice(n * dim, (n + 1) * dim)
        phi = 0.5 * (1.0 + lax.erf(pre * 0.7071067811865476))
        act = (pre * phi).astype(BF)
        act_ref[r, cs] = act
        slope_s[r, cs] = phi + pre * (jnp.exp(-0.5 * pre * pre) * 0.3989422804014327)
        state[i]["r3"] = state[i]["r3"] + nn(act, packed_out(pack_ref, n))

    in_turn(before_gelu, gelu)
    for at, r in zip(state, parts):
        xhat3, rstd3 = normalise(at["r3"])
        block_ref[r, :] = xhat3 * vec_ref[11:12] + vec_ref[12:13]
        dz = cot_ref[r, :].astype(F32)
        dr3 = norm_back(dz, xhat3, rstd3, vec_ref[11:12])
        at["e3"] = dr3.astype(BF)
        e3_ref[r, :] = at["e3"]
        at["back"] = dr3
        at["sums"] = [col_sum(at["e3"]), col_sum(dz * xhat3), col_sum(dz)]
        at["ff"] = []

    def act_grad(i, n):
        return nt(state[i]["e3"], packed_out(pack_ref, n))

    def gelu_back(i, n, grad):
        r, cs = parts[i], slice(n * dim, (n + 1) * dim)
        low = (grad * slope_s[r, cs]).astype(BF)
        dpre_ref[r, cs] = low
        state[i]["ff"].append(col_sum(low))
        state[i]["back"] = state[i]["back"] + nt(low, packed_in(pack_ref, n))

    in_turn(act_grad, gelu_back)
    first_step = pl.program_id(0) == 0
    total = jnp.where(first_step, 0.0, vsum_ref[...])
    ff_total = jnp.where(first_step, 0.0, fsum_ref[...])
    for at, r in zip(state, parts):
        back = at["back"]
        dr2 = norm_back(back, at["xhat2"], at["rstd2"], vec_ref[9:10])
        dr2_ref[r, :] = dr2
        br2 = dr2.astype(BF)
        br2_ref[r, :] = br2
        ga_ref[r, :] = nt(br2, packed_cross(pack_ref, core, 0)).astype(BF)
        gb_ref[r, :] = nt(br2, packed_cross(pack_ref, core, 1)).astype(BF)
        e3_sum, gain3, shift3 = at["sums"]
        sums = [col_sum(br2), e3_sum, col_sum(back * at["xhat2"]), col_sum(back), gain3, shift3]
        total = total + jnp.concatenate(sums + [jnp.zeros((2, dim), F32)], axis=0)
        ff_total = ff_total + jnp.concatenate(at["ff"] + [jnp.zeros((8 - len(at["ff"]), dim), F32)], axis=0)
    vsum_ref[...] = total
    fsum_ref[...] = ff_total


def middle(core, own, other, xhat1, cot, pack, vec, tile):
    tokens, dim = xhat1.shape
    hidden = 4 * dim
    half = dim // 2
    rows = lambda w: pl.BlockSpec((tile, w), lambda i, s: (i, 0))
    once = lambda a: pl.BlockSpec(a.shape, lambda *_: (0,) * a.ndim, pipeline_mode=pl.Buffered(1))
    sums = pl.BlockSpec((8, dim), lambda i, s: (0, 0))
    return call(
        "middle",
        middle_kernel,
        (tokens // tile,),
        [rows(half), rows(half), rows(dim), rows(dim), once(pack), once(vec)],
        [
            rows(dim),
            rows(hidden),
            rows(hidden),
            rows(dim),
            rows(dim),
            rows(dim),
            rows(dim),
            rows(half),
            rows(half),
            sums,
            sums,
        ],
        [
            shape((tokens, dim), F32),
            shape((tokens, hidden), BF),
            shape((tokens, hidden), BF),
            shape((tokens, dim), BF),
            shape((tokens, dim), BF),
            shape((tokens, dim), F32),
            shape((tokens, dim), BF),
            shape((tokens, half), BF),
            shape((tokens, half), BF),
            shape((8, dim), F32),
            shape((8, dim), F32),
        ],
        [core, own, other, xhat1, cot, pack, vec],
        scratch=[pltpu.VMEM((tile, hidden), F32)],
        room=60,
        flops=tokens * (4 * dim * dim + 8 * dim * hidden),
        prefetch=1,
    )


def before_self_kernel(
    core_ref,
    own_ref,
    oth_ref,
    dr2_ref,
    xhat_ref,
    rstd_ref,
    mat_ref,
    moth_ref,
    vec_ref,
    dr1_ref,
    br1_ref,
    ga_ref,
    gb_ref,
    vsum_ref,
    out_s,
):
    core = core_ref[0]
    width = own_ref.shape[1]

    @pl.when(pl.program_id(0) == 0)
    def _():
        join_columns(core, mat_ref.at[0], moth_ref.at[0], out_s)

    parts = [slice(i, i + CHUNK) for i in range(0, own_ref.shape[0], CHUNK)]
    grads = [dr2_ref[r, :] + nt(own_ref[r, :], mat_ref[1]) + nt(oth_ref[r, :], moth_ref[1]) for r in parts]
    total = jnp.where(pl.program_id(0) == 0, 0.0, vsum_ref[...])
    zero = jnp.zeros((5, xhat_ref.shape[1]), F32)
    for r, dfirst in zip(parts, grads):
        xhat = xhat_ref[r, :]
        dr1 = norm_back(dfirst, xhat, rstd_ref[r, :], vec_ref[7:8])
        dr1_ref[r, :] = dr1
        br1 = dr1.astype(BF)
        br1_ref[r, :] = br1
        ga_ref[r, :] = nt(br1, out_s[own_part(core, 0, width), :]).astype(BF)
        gb_ref[r, :] = nt(br1, out_s[own_part(core, 1, width), :]).astype(BF)
        total = total + jnp.concatenate([col_sum(br1), col_sum(dfirst * xhat), col_sum(dfirst), zero], axis=0)
    vsum_ref[...] = total


def before_self(core, own, other, dr2, xhat, rstd, mats, mats_other, vec, tile):
    tokens, dim = xhat.shape
    half = dim // 2
    rows = lambda w: pl.BlockSpec((tile, w), lambda i, s: (i, 0))
    return call(
        "before_self",
        before_self_kernel,
        (tokens // tile,),
        [rows(half), rows(half), rows(dim), rows(dim), rows(1), first_two(mats), first_two(mats), whole(vec)],
        [rows(dim), rows(dim), rows(half), rows(half), pl.BlockSpec((8, dim), lambda i, s: (0, 0))],
        [
            shape((tokens, dim), F32),
            shape((tokens, dim), BF),
            shape((tokens, half), BF),
            shape((tokens, half), BF),
            shape((8, dim), F32),
        ],
        [core, own, other, dr2, xhat, rstd, mats, mats_other, vec],
        scratch=[pltpu.VMEM((dim, dim), BF)],
        flops=4 * tokens * dim * dim,
        prefetch=1,
    )


def pair_grads_kernel(route, me_ref, xt_ref, yt_ref, a_ref, b_ref, *refs):
    n = pl.program_id(0)
    total = (nn(xt_ref[...], a_ref[0]) + nn(yt_ref[...], b_ref[0])).astype(BF)
    if route is None:
        refs[0][0] = total
        return
    bits, devices = route
    tile_ref, outs, block_s = refs[0], refs[1:-1], refs[-1]
    block_s[...] = total.reshape(block_s.shape)
    lot = block_s.shape[1]
    rows = pl.ds(pl.multiple_of(n * lot, lot), lot)
    last = outs[0].shape[1] - 8

    def store(out):
        def put(j, value):
            out[j, rows, :] = value

        return put

    def store_tile(out):
        def put(j, value):
            out[j, last:, :] = value

        return put

    send_blocks(bits, [], devices, me_ref[0], lambda k: block_s[k], [store(out) for out in outs])

    @pl.when(n == 0)
    def _():
        send_blocks(bits, [], devices, me_ref[0], lambda k: tile_ref[k], [store_tile(out) for out in outs])


def pair_grads(me, xt, yt, own, other, route=None):
    count, tokens, width = own.shape
    dim = xt.shape[0]
    grads = pl.BlockSpec((1, tokens, width), lambda i, *_: (i, 0, 0))
    operands, specs = [me, xt, yt, own, other], [whole(xt), whole(yt), grads, grads]
    if route is None:
        outs = [pl.BlockSpec((1, dim, width), lambda i, *_: (i, 0, 0))]
        shapes, scratch = [shape((count, dim, width), BF)], []
    else:
        bits, tiles = route
        devices = tiles.shape[0]
        lot, blocks = dim // devices, devices >> len(bits)
        shapes = [shape((blocks, count * lot + 8, width), BF)] * (1 << len(bits))
        outs = [whole(one) for one in shapes]
        scratch = [pltpu.VMEM((devices, lot, width), BF)]
        operands, specs, route = operands + [tiles], specs + [whole(tiles)], (bits, devices)
    return call(
        "pair_grads",
        functools.partial(pair_grads_kernel, route),
        (count,),
        specs,
        outs,
        shapes,
        operands,
        scratch=scratch,
        flops=4 * count * tokens * width * dim,
        prefetch=1,
    )


def route_sums(me, mine, received, plain, bits, count):
    lots = count
    _, dim, width = mine.shape
    lot = dim // lots
    total = mine.shape[0] + plain.shape[0]
    view = lambda a: a.reshape(a.shape[0], lots, lot, width)
    out = shape((lots >> len(bits), total, lot, width), BF)
    operands = [view(mine), view(received), view(plain)]

    def kernel(me_ref, a_ref, b_ref, p_ref, *outs):
        def load(k):
            both = (a_ref[:, k].astype(F32) + b_ref[:, k].astype(F32)).astype(BF)
            return both, p_ref[:, k]

        def store(out):
            def put(j, value):
                out[j, : a_ref.shape[0]] = value[0]
                out[j, a_ref.shape[0] :] = value[1]

            return put

        send_blocks(bits, [], count, me_ref[0], load, [store(o) for o in outs])

    return call(
        "route_sums",
        kernel,
        (1,),
        [whole(o) for o in operands],
        [whole(out)] * (1 << len(bits)),
        [out] * (1 << len(bits)),
        [me] + operands,
        prefetch=1,
    )


def by_rows_grads(core, own, other, grad, mine_ref, away_ref, full_s, n):
    width = own.shape[1]
    full_s[own_part(core, 0, width), :] = tn(own[...], grad[...]).astype(BF)
    full_s[own_part(core, 1, width), :] = tn(other[...], grad[...]).astype(BF)
    mine_ref[n] = full_s[:, own_part(core, 0, width)]
    away_ref[n] = full_s[:, own_part(core, 1, width)]


def output_grads_kernel(core_ref, own_ref, oth_ref, grad_ref, mine_ref, away_ref, full_s):
    by_rows_grads(core_ref[0], own_ref, oth_ref, grad_ref, mine_ref, away_ref, full_s, 0)


def token_grads_kernel(core_ref, so_ref, st_ref, br1_ref, low_ref, qo_ref, qt_ref, mine_ref, away_ref, full_s):
    by_rows_grads(core_ref[0], so_ref, st_ref, br1_ref, mine_ref, away_ref, full_s, 0)
    mine_ref[1] = tn(low_ref[...], qo_ref[...]).astype(BF)
    away_ref[1] = tn(low_ref[...], qt_ref[...]).astype(BF)


def token_grads(name, kernel, core, operands, count):
    tokens, dim = operands[2].shape
    out = shape((count, dim, dim // 2), BF)
    return call(
        name,
        kernel,
        (1,),
        [whole(o) for o in operands],
        [whole(out)] * 2,
        [out] * 2,
        [core] + operands,
        scratch=[pltpu.VMEM((dim, dim), BF)],
        flops=2 * count * tokens * dim * dim,
        prefetch=1,
    )


def feed_in_kernel(core_ref, low_ref, dpre_ref, mine_ref, away_ref, low_s, full_s):
    n = pl.program_id(0)

    @pl.when(n == 0)
    def _():
        low_s[...] = low_ref[...].T

    lots, _, half = mine_ref.shape
    lot = low_s.shape[0] // lots
    full_s[...] = nn(low_s[...], dpre_ref[...]).astype(BF)
    rows = pl.ds(pl.multiple_of(n * lot, lot), lot)
    mine_ref[:, rows, :] = full_s[:, own_part(core_ref[0], 0, half)].reshape(lots, lot, half)
    away_ref[:, rows, :] = full_s[:, own_part(core_ref[0], 1, half)].reshape(lots, lot, half)


def feed_out_kernel(core_ref, act_ref, e3_ref, mine_ref, away_ref, full_s):
    full_s[...] = tn(act_ref[...], e3_ref[...]).astype(BF)
    half = mine_ref.shape[2]
    mine_ref[...] = full_s[:, own_part(core_ref[0], 0, half)].reshape(mine_ref.shape)
    away_ref[...] = full_s[:, own_part(core_ref[0], 1, half)].reshape(away_ref.shape)


def feed_in_grads(core, low2, dpre):
    tokens, dim = low2.shape
    out = shape((LOTS, 4 * dim // LOTS, dim // 2), BF)
    return call(
        "feed_in_grads",
        feed_in_kernel,
        (4,),
        [whole(low2), pl.BlockSpec((tokens, dim), lambda i, s: (0, i))],
        [whole(out)] * 2,
        [out] * 2,
        [core, low2, dpre],
        scratch=[pltpu.VMEM((dim, tokens), BF), pltpu.VMEM((dim, dim), BF)],
        flops=8 * tokens * dim * dim,
        prefetch=1,
    )


def feed_out_grads(core, act, e3):
    tokens, dim = e3.shape
    lots = 4 * dim // LOTS
    out = shape((LOTS, lots, dim // 2), BF)
    return call(
        "feed_out_grads",
        feed_out_kernel,
        (4,),
        [pl.BlockSpec((tokens, dim), lambda i, s: (0, i)), whole(e3)],
        [pl.BlockSpec((LOTS // 4, lots, dim // 2), lambda i, s: (i, 0, 0))] * 2,
        [out] * 2,
        [core, act, e3],
        scratch=[pltpu.VMEM((dim, dim), BF)],
        flops=8 * tokens * dim * dim,
        prefetch=1,
    )


def route_feed(me, first, second, bits, count):
    rows = first[0].shape[1]
    out = shape((count >> len(bits), 2 * rows, first[0].shape[2]), BF)
    operands = list(first) + list(second)

    def kernel(me_ref, a_ref, b_ref, c_ref, d_ref, *outs):
        def load(k):
            one = (a_ref[k].astype(F32) + b_ref[k].astype(F32)).astype(BF)
            return one, (c_ref[k].astype(F32) + d_ref[k].astype(F32)).astype(BF)

        def store(out):
            def put(j, value):
                out[j, :rows] = value[0]
                out[j, rows:] = value[1]

            return put

        send_blocks(bits, [], count, me_ref[0], load, [store(o) for o in outs])

    return call(
        "route_feed",
        kernel,
        (1,),
        [whole(o) for o in operands],
        [whole(out)] * (1 << len(bits)),
        [out] * (1 << len(bits)),
        [me] + operands,
        prefetch=1,
        room=36,
    )


def vec_rows_kernel(core_ref, self_ref, cross_ref, first_ref, mid_ref, ff_ref, out_ref, tiles_ref=None):
    core = core_ref[0]
    width = self_ref.shape[2]
    out_ref[...] = jnp.zeros_like(out_ref)
    self_sum, cross_sum = self_ref[0], cross_ref[0]
    for m in range(1, self_ref.shape[0]):
        self_sum, cross_sum = self_sum + self_ref[m], cross_sum + cross_ref[m]
    own = own_part(core, 0, width)
    out_ref[0:1, own] = self_sum[0:1]
    out_ref[1:2, own] = self_sum[2:3]
    out_ref[3:4, own] = cross_sum[0:1]
    out_ref[4:5, own] = cross_sum[2:3]
    out_ref[2:3, :] = first_ref[0:1]
    out_ref[5:7, :] = mid_ref[0:2]
    out_ref[7:9, :] = first_ref[1:3]
    out_ref[9:13, :] = mid_ref[2:6]
    out_ref[13:17, :] = ff_ref[0:4]
    if tiles_ref is not None:
        lots = tiles_ref.shape[0]
        lot, third = out_ref.shape[1] // lots, tiles_ref.shape[2] // 3
        tiles_ref[...] = jnp.zeros_like(tiles_ref)
        for d in range(lots):
            for n in range(3):
                piece = out_ref[8 * n : 8 * n + 8, d * lot : (d + 1) * lot]
                tiles_ref[d, :, n * third : n * third + lot] = piece.astype(BF)


def vec_rows(core, self_sums, cross_sums, first_sums, mid_sums, ff_sums, devices=None):
    operands = [self_sums, cross_sums, first_sums, mid_sums, ff_sums]
    dim = first_sums.shape[1]
    outs = [shape((24, dim), F32)]
    if devices is not None:
        outs.append(shape((devices, 8, dim // 2), BF))
    return call(
        "vec_rows",
        vec_rows_kernel,
        (1,),
        [whole(o) for o in operands],
        [whole(o) for o in outs],
        outs,
        [core] + operands,
        prefetch=1,
    )


def input_grad_kernel(count, has_start, *refs):
    start = refs[0] if has_start else None
    own, oth, mats_a, mats_b, out = refs[has_start:]
    total = start[...] if has_start else None
    for n in range(count):
        for grads, mats in ((own, mats_a), (oth, mats_b)):
            t = nt(grads[n], mats[n])
            total = t if total is None else total + t
    out[...] = total


def input_grad(own, other, mats_own, mats_other, start, tile):
    count, tokens, half = own.shape
    dim = mats_own.shape[1]
    grads = pl.BlockSpec((count, tile, half), lambda i: (0, i, 0))
    rows = pl.BlockSpec((tile, dim), lambda i: (i, 0))
    has_start = start is not None
    return call(
        "input_grad",
        functools.partial(input_grad_kernel, count, has_start),
        (tokens // tile,),
        ([rows] if has_start else []) + [grads, grads, whole(mats_own), whole(mats_other)],
        [rows],
        [shape((tokens, dim), F32)],
        ([start] if has_start else []) + [own, other, mats_own, mats_other],
        flops=4 * count * tokens * half * dim,
    )[0]


def adam_step(master, first_m, second_m, grad_sum, rate, decay):
    first_new = 0.5 * first_m + 0.5 * grad_sum
    second_new = 0.5 * second_m + 0.5 * grad_sum * grad_sum
    fix_term = 1.0 - 0.5**STEP
    update = first_new / fix_term / (jnp.sqrt(second_new / fix_term) + adam_eps)
    master_new = master - rate * (update + decay * master)
    return (master_new, first_new, second_new, master_new.astype(BF))


def on_device(
    target,
    memory,
    cotangent,
    seg_target,
    seg_memory,
    attn_master,
    attn_first,
    attn_second,
    in_master,
    in_first,
    in_second,
    out_master,
    out_first,
    out_second,
    vec_master,
    vec_first,
    vec_second,
):
    both = ("seq", "fsdp")
    devices = lax.axis_size("seq") * lax.axis_size("fsdp")
    core_at = lax.axis_index("seq") & 1
    core = core_at.astype(jnp.int32).reshape(1)
    is_low = core_at == 0
    place = lax.axis_index("seq") * lax.axis_size("fsdp") + lax.axis_index("fsdp")
    me = place.astype(jnp.int32).reshape(1)
    micro, _, rows, dim = target.shape
    half, hidden = dim // 2, in_master.shape[1]
    tokens = micro * rows
    shard = attn_master.shape[1]
    sets = bit_sets(devices)
    near = flips(sets[0])
    thin = sets[:1] + [[b] for bits in sets[1:] for b in bits]
    chip_bits = [b for bits in sets[::-1] for b in bits[::-1]]
    all_bits = sorted(chip_bits + [1], reverse=True)
    direct = devices == LOTS
    partner = lambda a: moved(a, CORE)
    flat = lambda a: a.reshape(-1, a.shape[-1])

    x_own, m_own = target[:, 0], memory[:, 0]
    seg_own = jnp.concatenate([seg_target[:, 0], seg_memory[:, 0]], axis=0)
    attn_low = attn_master.astype(BF)
    in_low = in_master.astype(BF)
    out_low = out_master.astype(BF)
    vec_low = vec_master.astype(BF)

    def column_halves(mats):
        mine = jnp.where(is_low, mats[:, :, :half], mats[:, :, half:])
        other = partner(jnp.where(is_low, mats[:, :, half:], mats[:, :, :half]))
        return jnp.stack([jnp.where(is_low, mine, other), jnp.where(is_low, other, mine)])

    x_other, seg_other, m_other = partner(x_own), partner(seg_own), partner(m_own)
    if direct:
        halves = column_halves(attn_low[0:7]).reshape(2, 7 * shard, half)
        low_tile = as_tile(vec_low, half)
        far_tile = partner(low_tile)
        tiles = jnp.stack([jnp.where(is_low, low_tile, far_tile), jnp.where(is_low, far_tile, low_tile)])
        ends = (3 * shard, 7 * shard, 7 * shard + 8)
        cuts = list(zip((0,) + ends[:2], ends))
        across = [flat(a).T for a in (x_own, m_own)]
        (self_far, late_far, vec_far), rels, across = far_parts(
            jnp.concatenate([halves, tiles], axis=1), sets, cuts, across
        )
        feed_low = in_low.reshape(shard, 4, dim).transpose(1, 0, 2).reshape(4 * shard, dim)
        pack = jnp.concatenate([feed_low, out_low, attn_low[7]], axis=0)
        self_far, x_own, m_own, x_other, m_other, seg_other, pack, vec_far = lax.optimization_barrier(
            (self_far, x_own, m_own, x_other, m_other, seg_other, pack, vec_far)
        )
        pack = lax.all_gather(pack, both, axis=0, tiled=False)
        self_parts = near_parts(self_far, sets)
        vec_parts = near_parts(vec_far, sets)
        self_mats = (self_parts, near, rels)
        vec_tiles = assemble(me, vec_parts, near, rels, 8)[0].reshape(devices, 8, half)
        vec_all = from_tile(vec_tiles, vec_low.shape[0], vec_low.shape[1])
        vec_all, x_own, m_own = lax.optimization_barrier((vec_all, x_own, m_own))
        self_parts[1:], late_far = lax.optimization_barrier((self_parts[1:], late_far))
        late_parts = near_parts(late_far, sets)
    else:

        def gather_half(mats):
            stacked = jnp.moveaxis(column_halves(mats), 0, 1)
            return gather_bits(stacked, chip_bits, [1]).reshape(mats.shape[0], dim, half)

        self_mats = gather_half(attn_low[0:3])
        late_mats = gather_half(attn_low[3:7])
        lots = lambda a: a.reshape(LOTS, -1, dim)
        win = lax.all_gather(in_low, both, axis=0, tiled=True)
        pack = jnp.concatenate(
            [lots(win[:, n * dim : (n + 1) * dim]) for n in range(4)]
            + [lots(lax.all_gather(out_low, both, axis=0, tiled=True))]
            + [lots(lax.all_gather(attn_low[7], both, axis=0, tiled=True))],
            axis=1,
        )
        vec_all = gather_bits(vec_low[None], [1] + chip_bits).reshape(devices, *vec_low.shape)
    vec = vec_all.transpose(1, 0, 2).reshape(vec_low.shape[0], dim).astype(F32)

    seg_t, seg_m = (jnp.concatenate([a, b], axis=1) for a, b in zip(
        (seg_own[:micro], seg_own[micro:]), (seg_other[:micro], seg_other[micro:])
    ))
    seg_t_ordered = jnp.where(is_low, seg_t, jnp.concatenate([seg_other[:micro], seg_own[:micro]], axis=1))
    row = lambda a: a[:, None, :]
    own_cols = lambda n: jnp.where(is_low, vec[n, :half], vec[n, half:])
    zeros = jnp.zeros((half,), F32)
    flat3 = lambda a: a.reshape(a.shape[0], tokens, half)
    tall = lambda a: a.reshape(micro, rows, half)
    if not direct:
        across = [flat(a).T for a in (x_own, m_own)]
    across = [across[0], flat(x_other).T, across[1], flat(m_other).T]
    x_own, across = lax.optimization_barrier((x_own, across))

    qkv, self_mats = project(
        core, me, x_own, x_other, self_mats, jnp.stack([own_cols(0), zeros, own_cols(1)])[:, None], 0.125, True
    )
    self_own, self_send, self_exact, self_log = attention(
        True, core, None, (qkv, 1), row(seg_t_ordered), row(seg_t_ordered)
    )
    if direct:
        self_own, late_parts[0] = lax.optimization_barrier((self_own, late_parts[0]))
        late_mats = assemble(me, late_parts, near, rels, shard)
    late_other = partner(late_mats)
    mem_kv, _ = project(
        core, me, m_own, m_other, late_mats[2:4], jnp.stack([zeros, own_cols(4)])[:, None], 1.0, False
    )
    self_other_mats = partner(self_mats)
    mem_kv, late_other, self_other_mats = lax.optimization_barrier((mem_kv, late_other, self_other_mats))
    self_own, self_other = flat(self_own), flat(partner(self_send))
    xhat1, rstd1, first_low, cq_own, cq_send = after_self(
        core, self_own, self_other, flat(x_own), late_mats, late_other, vec, 2 * CHUNK
    )
    cq_own, cq_other = tall(cq_own), tall(partner(cq_send))
    cross_own, cross_send, cross_exact, cross_log = attention(
        False, core, (cq_own, cq_other), (mem_kv, 0), row(seg_t), row(seg_m)
    )
    cross_own, cross_other = flat(cross_own), flat(partner(cross_send))

    (block, act, d_pre, second_low, e3, d_r2, br2, dco_own, dco_send, mid_sums, ff_sums) = middle(
        core, cross_own, cross_other, xhat1, flat(cotangent[:, 0]), pack, vec, 2 * CHUNK
    )
    dco_own, dco_other = tall(dco_own), tall(partner(dco_send))
    feed_in, feed_in_away = feed_in_grads(core, second_low, d_pre)
    feed_out, feed_out_away = feed_out_grads(core, act, e3)
    feed_in_got, feed_out_got = partner(feed_in_away), partner(feed_out_away)
    last_mine, last_away = token_grads("output_grads", output_grads_kernel, core, [cross_own, cross_other, br2], 1)
    last_got = partner(last_away)
    if direct:
        feed_in_got, feed_out_got, last_mine = lax.optimization_barrier((feed_in_got, feed_out_got, last_mine))
        feed = list(route_feed(me, (feed_in, feed_in_got), (feed_out, feed_out_got), sets[0], devices))
        dco_own, feed[0] = lax.optimization_barrier((dco_own, feed[0]))
        feed_near, _ = reduce_near(me, feed, thin, devices)
    else:
        lot = dim // LOTS
        halves_of = lambda a, b: both_halves(is_low, (a.astype(F32) + b.astype(F32)).astype(BF), partner((a.astype(F32) + b.astype(F32)).astype(BF)))
        win_grad, wout_grad = halves_of(feed_in, feed_in_got), halves_of(feed_out, feed_out_got)
        in_parts = [win_grad[:, n * lot : (n + 1) * lot].reshape(dim, dim) for n in range(4)]
        keep = jnp.where(is_low, 1.0, 0.0).astype(BF)
        sum_in_mat = lax.psum_scatter(keep * jnp.concatenate(in_parts, axis=1), both, scatter_dimension=0, tiled=True)
        sum_out_mat = lax.psum_scatter(keep * wout_grad.reshape(hidden, dim), both, scatter_dimension=0, tiled=True)
    dcq_own, dcq_send, d_mem_own, d_mem_other, cross_sums = attention(
        False,
        core,
        (cq_own, cq_other),
        (mem_kv, 0),
        row(seg_t),
        row(seg_m),
        (dco_own, dco_other, cross_exact, cross_log),
    )
    dcq_own, dcq_other = flat(dcq_own), flat(partner(dcq_send))
    d_r1, br1, dso_own, dso_send, first_sums = before_self(
        core, dcq_own, dcq_other, d_r2, xhat1, rstd1, late_mats, late_other, vec, 2 * CHUNK
    )
    dso_own, dso_other = tall(dso_own), tall(partner(dso_send))
    if direct:
        br1, feed_near = lax.optimization_barrier((br1, feed_near))

    def reduce_whole(mats):
        spread = mats.reshape([mats.shape[0]] + [2] * len(all_bits) + [shard, half])
        summed = scatter_bits(spread, chip_bits[::-1], all_bits)
        mine = jnp.where(is_low, summed[:, 0], summed[:, 1])
        other = partner(jnp.where(is_low, summed[:, 1], summed[:, 0]))
        return both_halves(is_low, mine, other)

    d_mem_own, d_mem_other = flat3(d_mem_own), flat3(d_mem_other)
    grads_mine, grads_away = token_grads(
        "token_grads", token_grads_kernel, core, [self_own, self_other, br1, first_low, dcq_own, dcq_other], 2
    )
    grads_mine = jnp.concatenate([grads_mine, last_mine])
    grads_mem = pair_grads(me, across[2], across[3], d_mem_own, d_mem_other)[0]
    grads_got = jnp.concatenate([partner(grads_away), last_got])
    d_mem_in = partner(d_mem_other)
    if direct:
        routed = list(route_sums(me, grads_mine, grads_got, grads_mem, sets[0], devices))
        dso_own, routed[0], d_mem_in = lax.optimization_barrier((dso_own, routed[0], d_mem_in))
        cross_near, _ = reduce_near(me, routed, thin, devices)
    else:
        summed = (grads_mine.astype(F32) + grads_got.astype(F32)).astype(BF)
        sum_cross = reduce_whole(jnp.concatenate([summed, grads_mem]))

    d_self_own, d_self_away, self_sums = attention(
        True,
        core,
        None,
        (qkv, 1),
        row(seg_t_ordered),
        row(seg_t_ordered),
        (dso_own, dso_other, self_exact, self_log),
    )
    d_self_own, d_self_away = flat3(d_self_own), flat3(d_self_away)
    grad_m = input_grad(d_mem_own, d_mem_in, late_mats[2:4], late_other[2:4], None, 2 * CHUNK)
    vec_grad = vec_rows(core, self_sums, cross_sums, first_sums, mid_sums, ff_sums, devices if direct else None)
    if direct:
        feed_near, d_self_own = reduce_step(me, feed_near, thin, 1, devices, d_self_own)
        d_self_own, feed_near = lax.optimization_barrier((d_self_own, feed_near))
        routed = list(
            pair_grads(me, across[0], across[1], d_self_own, d_self_away, (sets[0], vec_grad[1]))
        )
        d_self_away, routed, cross_near = lax.optimization_barrier((d_self_away, routed, cross_near))

    d_self_other = partner(d_self_away)
    grad_x = input_grad(d_self_own, d_self_other, self_mats, self_other_mats, d_r1, 2 * CHUNK)
    if direct:
        mine, other, (grad_m, grad_x) = reduce_far(me, cross_near, thin, devices, [grad_m, grad_x])
        self_near, (mine, grad_m, grad_x) = reduce_near(me, routed, sets, devices, (mine, grad_m, grad_x))
        sum_cross = both_halves(is_low, mine, other)
        self_near = list(self_near)
        feed_near, self_near[0] = reduce_step(me, feed_near, thin, 2, devices, self_near[0])
        feed_mine, feed_other = feed_near[0][0], partner(feed_near[1])[0]
        feed_sum = both_halves(is_low, feed_mine, feed_other)
        sum_in_mat = feed_sum[: 4 * shard].reshape(4, shard, dim).transpose(1, 0, 2).reshape(shard, hidden)
        sum_out_mat = feed_sum[4 * shard :]
        mine, other, _ = reduce_far(me, self_near, sets, devices)
        last = 3 * shard
        sum_self = both_halves(is_low, mine[:last], other[:last]).reshape(3, shard, dim)
        tile = mine[last:].astype(F32) + other[last:].astype(F32)
        sum_vec = from_tile(tile, *vec_master.shape)
    else:
        sum_self = reduce_whole(pair_grads(me, across[0], across[1], d_self_own, d_self_away)[0])
        all_rows = vec_grad[0]
        for bit in [1] + chip_bits[::-1]:
            all_rows = all_rows + moved(all_rows, 1 << bit)
        width = vec_master.shape[1]
        sum_vec = lax.dynamic_slice_in_dim(all_rows[: vec_master.shape[0]], place * width, width, axis=1)

    sum_attn = jnp.concatenate(
        [sum_self, sum_cross[0:2], sum_cross[3:5], sum_cross[2:3]], axis=0
    ).astype(F32)
    attn_new, attn_m, attn_s, attn_w = adam_step(attn_master, attn_first, attn_second, sum_attn, 0.1, 0.01)
    in_new, in_m, in_s, in_w = adam_step(in_master, in_first, in_second, sum_in_mat.astype(F32), 0.05, 0.01)
    out_new, out_m, out_s, out_w = adam_step(out_master, out_first, out_second, sum_out_mat.astype(F32), 0.03, 0.01)
    vec_new, vec_m, vec_s, vec_w = adam_step(vec_master, vec_first, vec_second, sum_vec, 0.3, 0.0)
    return (
        block.reshape(micro, 1, rows, dim),
        grad_x.reshape(micro, 1, rows, dim),
        grad_m.reshape(micro, 1, rows, dim),
        attn_new,
        attn_m,
        attn_s,
        attn_w,
        in_new,
        in_m,
        in_s,
        in_w,
        out_new,
        out_m,
        out_s,
        out_w,
        vec_new,
        vec_m,
        vec_s,
        vec_w,
    )


def solution(mesh):
    tokens = P(None, "fsdp", "seq", None)
    marks = P(None, "fsdp", "seq")
    attn = P(None, ("seq", "fsdp"), None)
    feed = P(("seq", "fsdp"), None)
    rows = P(None, ("seq", "fsdp"))
    return jax.shard_map(
        on_device,
        mesh=mesh,
        in_specs=(tokens,) * 3 + (marks,) * 2 + (attn,) * 3 + (feed,) * 6 + (rows,) * 3,
        out_specs=(tokens,) * 3 + (attn,) * 4 + (feed,) * 8 + (rows,) * 4,
        check_vma=False,
    )
```

```python
import functools

import jax
import jax.numpy as jnp
from jax import lax
from jax.experimental import pallas as pl
from jax.experimental.pallas import tpu as pltpu
from jax.sharding import PartitionSpec as P

HDIM = 64
STEP = 10
PAIR = 2 * HDIM
CHUNK = 256
DOCS = 5
MASKED = -1e30
BOUND = 3000.0

BF = jnp.bfloat16
F32 = jnp.float32

norm_eps = 1e-05
adam_eps = 1e-08
MIB = 2**20


def nn(a, b):
    return lax.dot_general(a, b, (((1,), (0,)), ((), ())), preferred_element_type=F32)


def nt(a, b):
    return lax.dot_general(a, b, (((1,), (1,)), ((), ())), preferred_element_type=F32)


def tn(a, b):
    return lax.dot_general(a, b, (((0,), (0,)), ((), ())), preferred_element_type=F32)


def call(name, kernel, grid, in_specs, out_specs, out_shape, operands, scratch=(), flops=0, prefetch=0, room=24, cost=0.01):
    size = cost * sum(leaf.size * leaf.dtype.itemsize for leaf in list(operands) + list(out_shape))
    return pl.pallas_call(
        kernel,
        name=name,
        grid_spec=pltpu.PrefetchScalarGridSpec(
            num_scalar_prefetch=prefetch,
            grid=grid,
            in_specs=in_specs,
            out_specs=out_specs,
            scratch_shapes=scratch,
        ),
        out_shape=out_shape,
        compiler_params=pltpu.CompilerParams(vmem_limit_bytes=room * MIB),
        cost_estimate=pl.CostEstimate(flops=int(cost * flops), bytes_accessed=int(size), transcendentals=0),
    )(*operands)


def shape(dims, dtype):
    return jax.ShapeDtypeStruct(tuple(dims), dtype)


def whole(array):
    zeros = (0,) * array.ndim
    return pl.BlockSpec(array.shape, lambda *_: zeros)


CORE = 2


def moved(array, flip):
    count = lax.axis_size("seq") * lax.axis_size("fsdp")
    return lax.ppermute(array, ("seq", "fsdp"), [(i, i ^ flip) for i in range(count)])


def own_bit(bit):
    if bit == 0:
        return lax.axis_index("fsdp")
    return (lax.axis_index("seq") >> (bit - 1)) & 1


def bit_sets(count):
    bits = [0] + list(range(2, count.bit_length() - 1))
    return [bits[i : i + 2] for i in range(0, len(bits), 2)]


def flips(bits):
    out = [0]
    for bit in bits:
        out = out + [f | 1 << bit for f in out]
    return out


def gather_bits(array, order, present=()):
    present = sorted(present, reverse=True)
    for bit in order:
        other = moved(array, 1 << bit)
        place = 1 + sum(b > bit for b in present)
        low = own_bit(bit) == 0
        array = jnp.stack([jnp.where(low, array, other), jnp.where(low, other, array)], axis=place)
        present = sorted(present + [bit], reverse=True)
    return array


def scatter_bits(array, order, present):
    present = sorted(present, reverse=True)
    for bit in order:
        place = 1 + present.index(bit)
        mine = own_bit(bit)
        send = lax.dynamic_index_in_dim(array, 1 - mine, place, keepdims=False)
        keep = lax.dynamic_index_in_dim(array, mine, place, keepdims=False)
        array = (keep.astype(F32) + moved(send, 1 << bit).astype(F32)).astype(BF)
        present.remove(bit)
    return array


def as_tile(rows, width):
    third = width // 3
    full = jnp.pad(rows, ((0, 24 - rows.shape[0]), (0, third - rows.shape[1])))
    return jnp.concatenate([full[0:8], full[8:16], full[16:24]], axis=1)


def from_tile(tile, count, columns):
    third = tile.shape[-1] // 3
    groups = [tile[..., n * third : n * third + columns] for n in range(3)]
    return jnp.concatenate(groups, axis=-2)[..., :count, :]


def far_parts(stacked, sets, cuts, beside):
    rels, array = [0], stacked[None]
    for bits in sets[:1:-1]:
        rels = [f ^ r for f in flips(bits) for r in rels]
        array = jnp.concatenate([array] + [moved(array, f) for f in flips(bits)[1:]], axis=0)
    got = [array] + [moved(array, f) for f in flips(sets[1])[1:]]
    rels = [f ^ r for f in flips(sets[1]) for r in rels]
    got[1:], beside = lax.optimization_barrier((got[1:], beside))
    many = array.shape[0]

    def join_kernel(*refs):
        ins, outs = refs[: len(got)], refs[len(got) :]
        for out, (a, b) in zip(outs, cuts):
            for n, one in enumerate(ins):
                out[n * many : (n + 1) * many] = one[:, :, a:b]

    outs = [shape((many * len(got), 2, b - a, array.shape[3]), BF) for a, b in cuts]
    joined = call("join", join_kernel, (1,), [whole(one) for one in got], [whole(out) for out in outs], outs, got)
    return joined, rels, beside


def near_parts(array, sets):
    return [array] + [moved(array, f) for f in flips(sets[0])[1:]]


def assemble_kernel(near, rels, me_ref, *refs):
    parts, out = refs[: len(near)], refs[-1]
    for part, f in zip(parts, near):
        for i, r in enumerate(rels):
            for c in range(2):
                out[0, ((me_ref[0] & ~CORE) ^ (f ^ r)) + CORE * c] = part[i, c]


def part_specs(parts, rows):
    return [pl.BlockSpec((p.shape[0], 2, rows, p.shape[3]), lambda i, *_: (0, 0, i, 0)) for p in parts]


def assemble(me, parts, near, rels, rows):
    _, _, total, cols = parts[0].shape
    count = total // rows
    lots = 2 * len(near) * len(rels)
    out = call(
        "assemble",
        functools.partial(assemble_kernel, near, rels),
        (count,),
        part_specs(parts, rows),
        [pl.BlockSpec((1, lots, rows, cols), lambda i, *_: (i, 0, 0, 0))],
        [shape((count, lots, rows, cols), BF)],
        [me] + parts,
        prefetch=1,
    )[0]
    return out.reshape(count, lots * rows, cols)


def compact(number, removed):
    out, place = 0, 0
    for bit in range(number.bit_length()):
        if bit not in removed:
            out |= (number >> bit & 1) << place
            place += 1
    return out


def send_blocks(bits, gone, count, me, load, outs):
    kept = [b for b in range(count.bit_length() - 1) if b not in gone]
    mask = sum(1 << kept.index(b) for b in bits)
    here = 0
    for b in bits:
        here = here + (((me >> b) & 1) << kept.index(b))
    total = 1 << len(kept)
    for f, out in zip(flips(bits), outs):
        small = sum(((f >> b) & 1) << kept.index(b) for b in bits)
        j = 0
        for k in range(total):
            if k & mask == 0:
                out(j, load((here ^ small) + k))
                j += 1


def combine_kernel(bits, gone, count, me_ref, *refs):
    outs = refs[-(1 << len(bits)) :]
    ins = refs[: len(refs) - len(outs)]

    def load(k):
        total = ins[0][k].astype(F32)
        for ref in ins[1:]:
            total = total + ref[k].astype(F32)
        return total.astype(BF)

    def store(out):
        def put(j, value):
            out[j] = value

        return put

    send_blocks(bits, gone, count, me_ref[0], load, [store(out) for out in outs])


def combine(me, arrays, bits, gone, count):
    blocks = arrays[0].shape[0] >> len(bits)
    out = shape((blocks,) + arrays[0].shape[1:], BF)
    return call(
        "combine",
        functools.partial(combine_kernel, bits, gone, count),
        (1,),
        [whole(a) for a in arrays],
        [whole(out)] * (1 << len(bits)),
        [out] * (1 << len(bits)),
        [me] + arrays,
        prefetch=1,
    )


def reduce_near(me, outs, sets, count, beside=None):
    got = [outs[0]] + [moved(out, f) for out, f in zip(outs[1:], flips(sets[0])[1:])]
    if beside is not None:
        got[0], beside = lax.optimization_barrier((got[0], beside))
    return combine(me, got, (sets[1:] + [[1]])[0], sets[0], count), beside


def reduce_step(me, outs, sets, n, count, behind=None):
    got = [outs[0]] + [moved(out, f) for out, f in zip(outs[1:], flips(sets[n])[1:])]
    if behind is not None:
        got, behind = lax.optimization_barrier((got, behind))
    return combine(me, got, (sets + [[1]])[n + 1], sum(sets[: n + 1], []), count), behind


def reduce_far(me, outs, sets, count, beside=()):
    gone, beside = sets[0], list(beside)
    for n, (here, after) in enumerate(zip(sets[1:], sets[2:] + [[1]])):
        gone = gone + here
        got = [outs[0]] + [moved(out, f) for out, f in zip(outs[1:], flips(here)[1:])]
        if n < len(beside):
            got[0], beside[n] = lax.optimization_barrier((got[0], beside[n]))
        outs = combine(me, got, after, gone, count)
    return outs[0][0], moved(outs[1], CORE)[0], beside


def both_halves(is_low, mine, other):
    return jnp.concatenate([jnp.where(is_low, mine, other), jnp.where(is_low, other, mine)], axis=-1)


def with_marks(pair, seg, half, lanes, is_key):
    mark = lanes - (HDIM if half == 0 else 0)
    mine = (lanes < HDIM) if half == 0 else (lanes >= HDIM)
    hit = seg == mark
    if is_key:
        extra = jnp.where(hit, 1.0, 0.0)
    else:
        extra = jnp.where(hit | (mark < 0) | (mark >= DOCS), 0.0, MASKED)
    return jnp.where(mine, pair.astype(F32), extra).astype(BF)


def down(row):
    return jnp.broadcast_to(row, (PAIR, row.shape[1])).T


def causal_tile():
    keys = lax.broadcasted_iota(jnp.int32, (CHUNK, CHUNK), 0)
    places = lax.broadcasted_iota(jnp.int32, (CHUNK, CHUNK), 1)
    return jnp.where(places >= keys, 0.0, MASKED)


def masked_scores(keys, queries, c, causal, tile):
    length = keys.shape[0]
    end = (c + 1) * CHUNK if causal else length
    s = nt(keys[:end], queries[c * CHUNK : (c + 1) * CHUNK])
    if causal:
        last = s[c * CHUNK :] + tile
        s = jnp.concatenate([s[: c * CHUNK], last], axis=0) if c else last
    return s


def halves_in(ref_a, ref_b, core, scratch):
    rows = ref_a.shape[-2]
    if core is None:
        scratch[0:rows, :] = ref_a[...].reshape(rows, PAIR)
        scratch[rows:, :] = ref_b[...].reshape(rows, PAIR)
    else:
        scratch[pl.ds(pl.multiple_of(core * rows, rows), rows), :] = ref_a[...].reshape(rows, PAIR)
        scratch[pl.ds(pl.multiple_of((1 - core) * rows, rows), rows), :] = ref_b[...].reshape(rows, PAIR)


def halves_out(scratch, core, ref_a, ref_b):
    rows = scratch.shape[0] // 2
    if core is None:
        a, b = scratch[0:rows, :], scratch[rows:, :]
    else:
        a = scratch[pl.ds(pl.multiple_of(core * rows, rows), rows), :]
        b = scratch[pl.ds(pl.multiple_of((1 - core) * rows, rows), rows), :]
    ref_a[...] = a.reshape(ref_a.shape)
    ref_b[...] = b.reshape(ref_b.shape)


def head_lanes():
    pick = lax.broadcasted_iota(jnp.int32, (8, PAIR), 1) // HDIM == lax.broadcasted_iota(jnp.int32, (8, PAIR), 0)
    return jnp.where(pick, 1.0, 0.0)


def forward_kernel(causal, core_ref, *refs):
    if causal:
        q_ref, k_ref, v_ref, sq_ref, sk_ref, own_ref, send_ref, exact_ref, log_ref, out_s = refs
        core = core_ref[0]
        q = q_ref[0, 0]
    else:
        qa_ref, qb_ref, k_ref, v_ref, sq_ref, sk_ref, own_ref, send_ref, exact_ref, log_ref, out_s = refs
        core = None
        q = jnp.concatenate([qa_ref[0], qb_ref[0]], axis=0)
    k, v = k_ref[0, 0], v_ref[0, 0]
    sq, sk = down(sq_ref[0]), down(sk_ref[0])
    length = k.shape[0]
    lanes = lax.broadcasted_iota(jnp.int32, (length, PAIR), 1)
    tile = causal_tile() if causal else None
    across = v.astype(F32).T.astype(BF)
    ones = jnp.ones((16, length), BF)
    heads = [
        (
            with_marks(q, sq, half, lanes, False),
            with_marks(k, sk, half, lanes, True),
            jnp.concatenate([across[half * HDIM : (half + 1) * HDIM], ones], axis=0),
        )
        for half in range(2)
    ]
    square = lambda a: jnp.max(nt(head_lanes().astype(BF), (a.astype(F32) * a.astype(F32)).astype(BF)))
    bounded = square(q) * square(k) < BOUND

    def every_chunk(with_top):
        done = {}

        def finish(c, half, s):
            if with_top:
                top = jnp.max(s, axis=0, keepdims=True)
                s = s - top
            p = jnp.exp(s).astype(BF)
            mixed = nn(heads[half][2][:, : s.shape[0]], p)
            total = mixed[HDIM : HDIM + 1]
            log = jnp.log(total)
            done[half] = (mixed[:HDIM] * (1.0 / total), log + top if with_top else log)
            if half == 1:
                cs = slice(c * CHUNK, (c + 1) * CHUNK)
                both = jnp.concatenate([done[0][0], done[1][0]], axis=0).T
                exact_ref[0, cs, :] = both
                out_s[cs, :] = both.astype(BF)
                log_ref[0, 0, 0:1, cs] = done[0][1]
                log_ref[0, 0, 1:2, cs] = done[1][1]

        waiting = None
        for c in reversed(range(length // CHUNK)):
            for half in range(2):
                s = masked_scores(heads[half][1], heads[half][0], c, causal, tile)
                if waiting is not None:
                    finish(*waiting)
                waiting = (c, half, s)
        finish(*waiting)

    @pl.when(bounded)
    def _():
        every_chunk(False)

    @pl.when(jnp.logical_not(bounded))
    def _():
        every_chunk(True)

    halves_out(out_s, core, own_ref, send_ref)


def backward_kernel(causal, core_ref, *refs):
    if causal:
        q_ref, k_ref, v_ref, sq_ref, sk_ref, ga_ref, gb_ref, exact_ref, log_ref = refs[:9]
        own_ref, send_ref, sum_ref, p_s, ds_s, g_s, out_s = refs[9:]
        core = core_ref[0]
        q = q_ref[0, 0]
    else:
        qa_ref, qb_ref, k_ref, v_ref, sq_ref, sk_ref, ga_ref, gb_ref, exact_ref, log_ref = refs[:10]
        own_ref, send_ref, kv_own_ref, kv_oth_ref, sum_ref, p_s, ds_s, g_s, out_s = refs[10:]
        core = None
        q = jnp.concatenate([qa_ref[0], qb_ref[0]], axis=0)
    k, v = k_ref[0, 0], v_ref[0, 0]
    sq, sk = down(sq_ref[0]), down(sk_ref[0])
    length = k.shape[0]
    chunks = length // CHUNK
    halves_in(ga_ref, gb_ref, core, g_s)
    grad = g_s[...]
    lanes = lax.broadcasted_iota(jnp.int32, (length, PAIR), 1)
    tile = causal_tile() if causal else None
    pick = lax.broadcasted_iota(jnp.int32, (8, PAIR), 1) // HDIM == lax.broadcasted_iota(jnp.int32, (8, PAIR), 0)
    delta = lax.dot_general(
        jnp.where(pick, 1.0, 0.0),
        grad.astype(F32) * exact_ref[0],
        (((1,), (1,)), ((), ())),
        precision=lax.Precision.HIGHEST,
        preferred_element_type=F32,
    )
    heads = []
    for half in range(2):
        mine = (lanes < HDIM) if half == 0 else (lanes >= HDIM)
        only = lambda a: jnp.where(mine, a.astype(F32), 0.0)
        heads.append(
            dict(
                q=with_marks(q, sq, half, lanes, False),
                k=with_marks(k, sk, half, lanes, True),
                qm=only(q).astype(BF),
                kt=only(k).T.astype(BF),
                gm=only(grad).astype(BF),
                log=log_ref[0, 0, half : half + 1, :],
                delta=delta[half : half + 1, :],
            )
        )
    dq, dk, dv = {}, {}, {}

    def products(c, half):
        h = heads[half]
        cs = slice(c * CHUNK, (c + 1) * CHUNK)
        s = masked_scores(h["k"], h["q"], c, causal, tile)
        return s, nt(v[: s.shape[0]], h["gm"][cs])

    def finish(c, half, s, dp):
        h = heads[half]
        cs = slice(c * CHUNK, (c + 1) * CHUNK)
        end = s.shape[0]
        p = jnp.exp(s - h["log"][:, cs])
        ds = (p * (dp - h["delta"][:, cs])).astype(BF)
        p_s[half, :end, cs] = p.astype(BF)
        ds_s[half, :end, cs] = ds
        t = nn(h["kt"][:, :end], ds)
        dq[c] = t if half == 0 else dq[c] + t

    def keys_side(kb, half):
        h = heads[half]
        q0 = kb * CHUNK if causal else 0
        ks = slice(kb * CHUNK, (kb + 1) * CHUNK)
        a = nn(p_s[half, ks, q0:], h["gm"][q0:])
        b = nn(ds_s[half, ks, q0:], h["qm"][q0:])
        dv[kb] = a if half == 0 else dv[kb] + a
        dk[kb] = b if half == 0 else dk[kb] + b

    waiting = None
    for half in range(2):
        for c in range(chunks):
            pair = products(c, half)
            if waiting is not None:
                finish(*waiting)
            waiting = (c, half, *pair)
            if half == 1 and c > 0:
                keys_side(c - 1, 0)
    finish(*waiting)
    keys_side(chunks - 1, 0)
    for kb in range(chunks):
        keys_side(kb, 1)

    def put(n, parts):
        low = [part.astype(BF) for part in parts]
        for c in range(chunks):
            out_s[n, c * CHUNK : (c + 1) * CHUNK, :] = low[c]
        return sum(jnp.sum(one.astype(F32), axis=0, keepdims=True) for one in low)

    sum_q = put(0, [dq[c].T.astype(BF).astype(F32) * 0.125 for c in range(chunks)])
    sum_k = put(1, [dk[c] for c in range(chunks)])
    sum_v = put(2, [dv[c] for c in range(chunks)])
    pad = jnp.zeros((5, PAIR), F32)
    sum_ref[0] = jnp.concatenate([sum_q, sum_k, sum_v, pad], axis=0)
    if causal:
        for n in range(3):
            halves_out(out_s.at[n], core, own_ref.at[n], send_ref.at[n])
    else:
        halves_out(out_s.at[0], core, own_ref, send_ref)
        for n in range(2):
            halves_out(out_s.at[1 + n], None, kv_own_ref.at[n], kv_oth_ref.at[n])


def attention(causal, core, queries, keys, seg_q, seg_k, backward=None):
    source, k_at = keys
    _, micro, length, width = source.shape
    pairs = width // PAIR
    part = pl.BlockSpec((1, length // 2, PAIR), lambda i, j, s: (i, 0, j))
    full = pl.BlockSpec((1, length, PAIR), lambda i, j, s: (i, 0, j))
    at = lambda n: pl.BlockSpec((1, 1, length, PAIR), lambda i, j, s: (n, i, 0, j))
    seg = pl.BlockSpec((1, 1, length), lambda i, j, s: (i, 0, 0))
    stat = pl.BlockSpec((1, 1, 8, length), lambda i, j, s: (i, j, 0, 0))
    if causal:
        operands, specs = [source], [at(0)]
    else:
        operands, specs = list(queries), [part, part]
    operands += [source, source, seg_q, seg_k]
    specs += [at(k_at), at(k_at + 1), seg, seg]
    share = 0.625 if causal else 1.0
    unit = 2 * micro * pairs * 2 * length * length * PAIR * share
    half_out = shape((micro, length // 2, width), BF)
    if backward is None:
        return call(
            "attend",
            functools.partial(forward_kernel, causal),
            (micro, pairs),
            specs,
            [part, part, full, stat],
            [half_out, half_out, shape((micro, length, width), F32), shape((micro, pairs, 8, length), F32)],
            [core] + operands,
            scratch=[pltpu.VMEM((length, PAIR), BF)],
            cost=0.1,
            room=20,
            flops=unit * 2,
            prefetch=1,
        )
    operands += list(backward)
    specs += [part, part, full, stat]
    sums = pl.BlockSpec((1, 8, PAIR), lambda i, j, s: (i, 0, j))
    scratch = [
        pltpu.VMEM((2, length, length), BF),
        pltpu.VMEM((2, length, length), BF),
        pltpu.VMEM((length, PAIR), BF),
        pltpu.VMEM((3, length, PAIR), BF),
    ]
    if causal:
        part3 = pl.BlockSpec((3, 1, length // 2, PAIR), lambda i, j, s: (0, i, 0, j))
        outs = [part3, part3, sums]
        shapes = [shape((3, micro, length // 2, width), BF)] * 2
    else:
        part2 = pl.BlockSpec((2, 1, length // 2, PAIR), lambda i, j, s: (0, i, 0, j))
        outs = [part, part, part2, part2, sums]
        shapes = [half_out, half_out] + [shape((2, micro, length // 2, width), BF)] * 2
    return call(
        "attend_back",
        functools.partial(backward_kernel, causal),
        (micro, pairs),
        specs,
        outs,
        shapes + [shape((micro, 8, width), F32)],
        [core] + operands,
        scratch=scratch,
        room=30,
        cost=0.1,
        flops=unit * 5,
        prefetch=1,
    )


def project_kernel(first_scale, ordered, gather, *refs):
    core_ref, refs = refs[0], refs[1:]
    if gather is None:
        a_ref, b_ref, w_ref, bias_ref, out_ref = refs
        mat = w_ref[0]
    else:
        near, rels = gather
        me_ref, a_ref, b_ref = refs[:3]
        parts = refs[3 : 3 + len(near)]
        bias_ref, out_ref, mat_ref = refs[3 + len(near) :]
        assemble_kernel(near, rels, me_ref, *parts, mat_ref)
        mat = mat_ref[0].reshape(a_ref.shape[-1], mat_ref.shape[-1])
    rows = a_ref.shape[1]
    scale = jnp.where(pl.program_id(0) == 0, first_scale, 1.0).astype(F32)
    for m in range(a_ref.shape[0]):
        for slot, ref in enumerate((a_ref, b_ref)):
            low = ((nn(ref[m], mat) + bias_ref[0]) * scale).astype(BF)
            place = (core_ref[0] ^ slot) * rows if ordered else slot * rows
            out_ref[0, m, pl.ds(pl.multiple_of(place, rows), rows), :] = low


def project(core, me, own, other, mats, biases, scale, ordered):
    micro, rows, depth = own.shape
    count, _, width = biases.shape
    tokens = pl.BlockSpec(own.shape, lambda i, *_: (0, 0, 0))
    mat_spec = pl.BlockSpec((1, depth, width), lambda i, *_: (i, 0, 0))
    bias_spec = pl.BlockSpec((1, 1, width), lambda i, *_: (i, 0, 0))
    out_specs = [pl.BlockSpec((1, micro, 2 * rows, width), lambda i, *_: (i, 0, 0, 0))]
    out_shape = [shape((count, micro, 2 * rows, width), BF)]
    flops = 2 * count * micro * 2 * rows * depth * width
    if not isinstance(mats, tuple):
        out = call(
            "project",
            functools.partial(project_kernel, scale, ordered, None),
            (count,),
            [tokens, tokens, mat_spec, bias_spec],
            out_specs,
            out_shape,
            [core, own, other, mats, biases],
            flops=flops,
            prefetch=1,
        )[0]
        return out, mats
    parts, near, rels = mats
    lot = depth // (2 * len(near) * len(rels))
    out, full = call(
        "project",
        functools.partial(project_kernel, scale, ordered, (near, rels)),
        (count,),
        [tokens, tokens] + part_specs(parts, lot) + [bias_spec],
        out_specs + [pl.BlockSpec((1, depth // lot, lot, width), lambda i, *_: (i, 0, 0, 0))],
        out_shape + [shape((count, depth // lot, lot, width), BF)],
        [core, me, own, other] + parts + [biases],
        flops=flops,
        prefetch=2,
    )
    return out, full.reshape(count, depth, width)


def normalise(r):
    mean = jnp.mean(r, axis=-1, keepdims=True)
    centred = r - mean
    rstd = lax.rsqrt(jnp.mean(centred * centred, axis=-1, keepdims=True) + norm_eps)
    return centred * rstd, rstd


def norm_back(dz, xhat, rstd, gain):
    dxhat = dz * gain
    a = jnp.mean(dxhat, axis=-1, keepdims=True)
    b = jnp.mean(dxhat * xhat, axis=-1, keepdims=True)
    return (dxhat - a - xhat * b) * rstd


def col_sum(a):
    return jnp.sum(a.astype(F32), axis=0, keepdims=True)


def own_part(core, swap, width):
    return pl.ds(pl.multiple_of((core ^ swap) * width, width), width)


def join_columns(core, own_ref, oth_ref, scratch):
    width = own_ref.shape[-1]
    scratch[:, own_part(core, 0, width)] = own_ref[...]
    scratch[:, own_part(core, 1, width)] = oth_ref[...]


def after_self_kernel(
    core_ref, own_ref, oth_ref, x_ref, mat_ref, moth_ref, vec_ref, xhat_ref, rstd_ref, low_ref, qa_ref, qb_ref, out_s
):
    core = core_ref[0]
    width = own_ref.shape[1]

    @pl.when(pl.program_id(0) == 0)
    def _():
        join_columns(core, mat_ref.at[0], moth_ref.at[0], out_s)

    parts = [slice(i, i + CHUNK) for i in range(0, own_ref.shape[0], CHUNK)]
    mixed = [
        nn(own_ref[r, :], out_s[own_part(core, 0, width), :]) + nn(oth_ref[r, :], out_s[own_part(core, 1, width), :])
        for r in parts
    ]
    for r, one in zip(parts, mixed):
        xhat, rstd = normalise(x_ref[r, :].astype(F32) + one + vec_ref[2:3])
        xhat_ref[r, :] = xhat
        rstd_ref[r, :] = rstd
        low = (xhat * vec_ref[7:8] + vec_ref[8:9]).astype(BF)
        low_ref[r, :] = low
        qa_ref[r, :] = ((nn(low, mat_ref[1]) + vec_ref[3:4, own_part(core, 0, width)]) * 0.125).astype(BF)
        qb_ref[r, :] = ((nn(low, moth_ref[1]) + vec_ref[3:4, own_part(core, 1, width)]) * 0.125).astype(BF)


def first_two(mats):
    return pl.BlockSpec((2,) + mats.shape[1:], lambda *_: (0, 0, 0))


def after_self(core, own, other, x, mats, mats_other, vec, tile):
    tokens, dim = x.shape
    rows = lambda w: pl.BlockSpec((tile, w), lambda i, s: (i, 0))
    half = dim // 2
    return call(
        "after_self",
        after_self_kernel,
        (tokens // tile,),
        [rows(half), rows(half), rows(dim), first_two(mats), first_two(mats), whole(vec)],
        [rows(dim), rows(1), rows(dim), rows(half), rows(half)],
        [
            shape((tokens, dim), F32),
            shape((tokens, 1), F32),
            shape((tokens, dim), BF),
            shape((tokens, half), BF),
            shape((tokens, half), BF),
        ],
        [core, own, other, x, mats, mats_other, vec],
        scratch=[pltpu.VMEM((dim, dim), BF)],
        flops=4 * tokens * dim * dim,
        prefetch=1,
    )


LOTS = 32


def packed_in(pack_ref, n):
    lots, dim = pack_ref.shape[0], pack_ref.shape[2]
    lot = dim // lots
    return pack_ref[:, n * lot : (n + 1) * lot, :].reshape(dim, dim)


def packed_out(pack_ref, n):
    lots, dim = pack_ref.shape[0], pack_ref.shape[2]
    lot, some = dim // lots, lots // 4
    return pack_ref[n * some : (n + 1) * some, 4 * lot : 8 * lot, :].reshape(dim, dim)


def packed_cross(pack_ref, core, swap):
    lots, dim = pack_ref.shape[0], pack_ref.shape[2]
    lot, some = dim // lots, lots // 2
    return pack_ref[own_part(core, swap, some), 8 * lot : 9 * lot, :].reshape(dim // 2, dim)


def middle_kernel(
    core_ref,
    own_ref,
    oth_ref,
    xhat1_ref,
    cot_ref,
    pack_ref,
    vec_ref,
    block_ref,
    act_ref,
    dpre_ref,
    low2_ref,
    e3_ref,
    dr2_ref,
    br2_ref,
    ga_ref,
    gb_ref,
    vsum_ref,
    fsum_ref,
    slope_s,
):
    core = core_ref[0]
    rows, dim = xhat1_ref.shape
    hidden = act_ref.shape[1]
    parts = [slice(i, i + CHUNK) for i in range(0, rows, CHUNK)]
    jobs = [(i, n) for n in range(hidden // dim) for i in range(len(parts))]
    state = [{} for _ in parts]

    def in_turn(make, use):
        waiting = None
        for job in jobs:
            made = make(*job)
            if waiting is not None:
                use(*waiting)
            waiting = (*job, made)
        use(*waiting)

    for at, r in zip(state, parts):
        first = xhat1_ref[r, :] * vec_ref[7:8] + vec_ref[8:9]
        mixed = nn(own_ref[r, :], packed_cross(pack_ref, core, 0)) + nn(oth_ref[r, :], packed_cross(pack_ref, core, 1))
        at["r2"] = first + mixed + vec_ref[5:6]
    for at, r in zip(state, parts):
        at["xhat2"], at["rstd2"] = normalise(at["r2"])
        second = at["xhat2"] * vec_ref[9:10] + vec_ref[10:11]
        at["low2"] = second.astype(BF)
        low2_ref[r, :] = at["low2"]
        at["r3"] = second + vec_ref[6:7]

    def before_gelu(i, n):
        return nn(state[i]["low2"], packed_in(pack_ref, n)) + vec_ref[13 + n : 14 + n]

    def gelu(i, n, pre):
        r, cs = parts[i], slice(n * dim, (n + 1) * dim)
        phi = 0.5 * (1.0 + lax.erf(pre * 0.7071067811865476))
        act = (pre * phi).astype(BF)
        act_ref[r, cs] = act
        slope_s[r, cs] = phi + pre * (jnp.exp(-0.5 * pre * pre) * 0.3989422804014327)
        state[i]["r3"] = state[i]["r3"] + nn(act, packed_out(pack_ref, n))

    in_turn(before_gelu, gelu)
    for at, r in zip(state, parts):
        xhat3, rstd3 = normalise(at["r3"])
        block_ref[r, :] = xhat3 * vec_ref[11:12] + vec_ref[12:13]
        dz = cot_ref[r, :].astype(F32)
        dr3 = norm_back(dz, xhat3, rstd3, vec_ref[11:12])
        at["e3"] = dr3.astype(BF)
        e3_ref[r, :] = at["e3"]
        at["back"] = dr3
        at["sums"] = [col_sum(at["e3"]), col_sum(dz * xhat3), col_sum(dz)]
        at["ff"] = []

    def act_grad(i, n):
        return nt(state[i]["e3"], packed_out(pack_ref, n))

    def gelu_back(i, n, grad):
        r, cs = parts[i], slice(n * dim, (n + 1) * dim)
        low = (grad * slope_s[r, cs]).astype(BF)
        dpre_ref[r, cs] = low
        state[i]["ff"].append(col_sum(low))
        state[i]["back"] = state[i]["back"] + nt(low, packed_in(pack_ref, n))

    in_turn(act_grad, gelu_back)
    first_step = pl.program_id(0) == 0
    total = jnp.where(first_step, 0.0, vsum_ref[...])
    ff_total = jnp.where(first_step, 0.0, fsum_ref[...])
    for at, r in zip(state, parts):
        back = at["back"]
        dr2 = norm_back(back, at["xhat2"], at["rstd2"], vec_ref[9:10])
        dr2_ref[r, :] = dr2
        br2 = dr2.astype(BF)
        br2_ref[r, :] = br2
        ga_ref[r, :] = nt(br2, packed_cross(pack_ref, core, 0)).astype(BF)
        gb_ref[r, :] = nt(br2, packed_cross(pack_ref, core, 1)).astype(BF)
        e3_sum, gain3, shift3 = at["sums"]
        sums = [col_sum(br2), e3_sum, col_sum(back * at["xhat2"]), col_sum(back), gain3, shift3]
        total = total + jnp.concatenate(sums + [jnp.zeros((2, dim), F32)], axis=0)
        ff_total = ff_total + jnp.concatenate(at["ff"] + [jnp.zeros((8 - len(at["ff"]), dim), F32)], axis=0)
    vsum_ref[...] = total
    fsum_ref[...] = ff_total


def middle(core, own, other, xhat1, cot, pack, vec, tile):
    tokens, dim = xhat1.shape
    hidden = 4 * dim
    half = dim // 2
    rows = lambda w: pl.BlockSpec((tile, w), lambda i, s: (i, 0))
    once = lambda a: pl.BlockSpec(a.shape, lambda *_: (0,) * a.ndim, pipeline_mode=pl.Buffered(1))
    sums = pl.BlockSpec((8, dim), lambda i, s: (0, 0))
    return call(
        "middle",
        middle_kernel,
        (tokens // tile,),
        [rows(half), rows(half), rows(dim), rows(dim), once(pack), once(vec)],
        [
            rows(dim),
            rows(hidden),
            rows(hidden),
            rows(dim),
            rows(dim),
            rows(dim),
            rows(dim),
            rows(half),
            rows(half),
            sums,
            sums,
        ],
        [
            shape((tokens, dim), F32),
            shape((tokens, hidden), BF),
            shape((tokens, hidden), BF),
            shape((tokens, dim), BF),
            shape((tokens, dim), BF),
            shape((tokens, dim), F32),
            shape((tokens, dim), BF),
            shape((tokens, half), BF),
            shape((tokens, half), BF),
            shape((8, dim), F32),
            shape((8, dim), F32),
        ],
        [core, own, other, xhat1, cot, pack, vec],
        scratch=[pltpu.VMEM((tile, hidden), F32)],
        room=60,
        flops=tokens * (4 * dim * dim + 8 * dim * hidden),
        prefetch=1,
    )


def before_self_kernel(
    core_ref,
    own_ref,
    oth_ref,
    dr2_ref,
    xhat_ref,
    rstd_ref,
    mat_ref,
    moth_ref,
    vec_ref,
    dr1_ref,
    br1_ref,
    ga_ref,
    gb_ref,
    vsum_ref,
    out_s,
):
    core = core_ref[0]
    width = own_ref.shape[1]

    @pl.when(pl.program_id(0) == 0)
    def _():
        join_columns(core, mat_ref.at[0], moth_ref.at[0], out_s)

    parts = [slice(i, i + CHUNK) for i in range(0, own_ref.shape[0], CHUNK)]
    grads = [dr2_ref[r, :] + nt(own_ref[r, :], mat_ref[1]) + nt(oth_ref[r, :], moth_ref[1]) for r in parts]
    total = jnp.where(pl.program_id(0) == 0, 0.0, vsum_ref[...])
    zero = jnp.zeros((5, xhat_ref.shape[1]), F32)
    for r, dfirst in zip(parts, grads):
        xhat = xhat_ref[r, :]
        dr1 = norm_back(dfirst, xhat, rstd_ref[r, :], vec_ref[7:8])
        dr1_ref[r, :] = dr1
        br1 = dr1.astype(BF)
        br1_ref[r, :] = br1
        ga_ref[r, :] = nt(br1, out_s[own_part(core, 0, width), :]).astype(BF)
        gb_ref[r, :] = nt(br1, out_s[own_part(core, 1, width), :]).astype(BF)
        total = total + jnp.concatenate([col_sum(br1), col_sum(dfirst * xhat), col_sum(dfirst), zero], axis=0)
    vsum_ref[...] = total


def before_self(core, own, other, dr2, xhat, rstd, mats, mats_other, vec, tile):
    tokens, dim = xhat.shape
    half = dim // 2
    rows = lambda w: pl.BlockSpec((tile, w), lambda i, s: (i, 0))
    return call(
        "before_self",
        before_self_kernel,
        (tokens // tile,),
        [rows(half), rows(half), rows(dim), rows(dim), rows(1), first_two(mats), first_two(mats), whole(vec)],
        [rows(dim), rows(dim), rows(half), rows(half), pl.BlockSpec((8, dim), lambda i, s: (0, 0))],
        [
            shape((tokens, dim), F32),
            shape((tokens, dim), BF),
            shape((tokens, half), BF),
            shape((tokens, half), BF),
            shape((8, dim), F32),
        ],
        [core, own, other, dr2, xhat, rstd, mats, mats_other, vec],
        scratch=[pltpu.VMEM((dim, dim), BF)],
        flops=4 * tokens * dim * dim,
        prefetch=1,
    )


def pair_grads_kernel(route, me_ref, xt_ref, yt_ref, a_ref, b_ref, *refs):
    n = pl.program_id(0)
    total = (nn(xt_ref[...], a_ref[0]) + nn(yt_ref[...], b_ref[0])).astype(BF)
    if route is None:
        refs[0][0] = total
        return
    bits, devices = route
    tile_ref, outs, block_s = refs[0], refs[1:-1], refs[-1]
    block_s[...] = total.reshape(block_s.shape)
    lot = block_s.shape[1]
    rows = pl.ds(pl.multiple_of(n * lot, lot), lot)
    last = outs[0].shape[1] - 8

    def store(out):
        def put(j, value):
            out[j, rows, :] = value

        return put

    def store_tile(out):
        def put(j, value):
            out[j, last:, :] = value

        return put

    send_blocks(bits, [], devices, me_ref[0], lambda k: block_s[k], [store(out) for out in outs])

    @pl.when(n == 0)
    def _():
        send_blocks(bits, [], devices, me_ref[0], lambda k: tile_ref[k], [store_tile(out) for out in outs])


def pair_grads(me, xt, yt, own, other, route=None):
    count, tokens, width = own.shape
    dim = xt.shape[0]
    grads = pl.BlockSpec((1, tokens, width), lambda i, *_: (i, 0, 0))
    operands, specs = [me, xt, yt, own, other], [whole(xt), whole(yt), grads, grads]
    if route is None:
        outs = [pl.BlockSpec((1, dim, width), lambda i, *_: (i, 0, 0))]
        shapes, scratch = [shape((count, dim, width), BF)], []
    else:
        bits, tiles = route
        devices = tiles.shape[0]
        lot, blocks = dim // devices, devices >> len(bits)
        shapes = [shape((blocks, count * lot + 8, width), BF)] * (1 << len(bits))
        outs = [whole(one) for one in shapes]
        scratch = [pltpu.VMEM((devices, lot, width), BF)]
        operands, specs, route = operands + [tiles], specs + [whole(tiles)], (bits, devices)
    return call(
        "pair_grads",
        functools.partial(pair_grads_kernel, route),
        (count,),
        specs,
        outs,
        shapes,
        operands,
        scratch=scratch,
        flops=4 * count * tokens * width * dim,
        prefetch=1,
    )


def route_sums(me, mine, received, plain, bits, count):
    lots = count
    _, dim, width = mine.shape
    lot = dim // lots
    total = mine.shape[0] + plain.shape[0]
    view = lambda a: a.reshape(a.shape[0], lots, lot, width)
    out = shape((lots >> len(bits), total, lot, width), BF)
    operands = [view(mine), view(received), view(plain)]

    def kernel(me_ref, a_ref, b_ref, p_ref, *outs):
        def load(k):
            both = (a_ref[:, k].astype(F32) + b_ref[:, k].astype(F32)).astype(BF)
            return both, p_ref[:, k]

        def store(out):
            def put(j, value):
                out[j, : a_ref.shape[0]] = value[0]
                out[j, a_ref.shape[0] :] = value[1]

            return put

        send_blocks(bits, [], count, me_ref[0], load, [store(o) for o in outs])

    return call(
        "route_sums",
        kernel,
        (1,),
        [whole(o) for o in operands],
        [whole(out)] * (1 << len(bits)),
        [out] * (1 << len(bits)),
        [me] + operands,
        prefetch=1,
    )


def by_rows_grads(core, own, other, grad, mine_ref, away_ref, full_s, n):
    width = own.shape[1]
    full_s[own_part(core, 0, width), :] = tn(own[...], grad[...]).astype(BF)
    full_s[own_part(core, 1, width), :] = tn(other[...], grad[...]).astype(BF)
    mine_ref[n] = full_s[:, own_part(core, 0, width)]
    away_ref[n] = full_s[:, own_part(core, 1, width)]


def output_grads_kernel(core_ref, own_ref, oth_ref, grad_ref, mine_ref, away_ref, full_s):
    by_rows_grads(core_ref[0], own_ref, oth_ref, grad_ref, mine_ref, away_ref, full_s, 0)


def token_grads_kernel(core_ref, so_ref, st_ref, br1_ref, low_ref, qo_ref, qt_ref, mine_ref, away_ref, full_s):
    by_rows_grads(core_ref[0], so_ref, st_ref, br1_ref, mine_ref, away_ref, full_s, 0)
    mine_ref[1] = tn(low_ref[...], qo_ref[...]).astype(BF)
    away_ref[1] = tn(low_ref[...], qt_ref[...]).astype(BF)


def token_grads(name, kernel, core, operands, count):
    tokens, dim = operands[2].shape
    out = shape((count, dim, dim // 2), BF)
    return call(
        name,
        kernel,
        (1,),
        [whole(o) for o in operands],
        [whole(out)] * 2,
        [out] * 2,
        [core] + operands,
        scratch=[pltpu.VMEM((dim, dim), BF)],
        flops=2 * count * tokens * dim * dim,
        prefetch=1,
    )


def feed_in_kernel(core_ref, low_ref, dpre_ref, mine_ref, away_ref, low_s, full_s):
    n = pl.program_id(0)

    @pl.when(n == 0)
    def _():
        low_s[...] = low_ref[...].T

    lots, _, half = mine_ref.shape
    lot = low_s.shape[0] // lots
    full_s[...] = nn(low_s[...], dpre_ref[...]).astype(BF)
    rows = pl.ds(pl.multiple_of(n * lot, lot), lot)
    mine_ref[:, rows, :] = full_s[:, own_part(core_ref[0], 0, half)].reshape(lots, lot, half)
    away_ref[:, rows, :] = full_s[:, own_part(core_ref[0], 1, half)].reshape(lots, lot, half)


def feed_out_kernel(core_ref, act_ref, e3_ref, mine_ref, away_ref, full_s):
    full_s[...] = tn(act_ref[...], e3_ref[...]).astype(BF)
    half = mine_ref.shape[2]
    mine_ref[...] = full_s[:, own_part(core_ref[0], 0, half)].reshape(mine_ref.shape)
    away_ref[...] = full_s[:, own_part(core_ref[0], 1, half)].reshape(away_ref.shape)


def feed_in_grads(core, low2, dpre):
    tokens, dim = low2.shape
    out = shape((LOTS, 4 * dim // LOTS, dim // 2), BF)
    return call(
        "feed_in_grads",
        feed_in_kernel,
        (4,),
        [whole(low2), pl.BlockSpec((tokens, dim), lambda i, s: (0, i))],
        [whole(out)] * 2,
        [out] * 2,
        [core, low2, dpre],
        scratch=[pltpu.VMEM((dim, tokens), BF), pltpu.VMEM((dim, dim), BF)],
        flops=8 * tokens * dim * dim,
        prefetch=1,
    )


def feed_out_grads(core, act, e3):
    tokens, dim = e3.shape
    lots = 4 * dim // LOTS
    out = shape((LOTS, lots, dim // 2), BF)
    return call(
        "feed_out_grads",
        feed_out_kernel,
        (4,),
        [pl.BlockSpec((tokens, dim), lambda i, s: (0, i)), whole(e3)],
        [pl.BlockSpec((LOTS // 4, lots, dim // 2), lambda i, s: (i, 0, 0))] * 2,
        [out] * 2,
        [core, act, e3],
        scratch=[pltpu.VMEM((dim, dim), BF)],
        flops=8 * tokens * dim * dim,
        prefetch=1,
    )


def route_feed(me, first, second, bits, count):
    rows = first[0].shape[1]
    out = shape((count >> len(bits), 2 * rows, first[0].shape[2]), BF)
    operands = list(first) + list(second)

    def kernel(me_ref, a_ref, b_ref, c_ref, d_ref, *outs):
        def load(k):
            one = (a_ref[k].astype(F32) + b_ref[k].astype(F32)).astype(BF)
            return one, (c_ref[k].astype(F32) + d_ref[k].astype(F32)).astype(BF)

        def store(out):
            def put(j, value):
                out[j, :rows] = value[0]
                out[j, rows:] = value[1]

            return put

        send_blocks(bits, [], count, me_ref[0], load, [store(o) for o in outs])

    return call(
        "route_feed",
        kernel,
        (1,),
        [whole(o) for o in operands],
        [whole(out)] * (1 << len(bits)),
        [out] * (1 << len(bits)),
        [me] + operands,
        prefetch=1,
        room=36,
    )


def vec_rows_kernel(core_ref, self_ref, cross_ref, first_ref, mid_ref, ff_ref, out_ref, tiles_ref=None):
    core = core_ref[0]
    width = self_ref.shape[2]
    out_ref[...] = jnp.zeros_like(out_ref)
    self_sum, cross_sum = self_ref[0], cross_ref[0]
    for m in range(1, self_ref.shape[0]):
        self_sum, cross_sum = self_sum + self_ref[m], cross_sum + cross_ref[m]
    own = own_part(core, 0, width)
    out_ref[0:1, own] = self_sum[0:1]
    out_ref[1:2, own] = self_sum[2:3]
    out_ref[3:4, own] = cross_sum[0:1]
    out_ref[4:5, own] = cross_sum[2:3]
    out_ref[2:3, :] = first_ref[0:1]
    out_ref[5:7, :] = mid_ref[0:2]
    out_ref[7:9, :] = first_ref[1:3]
    out_ref[9:13, :] = mid_ref[2:6]
    out_ref[13:17, :] = ff_ref[0:4]
    if tiles_ref is not None:
        lots = tiles_ref.shape[0]
        lot, third = out_ref.shape[1] // lots, tiles_ref.shape[2] // 3
        tiles_ref[...] = jnp.zeros_like(tiles_ref)
        for d in range(lots):
            for n in range(3):
                piece = out_ref[8 * n : 8 * n + 8, d * lot : (d + 1) * lot]
                tiles_ref[d, :, n * third : n * third + lot] = piece.astype(BF)


def vec_rows(core, self_sums, cross_sums, first_sums, mid_sums, ff_sums, devices=None):
    operands = [self_sums, cross_sums, first_sums, mid_sums, ff_sums]
    dim = first_sums.shape[1]
    outs = [shape((24, dim), F32)]
    if devices is not None:
        outs.append(shape((devices, 8, dim // 2), BF))
    return call(
        "vec_rows",
        vec_rows_kernel,
        (1,),
        [whole(o) for o in operands],
        [whole(o) for o in outs],
        outs,
        [core] + operands,
        prefetch=1,
    )


def input_grad_kernel(count, has_start, *refs):
    start = refs[0] if has_start else None
    own, oth, mats_a, mats_b, out = refs[has_start:]
    total = start[...] if has_start else None
    for n in range(count):
        for grads, mats in ((own, mats_a), (oth, mats_b)):
            t = nt(grads[n], mats[n])
            total = t if total is None else total + t
    out[...] = total


def input_grad(own, other, mats_own, mats_other, start, tile):
    count, tokens, half = own.shape
    dim = mats_own.shape[1]
    grads = pl.BlockSpec((count, tile, half), lambda i: (0, i, 0))
    rows = pl.BlockSpec((tile, dim), lambda i: (i, 0))
    has_start = start is not None
    return call(
        "input_grad",
        functools.partial(input_grad_kernel, count, has_start),
        (tokens // tile,),
        ([rows] if has_start else []) + [grads, grads, whole(mats_own), whole(mats_other)],
        [rows],
        [shape((tokens, dim), F32)],
        ([start] if has_start else []) + [own, other, mats_own, mats_other],
        flops=4 * count * tokens * half * dim,
    )[0]


def adam_step(master, first_m, second_m, grad_sum, rate, decay):
    first_new = 0.5 * first_m + 0.5 * grad_sum
    second_new = 0.5 * second_m + 0.5 * grad_sum * grad_sum
    fix_term = 1.0 - 0.5**STEP
    update = first_new / fix_term / (jnp.sqrt(second_new / fix_term) + adam_eps)
    master_new = master - rate * (update + decay * master)
    return (master_new, first_new, second_new, master_new.astype(BF))


def on_device(
    target,
    memory,
    cotangent,
    seg_target,
    seg_memory,
    attn_master,
    attn_first,
    attn_second,
    in_master,
    in_first,
    in_second,
    out_master,
    out_first,
    out_second,
    vec_master,
    vec_first,
    vec_second,
):
    both = ("seq", "fsdp")
    devices = lax.axis_size("seq") * lax.axis_size("fsdp")
    core_at = lax.axis_index("seq") & 1
    core = core_at.astype(jnp.int32).reshape(1)
    is_low = core_at == 0
    place = lax.axis_index("seq") * lax.axis_size("fsdp") + lax.axis_index("fsdp")
    me = place.astype(jnp.int32).reshape(1)
    micro, _, rows, dim = target.shape
    half, hidden = dim // 2, in_master.shape[1]
    tokens = micro * rows
    shard = attn_master.shape[1]
    sets = bit_sets(devices)
    near = flips(sets[0])
    thin = sets[:1] + [[b] for bits in sets[1:] for b in bits]
    chip_bits = [b for bits in sets[::-1] for b in bits[::-1]]
    all_bits = sorted(chip_bits + [1], reverse=True)
    direct = devices == LOTS
    partner = lambda a: moved(a, CORE)
    flat = lambda a: a.reshape(-1, a.shape[-1])

    x_own, m_own = target[:, 0], memory[:, 0]
    seg_own = jnp.concatenate([seg_target[:, 0], seg_memory[:, 0]], axis=0)
    attn_low = attn_master.astype(BF)
    in_low = in_master.astype(BF)
    out_low = out_master.astype(BF)
    vec_low = vec_master.astype(BF)

    def column_halves(mats):
        mine = jnp.where(is_low, mats[:, :, :half], mats[:, :, half:])
        other = partner(jnp.where(is_low, mats[:, :, half:], mats[:, :, :half]))
        return jnp.stack([jnp.where(is_low, mine, other), jnp.where(is_low, other, mine)])

    x_other, seg_other, m_other = partner(x_own), partner(seg_own), partner(m_own)
    if direct:
        halves = column_halves(attn_low[0:7]).reshape(2, 7 * shard, half)
        low_tile = as_tile(vec_low, half)
        far_tile = partner(low_tile)
        tiles = jnp.stack([jnp.where(is_low, low_tile, far_tile), jnp.where(is_low, far_tile, low_tile)])
        ends = (3 * shard, 7 * shard, 7 * shard + 8)
        cuts = list(zip((0,) + ends[:2], ends))
        across = [flat(a).T for a in (x_own, m_own)]
        (self_far, late_far, vec_far), rels, across = far_parts(
            jnp.concatenate([halves, tiles], axis=1), sets, cuts, across
        )
        feed_low = in_low.reshape(shard, 4, dim).transpose(1, 0, 2).reshape(4 * shard, dim)
        pack = jnp.concatenate([feed_low, out_low, attn_low[7]], axis=0)
        self_far, x_own, m_own, x_other, m_other, seg_other, pack, vec_far = lax.optimization_barrier(
            (self_far, x_own, m_own, x_other, m_other, seg_other, pack, vec_far)
        )
        pack = lax.all_gather(pack, both, axis=0, tiled=False)
        self_parts = near_parts(self_far, sets)
        vec_parts = near_parts(vec_far, sets)
        self_mats = (self_parts, near, rels)
        vec_tiles = assemble(me, vec_parts, near, rels, 8)[0].reshape(devices, 8, half)
        vec_all = from_tile(vec_tiles, vec_low.shape[0], vec_low.shape[1])
        vec_all, x_own, m_own = lax.optimization_barrier((vec_all, x_own, m_own))
        self_parts[1:], late_far = lax.optimization_barrier((self_parts[1:], late_far))
        late_parts = near_parts(late_far, sets)
    else:

        def gather_half(mats):
            stacked = jnp.moveaxis(column_halves(mats), 0, 1)
            return gather_bits(stacked, chip_bits, [1]).reshape(mats.shape[0], dim, half)

        self_mats = gather_half(attn_low[0:3])
        late_mats = gather_half(attn_low[3:7])
        lots = lambda a: a.reshape(LOTS, -1, dim)
        win = lax.all_gather(in_low, both, axis=0, tiled=True)
        pack = jnp.concatenate(
            [lots(win[:, n * dim : (n + 1) * dim]) for n in range(4)]
            + [lots(lax.all_gather(out_low, both, axis=0, tiled=True))]
            + [lots(lax.all_gather(attn_low[7], both, axis=0, tiled=True))],
            axis=1,
        )
        vec_all = gather_bits(vec_low[None], [1] + chip_bits).reshape(devices, *vec_low.shape)
    vec = vec_all.transpose(1, 0, 2).reshape(vec_low.shape[0], dim).astype(F32)

    seg_t, seg_m = (jnp.concatenate([a, b], axis=1) for a, b in zip(
        (seg_own[:micro], seg_own[micro:]), (seg_other[:micro], seg_other[micro:])
    ))
    seg_t_ordered = jnp.where(is_low, seg_t, jnp.concatenate([seg_other[:micro], seg_own[:micro]], axis=1))
    row = lambda a: a[:, None, :]
    own_cols = lambda n: jnp.where(is_low, vec[n, :half], vec[n, half:])
    zeros = jnp.zeros((half,), F32)
    flat3 = lambda a: a.reshape(a.shape[0], tokens, half)
    tall = lambda a: a.reshape(micro, rows, half)
    if not direct:
        across = [flat(a).T for a in (x_own, m_own)]
    across = [across[0], flat(x_other).T, across[1], flat(m_other).T]
    x_own, across = lax.optimization_barrier((x_own, across))

    qkv, self_mats = project(
        core, me, x_own, x_other, self_mats, jnp.stack([own_cols(0), zeros, own_cols(1)])[:, None], 0.125, True
    )
    self_own, self_send, self_exact, self_log = attention(
        True, core, None, (qkv, 1), row(seg_t_ordered), row(seg_t_ordered)
    )
    if direct:
        self_own, late_parts[0] = lax.optimization_barrier((self_own, late_parts[0]))
        late_mats = assemble(me, late_parts, near, rels, shard)
    late_other = partner(late_mats)
    mem_kv, _ = project(
        core, me, m_own, m_other, late_mats[2:4], jnp.stack([zeros, own_cols(4)])[:, None], 1.0, False
    )
    self_other_mats = partner(self_mats)
    mem_kv, late_other, self_other_mats = lax.optimization_barrier((mem_kv, late_other, self_other_mats))
    self_own, self_other = flat(self_own), flat(partner(self_send))
    xhat1, rstd1, first_low, cq_own, cq_send = after_self(
        core, self_own, self_other, flat(x_own), late_mats, late_other, vec, 2 * CHUNK
    )
    cq_own, cq_other = tall(cq_own), tall(partner(cq_send))
    cross_own, cross_send, cross_exact, cross_log = attention(
        False, core, (cq_own, cq_other), (mem_kv, 0), row(seg_t), row(seg_m)
    )
    cross_own, cross_other = flat(cross_own), flat(partner(cross_send))

    (block, act, d_pre, second_low, e3, d_r2, br2, dco_own, dco_send, mid_sums, ff_sums) = middle(
        core, cross_own, cross_other, xhat1, flat(cotangent[:, 0]), pack, vec, 2 * CHUNK
    )
    dco_own, dco_other = tall(dco_own), tall(partner(dco_send))
    feed_in, feed_in_away = feed_in_grads(core, second_low, d_pre)
    feed_out, feed_out_away = feed_out_grads(core, act, e3)
    feed_in_got, feed_out_got = partner(feed_in_away), partner(feed_out_away)
    last_mine, last_away = token_grads("output_grads", output_grads_kernel, core, [cross_own, cross_other, br2], 1)
    last_got = partner(last_away)
    if direct:
        feed_in_got, feed_out_got, last_mine = lax.optimization_barrier((feed_in_got, feed_out_got, last_mine))
        feed = list(route_feed(me, (feed_in, feed_in_got), (feed_out, feed_out_got), sets[0], devices))
        dco_own, feed[0] = lax.optimization_barrier((dco_own, feed[0]))
        feed_near, _ = reduce_near(me, feed, thin, devices)
    else:
        lot = dim // LOTS
        halves_of = lambda a, b: both_halves(is_low, (a.astype(F32) + b.astype(F32)).astype(BF), partner((a.astype(F32) + b.astype(F32)).astype(BF)))
        win_grad, wout_grad = halves_of(feed_in, feed_in_got), halves_of(feed_out, feed_out_got)
        in_parts = [win_grad[:, n * lot : (n + 1) * lot].reshape(dim, dim) for n in range(4)]
        keep = jnp.where(is_low, 1.0, 0.0).astype(BF)
        sum_in_mat = lax.psum_scatter(keep * jnp.concatenate(in_parts, axis=1), both, scatter_dimension=0, tiled=True)
        sum_out_mat = lax.psum_scatter(keep * wout_grad.reshape(hidden, dim), both, scatter_dimension=0, tiled=True)
    dcq_own, dcq_send, d_mem_own, d_mem_other, cross_sums = attention(
        False,
        core,
        (cq_own, cq_other),
        (mem_kv, 0),
        row(seg_t),
        row(seg_m),
        (dco_own, dco_other, cross_exact, cross_log),
    )
    dcq_own, dcq_other = flat(dcq_own), flat(partner(dcq_send))
    d_r1, br1, dso_own, dso_send, first_sums = before_self(
        core, dcq_own, dcq_other, d_r2, xhat1, rstd1, late_mats, late_other, vec, 2 * CHUNK
    )
    dso_own, dso_other = tall(dso_own), tall(partner(dso_send))
    if direct:
        br1, feed_near = lax.optimization_barrier((br1, feed_near))

    def reduce_whole(mats):
        spread = mats.reshape([mats.shape[0]] + [2] * len(all_bits) + [shard, half])
        summed = scatter_bits(spread, chip_bits[::-1], all_bits)
        mine = jnp.where(is_low, summed[:, 0], summed[:, 1])
        other = partner(jnp.where(is_low, summed[:, 1], summed[:, 0]))
        return both_halves(is_low, mine, other)

    d_mem_own, d_mem_other = flat3(d_mem_own), flat3(d_mem_other)
    grads_mine, grads_away = token_grads(
        "token_grads", token_grads_kernel, core, [self_own, self_other, br1, first_low, dcq_own, dcq_other], 2
    )
    grads_mine = jnp.concatenate([grads_mine, last_mine])
    grads_mem = pair_grads(me, across[2], across[3], d_mem_own, d_mem_other)[0]
    grads_got = jnp.concatenate([partner(grads_away), last_got])
    d_mem_in = partner(d_mem_other)
    if direct:
        routed = list(route_sums(me, grads_mine, grads_got, grads_mem, sets[0], devices))
        dso_own, routed[0], d_mem_in = lax.optimization_barrier((dso_own, routed[0], d_mem_in))
        cross_near, _ = reduce_near(me, routed, thin, devices)
    else:
        summed = (grads_mine.astype(F32) + grads_got.astype(F32)).astype(BF)
        sum_cross = reduce_whole(jnp.concatenate([summed, grads_mem]))

    d_self_own, d_self_away, self_sums = attention(
        True,
        core,
        None,
        (qkv, 1),
        row(seg_t_ordered),
        row(seg_t_ordered),
        (dso_own, dso_other, self_exact, self_log),
    )
    d_self_own, d_self_away = flat3(d_self_own), flat3(d_self_away)
    grad_m = input_grad(d_mem_own, d_mem_in, late_mats[2:4], late_other[2:4], None, 2 * CHUNK)
    vec_grad = vec_rows(core, self_sums, cross_sums, first_sums, mid_sums, ff_sums, devices if direct else None)
    if direct:
        feed_near, d_self_own = reduce_step(me, feed_near, thin, 1, devices, d_self_own)
        d_self_own, feed_near = lax.optimization_barrier((d_self_own, feed_near))
        routed = list(
            pair_grads(me, across[0], across[1], d_self_own, d_self_away, (sets[0], vec_grad[1]))
        )
        d_self_away, routed, cross_near = lax.optimization_barrier((d_self_away, routed, cross_near))

    d_self_other = partner(d_self_away)
    grad_x = input_grad(d_self_own, d_self_other, self_mats, self_other_mats, d_r1, 2 * CHUNK)
    if direct:
        mine, other, (grad_m, grad_x) = reduce_far(me, cross_near, thin, devices, [grad_m, grad_x])
        self_near, (mine, grad_m, grad_x) = reduce_near(me, routed, sets, devices, (mine, grad_m, grad_x))
        sum_cross = both_halves(is_low, mine, other)
        self_near = list(self_near)
        feed_near, self_near[0] = reduce_step(me, feed_near, thin, 2, devices, self_near[0])
        feed_mine, feed_other = feed_near[0][0], partner(feed_near[1])[0]
        feed_sum = both_halves(is_low, feed_mine, feed_other)
        sum_in_mat = feed_sum[: 4 * shard].reshape(4, shard, dim).transpose(1, 0, 2).reshape(shard, hidden)
        sum_out_mat = feed_sum[4 * shard :]
        mine, other, _ = reduce_far(me, self_near, sets, devices)
        last = 3 * shard
        sum_self = both_halves(is_low, mine[:last], other[:last]).reshape(3, shard, dim)
        tile = mine[last:].astype(F32) + other[last:].astype(F32)
        sum_vec = from_tile(tile, *vec_master.shape)
    else:
        sum_self = reduce_whole(pair_grads(me, across[0], across[1], d_self_own, d_self_away)[0])
        all_rows = vec_grad[0]
        for bit in [1] + chip_bits[::-1]:
            all_rows = all_rows + moved(all_rows, 1 << bit)
        width = vec_master.shape[1]
        sum_vec = lax.dynamic_slice_in_dim(all_rows[: vec_master.shape[0]], place * width, width, axis=1)

    sum_attn = jnp.concatenate(
        [sum_self, sum_cross[0:2], sum_cross[3:5], sum_cross[2:3]], axis=0
    ).astype(F32)
    attn_new, attn_m, attn_s, attn_w = adam_step(attn_master, attn_first, attn_second, sum_attn, 0.1, 0.01)
    in_new, in_m, in_s, in_w = adam_step(in_master, in_first, in_second, sum_in_mat.astype(F32), 0.05, 0.01)
    out_new, out_m, out_s, out_w = adam_step(out_master, out_first, out_second, sum_out_mat.astype(F32), 0.03, 0.01)
    vec_new, vec_m, vec_s, vec_w = adam_step(vec_master, vec_first, vec_second, sum_vec, 0.3, 0.0)
    return (
        block.reshape(micro, 1, rows, dim),
        grad_x.reshape(micro, 1, rows, dim),
        grad_m.reshape(micro, 1, rows, dim),
        attn_new,
        attn_m,
        attn_s,
        attn_w,
        in_new,
        in_m,
        in_s,
        in_w,
        out_new,
        out_m,
        out_s,
        out_w,
        vec_new,
        vec_m,
        vec_s,
        vec_w,
    )


def solution(mesh):
    tokens = P(None, "fsdp", "seq", None)
    marks = P(None, "fsdp", "seq")
    attn = P(None, ("seq", "fsdp"), None)
    feed = P(("seq", "fsdp"), None)
    rows = P(None, ("seq", "fsdp"))
    return jax.shard_map(
        on_device,
        mesh=mesh,
        in_specs=(tokens,) * 3 + (marks,) * 2 + (attn,) * 3 + (feed,) * 6 + (rows,) * 3,
        out_specs=(tokens,) * 3 + (attn,) * 4 + (feed,) * 8 + (rows,) * 4,
        check_vma=False,
    )
```
